32 devices in a mesh: slab: 8 (over z, core), filt: 4 (over y, x).
Axes of the slice: x: 2, y: 2, z: 4, core: 2. Of those that a mesh axis runs over, the one named last changes fastest.
Arguments:
- features: bfloat16 [16, 512, 256], P('slab', 'filt'), may hold values from -6 to 6
- first_weight: bfloat16 [27, 512, 512], P(None, 'filt'), may hold values from -0.0546875 to 0.0546875
- second_weight: bfloat16 [27, 512, 512], P(None, 'filt'), may hold values from -0.0546875 to 0.0546875
- head_weight: bfloat16 [8, 512], P(None, 'filt'), may hold values from -0.25 to 0.25
- labels: int32 [16, 256], P('slab'), may hold values from 0 to 7
Outputs:
- first_grad: float32 [27, 512, 512], P(None, 'filt', 'slab')
- second_grad: float32 [27, 512, 512], P(None, 'filt', 'slab')
The draws below stay inside these ranges and needn't reach their ends.
All inputs are finite; a program needn't handle non-finite values.
Results may differ from the reference program's by a relative error of at most 0.0075.
Values may be sent and summed in bfloat16 or wider, within the bound.
No kernel may reach another device: no remote copies, remote signals or barrier semaphores. Data moves between devices by JAX's collectives and lax.ppermute only.
A program may use at most 128 MiB of HBM per device.

```python
import jax
import jax.numpy as jnp
from jax import lax

CHANNELS = 512
CLASSES = 8
HEIGHT = 32
WIDTH = 8
DEPTH = 16
PLANE = 256


def place_ends(entries, key, smallest, top_value):
    dims = entries.shape
    spot = [jax.random.randint(jax.random.fold_in(key, axis), (), 0, dims[axis]) for axis in range(len(dims))]
    entries = entries.at[tuple(spot)].set(smallest)
    longest = dims.index(max(dims))
    spot[longest] = (spot[longest] + 1) % dims[longest]
    return entries.at[tuple(spot)].set(top_value)


def levels(key, dims, cuts, smallest, largest):
    level = 1.0
    for position, parts in cuts:
        heights = jax.random.uniform(jax.random.fold_in(jax.random.fold_in(key, 6), position), (parts,), jnp.float32, smallest / len(cuts), largest / len(cuts))
        level = level * jnp.repeat(jnp.exp(heights), dims[position] // parts).reshape((-1,) + (1,) * (len(dims) - 1 - position))
    return level


def gaussian(rng, shape, scale, bound, cuts=(), kind=jnp.bfloat16):
    array = jax.random.normal(rng, shape, jnp.float32) * scale
    if len(cuts) > 0:
        array = levels(rng, shape, cuts, -0.22, 0.18) * array
    return jnp.clip(array, min=-bound, max=bound).astype(kind)


def setup_inputs(seed: int = 0) -> dict:
    seeds = jax.random.split(jax.random.key(seed), 6)
    return {
        "features": gaussian(seeds[0], (DEPTH, CHANNELS, PLANE), 1.0, 6.0, ((0, 8), (1, 4))),
        "first_weight": gaussian(seeds[1], (27, CHANNELS, CHANNELS), (27 * CHANNELS) ** -0.5, 0.0546875, ((1, 4),)),
        "second_weight": gaussian(seeds[2], (27, CHANNELS, CHANNELS), (27 * CHANNELS) ** -0.5, 0.0546875, ((1, 4),)),
        "head_weight": gaussian(seeds[3], (CLASSES, CHANNELS), CHANNELS ** -0.5, 0.25, ((1, 4),)),
        "labels": place_ends(jax.random.randint(seeds[4], (DEPTH, PLANE), 0, CLASSES), jax.random.fold_in(seeds[4], 1), 0, CLASSES - 1).astype(jnp.int32),
    }


def offset_list():
    found = []
    for depth_off in (-1, 0, 1):
        for row_off in (-1, 0, 1):
            for col_off in (-1, 0, 1):
                found.append((depth_off, row_off, col_off))
    return found

def silu_slope(values):
    sig = jax.nn.sigmoid(values)
    return sig * (1.0 + values * (1.0 - sig))

def shifted(volume, depth_off, row_off, col_off):
    planes = volume.shape[0]
    count_c = volume.shape[1]
    grid = volume.reshape(planes, count_c, HEIGHT, WIDTH)
    padded = jnp.pad(grid, ((1, 1), (0, 0), (1, 1), (1, 1)))
    moved = padded[1 + depth_off:1 + depth_off + planes, :, 1 + row_off:1 + row_off + HEIGHT, 1 + col_off:1 + col_off + WIDTH]
    return moved.reshape(planes, count_c, HEIGHT * WIDTH)

def forward_conv(volume, weight):
    summed = jnp.zeros((volume.shape[0], weight.shape[1], volume.shape[2]), jnp.float32)
    for number, offsets in enumerate(offset_list()):
        moved = shifted(volume, offsets[0], offsets[1], offsets[2]).astype(jnp.float32)
        summed = summed + jnp.einsum('fc,dcp->dfp', weight[number].astype(jnp.float32), moved, precision=lax.Precision.HIGHEST)
    return summed

def backward_conv(grad_out, weight):
    summed = jnp.zeros((grad_out.shape[0], weight.shape[2], grad_out.shape[2]), jnp.float32)
    for number, offsets in enumerate(offset_list()):
        moved = shifted(grad_out, -offsets[0], -offsets[1], -offsets[2]).astype(jnp.float32)
        summed = summed + jnp.einsum('fc,dfp->dcp', weight[number].astype(jnp.float32), moved, precision=lax.Precision.HIGHEST)
    return summed

def weight_grad(grad_out, volume):
    outer = grad_out.astype(jnp.float32)
    pieces = []
    for offsets in offset_list():
        moved = shifted(volume, offsets[0], offsets[1], offsets[2]).astype(jnp.float32)
        pieces.append(jnp.einsum('dfp,dcp->fc', outer, moved, precision=lax.Precision.HIGHEST))
    return jnp.stack(pieces)

def reference(features, first_weight, second_weight, head_weight, labels):
    pre_first = forward_conv(features, first_weight)
    hidden = jax.nn.silu(pre_first).astype(jnp.bfloat16)
    pre_second = forward_conv(hidden, second_weight)
    activated = jax.nn.silu(pre_second).astype(jnp.bfloat16)
    head_f = head_weight.astype(jnp.float32)
    logits = jnp.einsum('kc,dcp->dkp', head_f, activated.astype(jnp.float32), precision=lax.Precision.HIGHEST)
    powers = jnp.exp(logits)
    likely = powers / lax.optimization_barrier(jnp.sum(powers, axis=1, keepdims=True))
    classes_iota = jnp.arange(head_weight.shape[0], dtype=jnp.int32)
    onehot = (labels[:, None, :] == classes_iota[None, :, None]).astype(jnp.float32)
    logit_grad = (likely - onehot).astype(jnp.bfloat16)
    second_in = jnp.einsum('kc,dkp->dcp', head_f, logit_grad.astype(jnp.float32), precision=lax.Precision.HIGHEST)
    second_out_grad = (second_in * silu_slope(pre_second)).astype(jnp.bfloat16)
    second_grad = weight_grad(second_out_grad, hidden)
    hidden_grad = backward_conv(second_out_grad, second_weight)
    first_out_grad = (hidden_grad * silu_slope(pre_first)).astype(jnp.bfloat16)
    first_grad = weight_grad(first_out_grad, features)
    return (first_grad, second_grad)
```

```python
import jax
import jax.numpy as jnp
from jax import lax
from jax.sharding import PartitionSpec as P

WIDTH = 8


def swap(block, axis, step):
    count = lax.axis_size(axis)
    return lax.ppermute(block, axis, [(i, i ^ step) for i in range(count)])


def exchanged(block, axis):
    return [block] + [swap(block, axis, step) for step in range(1, lax.axis_size(axis))]


def gathered(block, axis, dim):
    me = lax.axis_index(axis)
    parts = exchanged(block, axis)
    size = block.shape[dim]
    shape = list(block.shape)
    shape[dim] = size * len(parts)
    whole = jnp.zeros(shape, block.dtype)
    for step, part in enumerate(parts):
        whole = lax.dynamic_update_slice_in_dim(whole, part, (me ^ step) * size, dim)
    return whole


def scattered_sum(terms, axis):
    me = lax.axis_index(axis)
    total = lax.dynamic_index_in_dim(terms, me, 0, False).astype(jnp.float32)
    for step in range(1, lax.axis_size(axis)):
        part = lax.dynamic_index_in_dim(terms, me ^ step, 0, False).astype(jnp.bfloat16)
        total = total + swap(part, axis, step).astype(jnp.float32)
    return total


def faces(volume):
    count = lax.axis_size("slab")
    planes = volume.shape[0]
    before = lax.ppermute(volume[planes - 1 :], "slab", [(i, i + 1) for i in range(count - 1)])
    after = lax.ppermute(volume[:1], "slab", [(i + 1, i) for i in range(count - 1)])
    return jnp.concatenate([before, volume, after], axis=0)


def offset_list():
    return [(a, b, e) for a in (-1, 0, 1) for b in (-1, 0, 1) for e in (-1, 0, 1)]


def silu_slope(values):
    sig = jax.nn.sigmoid(values)
    return sig * (1.0 + values * (1.0 - sig))


def plane_shift(volume, row_off, col_off):
    plane = volume.shape[2]
    padded = jnp.pad(volume, ((0, 0), (0, 0), (WIDTH + 1, WIDTH + 1)))
    begin = WIDTH + 1 + row_off * WIDTH + col_off
    moved = padded[:, :, begin : begin + plane]
    column = lax.iota(jnp.int32, plane) % WIDTH + col_off
    inside = (column >= 0) & (column < WIDTH)
    return jnp.where(inside[None, None, :], moved, jnp.zeros_like(moved))


def tap_view(widened, planes, depth_off, row_off, col_off):
    return plane_shift(widened[1 + depth_off : 1 + depth_off + planes], row_off, col_off)


def forward_conv(widened, weight, planes):
    summed = jnp.zeros((planes, weight.shape[1], widened.shape[2]), jnp.float32)
    for number, offsets in enumerate(offset_list()):
        moved = tap_view(widened, planes, *offsets)
        summed = summed + jnp.einsum(
            "fc,dcp->dfp", weight[number], moved, preferred_element_type=jnp.float32
        )
    return summed


def weight_grad(grad_out, volume):
    depth = volume.shape[0]
    widened = jnp.pad(volume, ((1, 1), (0, 0), (0, 0)))
    pieces = []
    for offsets in offset_list():
        moved = tap_view(widened, depth, *offsets)
        pieces.append(
            jnp.einsum("dfp,dcp->fc", grad_out, moved, preferred_element_type=jnp.float32)
        )
    return jnp.stack(pieces)


def every_plane(volume):
    return lax.all_gather(volume, "slab", axis=0, tiled=True)


def channel_share(volume):
    return lax.all_to_all(volume, "slab", split_axis=1, concat_axis=0, tiled=True)


def shards(features, first_weight, second_weight, head_weight, labels):
    planes, block_c, plane = features.shape
    all_in = gathered(features, "filt", 1)
    share_in = channel_share(all_in)
    pre_first = forward_conv(faces(all_in), first_weight, planes)
    hidden = jax.nn.silu(pre_first).astype(jnp.bfloat16)
    all_hidden = gathered(hidden, "filt", 1)
    share_hidden = channel_share(all_hidden)
    pre_second = forward_conv(faces(all_hidden), second_weight, planes)
    activated = jax.nn.silu(pre_second).astype(jnp.bfloat16)
    partial_logits = jnp.einsum(
        "kc,dcp->dkp", head_weight, activated, preferred_element_type=jnp.float32
    )
    logits = sum(exchanged(partial_logits, "filt"))
    powers = jnp.exp(logits)
    likely = powers / jnp.sum(powers, axis=1, keepdims=True)
    classes_iota = lax.iota(jnp.int32, head_weight.shape[0])
    onehot = (labels[:, None, :] == classes_iota[None, :, None]).astype(jnp.float32)
    logit_grad = (likely - onehot).astype(jnp.bfloat16)
    second_in = jnp.einsum(
        "kc,dkp->dcp", head_weight, logit_grad, preferred_element_type=jnp.float32
    )
    second_out_grad = (second_in * silu_slope(pre_second)).astype(jnp.bfloat16)
    widened_grad = faces(second_out_grad)
    second_grad = weight_grad(every_plane(second_out_grad), share_hidden)
    channels = block_c * lax.axis_size("filt")
    summed = jnp.zeros((channels, planes, plane), jnp.float32)
    for number, (a, b, e) in enumerate(offset_list()):
        moved = tap_view(widened_grad, planes, -a, -b, -e)
        summed = summed + jnp.einsum(
            "fc,dfp->cdp", second_weight[number], moved, preferred_element_type=jnp.float32
        )
    terms = summed.reshape(lax.axis_size("filt"), block_c, planes, plane)
    hidden_grad = jnp.transpose(scattered_sum(terms, "filt"), (1, 0, 2))
    first_out_grad = (hidden_grad * silu_slope(pre_first)).astype(jnp.bfloat16)
    first_grad = weight_grad(every_plane(first_out_grad), share_in)
    return (first_grad, second_grad)


def solution(mesh):
    placed = (
        P("slab", "filt", None),
        P(None, "filt", None),
        P(None, "filt", None),
        P(None, "filt"),
        P("slab", None),
    )
    return jax.shard_map(
        shards,
        mesh=mesh,
        in_specs=placed,
        out_specs=(P(None, "filt", "slab"), P(None, "filt", "slab")),
        check_vma=False,
    )
```

```python
import functools

import jax
import jax.numpy as jnp
from jax import lax
from jax.experimental import pallas as pl
from jax.experimental.pallas import tpu as pltpu
from jax.sharding import PartitionSpec as P

WIDTH = 8
SHIFTS = [(b, e) for b in (-1, 0, 1) for e in (-1, 0, 1)]
LIMIT = 48 * 1024 * 1024
VMEM = pl.BlockSpec(memory_space=pltpu.VMEM)
SMEM = pl.BlockSpec(memory_space=pltpu.SMEM)


def swap(block, axis, step):
    count = lax.axis_size(axis)
    return lax.ppermute(block, axis, [(i, i ^ step) for i in range(count)])


def exchanged(block, axis):
    return [block] + [swap(block, axis, step) for step in range(1, lax.axis_size(axis))]


def neighbours(first, last):
    count = lax.axis_size("slab")
    before = lax.ppermute(last, "slab", [(i, i + 1) for i in range(count - 1)])
    after = lax.ppermute(first, "slab", [(i + 1, i) for i in range(count - 1)])
    return before, after


def every_plane(block):
    count = lax.axis_size("slab")
    me = lax.axis_index("slab")
    if count == 1:
        return [block], [me]
    other = swap(block, "slab", 1)
    steps = list(range(2, count, 2))
    far = [swap(block, "slab", step) for step in steps]
    crossed = [swap(part, "slab", 1) for part in far]
    blocks = [block, other] + far + crossed
    owners = [me, me ^ 1] + [me ^ step for step in steps] + [me ^ step ^ 1 for step in steps]
    return blocks, owners


def call(body, out_shape, cost, **options):
    flops, moved = cost
    return pl.pallas_call(
        body,
        out_shape=out_shape,
        cost_estimate=pl.CostEstimate(flops=flops, bytes_accessed=moved, transcendentals=0),
        compiler_params=pltpu.CompilerParams(vmem_limit_bytes=LIMIT),
        **options,
    )


def struct(shape, dtype):
    return jax.ShapeDtypeStruct(tuple(shape), dtype)


def inside(shape, axis, b, e):
    spot = lax.broadcasted_iota(jnp.int32, shape, axis)
    column = spot % WIDTH + e
    moved = spot + WIDTH * b
    return (column >= 0) & (column < WIDTH) & (moved >= 0) & (moved < shape[axis])


def shifted(values, axis, b, e):
    if b == 0 and e == 0:
        return values
    size = values.shape[axis]
    turned = pltpu.roll(values, (-(WIDTH * b + e)) % size, axis)
    return jnp.where(inside(values.shape, axis, b, e), turned, 0.0)


def fold_shifts(products):
    rows = products.shape[0] // len(SHIFTS)
    total = None
    for number, (b, e) in enumerate(SHIFTS):
        term = shifted(products[number * rows : (number + 1) * rows, :], 1, b, e)
        total = term if total is None else total + term
    return total


def dot(left, right):
    return jnp.dot(left, right, preferred_element_type=jnp.float32)


def flat(ref):
    block = ref[...]
    return block.reshape(block.shape[0] * block.shape[1], block.shape[2])


def assemble_body(count, me_ref, *refs):
    parts, (whole_ref, first_ref, last_ref) = refs[:count], refs[count:]
    planes, size = parts[0].shape[0], parts[0].shape[1]
    for step in range(count):
        place = pl.ds(pl.multiple_of((me_ref[0] ^ step) * size, size), size)
        block = parts[step][...]
        whole_ref[:, place, :] = block
        first_ref[:, place, :] = block[:1]
        last_ref[:, place, :] = block[planes - 1 :]


def assemble(parts):
    planes, size, plane = parts[0].shape
    count = len(parts)
    me = lax.axis_index("filt").astype(jnp.int32).reshape(1)
    shapes = [struct((n, size * count, plane), parts[0].dtype) for n in (planes, 1, 1)]
    return call(
        functools.partial(assemble_body, count),
        shapes,
        (0, 4 * planes * size * count * plane),
        in_specs=[SMEM] + [VMEM] * count,
        out_specs=[VMEM] * 3,
    )(me, *parts)


def forward_own_body(planes, volume_ref, weight_ref, out_ref, acc_ref):
    step = pl.program_id(0)
    weight = flat(weight_ref)
    for number, a in enumerate((0, 1, -1)):

        @pl.when(step == number)
        def _():
            for j in range(planes):
                if 0 <= j + a < planes:
                    product = dot(weight, volume_ref[j + a])
                    acc_ref[j] = product if a == 0 else acc_ref[j] + product

    @pl.when(step == 2)
    def _():
        for j in range(planes):
            out_ref[j] = fold_shifts(acc_ref.at[j])


def forward_own(volume, weight):
    planes, channels, plane = volume.shape
    filters = weight.shape[1]
    return call(
        functools.partial(forward_own_body, planes),
        struct((planes, filters, plane), jnp.float32),
        (2 * 9 * filters * channels * plane * (3 * planes - 2), weight.size * 2),
        grid=(3,),
        in_specs=[
            pl.BlockSpec((planes, channels, plane), lambda i: (0, 0, 0)),
            pl.BlockSpec((9, filters, channels), lambda i: ((i + 1) % 3, 0, 0)),
        ],
        out_specs=pl.BlockSpec((planes, filters, plane), lambda i: (0, 0, 0)),
        scratch_shapes=[pltpu.VMEM((planes, 9 * filters, plane), jnp.float32)],
    )(volume, weight)


def silu_and_slope(values):
    sig = 1.0 / (1.0 + jnp.exp(-values))
    return values * sig, sig * (1.0 + values * (1.0 - sig))


def forward_rest_body(planes, has_head, before_ref, after_ref, weight_ref, own_ref, *refs):
    if has_head:
        head_ref, slope_ref, made_ref, acc_ref = refs
    else:
        slope_ref, made_ref, first_ref, last_ref, acc_ref = refs
    step = pl.program_id(0)
    weight = flat(weight_ref)

    @pl.when(step == 0)
    def _():
        acc_ref[...] = dot(weight, before_ref[0])
        for j in range(1, planes):
            slope_ref[j] = own_ref[j]
        slope_ref[0] = own_ref[0] + fold_shifts(acc_ref)

    @pl.when(step == 1)
    def _():
        acc_ref[...] = dot(weight, after_ref[0])
        slope_ref[planes - 1] = slope_ref[planes - 1] + fold_shifts(acc_ref)
        for j in range(planes):
            value, slope = silu_and_slope(slope_ref[j])
            value = value.astype(jnp.bfloat16)
            slope_ref[j] = slope
            if has_head:
                made_ref[j] = dot(head_ref[...], value)
            else:
                made_ref[j] = value


def forward_rest(before, after, weight, own, head=None):
    planes, filters, plane = own.shape
    channels = weight.shape[2]
    whole = lambda *dims: pl.BlockSpec(dims, lambda i: (0,) * len(dims))
    outs = [struct(own.shape, jnp.float32)]
    ins = [before, after, weight, own]
    specs = [
        whole(1, channels, plane),
        whole(1, channels, plane),
        pl.BlockSpec((9, filters, channels), lambda i: (2 * i, 0, 0)),
        whole(*own.shape),
    ]
    if head is None:
        outs.append(struct(own.shape, jnp.bfloat16))
        refs_extra = 2
    else:
        ins.append(head)
        specs.append(whole(*head.shape))
        outs.append(struct((planes, head.shape[0], plane), jnp.float32))
    body = functools.partial(forward_rest_body, planes, head is not None)
    if head is None:
        body = functools.partial(forward_rest_plain, planes)
    return call(
        body,
        outs,
        (2 * 9 * filters * channels * plane * 2, weight.size * 4 // 3),
        grid=(2,),
        in_specs=specs,
        out_specs=[whole(*out.shape) for out in outs],
        scratch_shapes=[pltpu.VMEM((9 * filters, plane), jnp.float32)],
    )(*ins)


def forward_rest_plain(planes, before_ref, after_ref, weight_ref, own_ref, slope_ref, made_ref, acc_ref):
    forward_rest_body(
        planes, False, before_ref, after_ref, weight_ref, own_ref, slope_ref, made_ref, None, None, acc_ref
    )


def loss_body(count, labels_ref, head_ref, slope_ref, *refs):
    parts, grad_ref = refs[:count], refs[count]
    for j in range(grad_ref.shape[0]):
        logits = parts[0][j]
        for part in parts[1:]:
            logits = logits + part[j]
        powers = jnp.exp(logits)
        likely = powers / jnp.sum(powers, axis=0, keepdims=True)
        classes = lax.broadcasted_iota(jnp.int32, logits.shape, 0)
        onehot = (labels_ref[j] == classes).astype(jnp.float32)
        logit_grad = (likely - onehot).astype(jnp.bfloat16).astype(jnp.float32)
        back = lax.dot_general(
            head_ref[...].astype(jnp.float32),
            logit_grad,
            (((0,), (0,)), ((), ())),
            preferred_element_type=jnp.float32,
        )
        grad_ref[j] = (back * slope_ref[j]).astype(jnp.bfloat16)


def loss_grad(parts, labels, head, slope):
    planes, plane = labels.shape
    return call(
        functools.partial(loss_body, len(parts)),
        struct(slope.shape, jnp.bfloat16),
        (2 * slope.size * head.shape[0], slope.size * 6),
        in_specs=[VMEM] * (3 + len(parts)),
        out_specs=VMEM,
    )(labels.reshape(planes, 1, plane), head, slope, *parts)


def spread_back(grad, spread_ref):
    filters = grad.shape[0]
    turned = grad.astype(jnp.float32).T
    for number, (b, e) in enumerate(SHIFTS):
        moved = shifted(turned, 0, -b, -e).astype(jnp.bfloat16)
        spread_ref[:, number * filters : (number + 1) * filters] = moved


def backward_own_body(planes, grad_ref, weight_ref, out_ref, spread_ref):
    step = pl.program_id(0)
    weight = flat(weight_ref)

    @pl.when(step == 0)
    def _():
        for j in range(planes):
            spread_back(grad_ref[j], spread_ref.at[j])

    for number, a in enumerate((0, 1, -1)):

        @pl.when(step == number)
        def _():
            for j in range(planes):
                if 0 <= j - a < planes:
                    product = dot(spread_ref[j - a], weight)
                    out_ref[j] = product if a == 0 else out_ref[j] + product


def backward_own(grad, weight):
    planes, filters, plane = grad.shape
    channels = weight.shape[2]
    return call(
        functools.partial(backward_own_body, planes),
        struct((planes, plane, channels), jnp.float32),
        (2 * 9 * filters * channels * plane * (3 * planes - 2), weight.size * 2),
        grid=(3,),
        in_specs=[
            pl.BlockSpec(grad.shape, lambda i: (0, 0, 0)),
            pl.BlockSpec((9, filters, channels), lambda i: ((i + 1) % 3, 0, 0)),
        ],
        out_specs=pl.BlockSpec((planes, plane, channels), lambda i: (0, 0, 0)),
        scratch_shapes=[pltpu.VMEM((planes, plane, 9 * filters), jnp.bfloat16)],
    )(grad, weight)


def backward_rest_body(planes, count, me_ref, before_ref, after_ref, weight_ref, own_ref, *refs):
    kept_ref, sent, (spread_ref, total_ref) = refs[0], refs[1:count], refs[count:]
    step = pl.program_id(0)
    size = kept_ref.shape[2]
    weight = flat(weight_ref)

    def place(j, product):
        for block in range(count):
            total_ref[block, j] = product[:, block * size : (block + 1) * size]

    @pl.when(step == 0)
    def _():
        spread_back(after_ref[0], spread_ref)
        place(planes - 1, own_ref[planes - 1] + dot(spread_ref[...], weight))
        for j in range(planes - 1):
            place(j, own_ref[j])

    @pl.when(step == 1)
    def _():
        spread_back(before_ref[0], spread_ref)
        product = dot(spread_ref[...], weight)
        for block in range(count):
            total_ref[block, 0] = total_ref[block, 0] + product[:, block * size : (block + 1) * size]
        kept_ref[...] = total_ref[me_ref[0]]
        for number in range(1, count):
            sent[number - 1][...] = total_ref[me_ref[0] ^ number].astype(jnp.bfloat16)


def backward_rest(before, after, weight, own, count):
    planes, plane, channels = own.shape
    filters = weight.shape[1]
    size = channels // count
    me = lax.axis_index("filt").astype(jnp.int32).reshape(1)
    whole = lambda *dims: pl.BlockSpec(dims, lambda i: (0,) * len(dims))
    outs = [struct((planes, plane, size), jnp.float32)]
    outs += [struct((planes, plane, size), jnp.bfloat16)] * (count - 1)
    return call(
        functools.partial(backward_rest_body, planes, count),
        outs,
        (2 * 9 * filters * channels * plane * 2, weight.size * 4 // 3),
        grid=(2,),
        in_specs=[
            SMEM,
            whole(1, filters, plane),
            whole(1, filters, plane),
            pl.BlockSpec((9, filters, channels), lambda i: (2 * i, 0, 0)),
            whole(*own.shape),
        ],
        out_specs=[whole(*out.shape) for out in outs],
        scratch_shapes=[
            pltpu.VMEM((plane, 9 * filters), jnp.bfloat16),
            pltpu.VMEM((count, planes, plane, size), jnp.float32),
        ],
    )(me, before, after, weight, own)


def first_grad_body(count, slope_ref, *refs):
    parts, out_ref = refs[:count], refs[count]
    for j in range(out_ref.shape[0]):
        total = parts[0][j]
        for part in parts[1:]:
            total = total + part[j].astype(jnp.float32)
        out_ref[j] = (total.T * slope_ref[j]).astype(jnp.bfloat16)


def first_out(parts, slope):
    return call(
        functools.partial(first_grad_body, len(parts)),
        struct(slope.shape, jnp.bfloat16),
        (slope.size * 4, slope.size * 14),
        in_specs=[VMEM] * (1 + len(parts)),
        out_specs=VMEM,
    )(slope, *parts)


def weight_grad_body(count, group, owner_ref, volume_ref, *refs):
    parts, (out_ref, grad_ref, spread_ref, acc_ref) = refs[:count], refs[count:]
    depth, channels, plane = volume_ref.shape
    planes, filters = parts[0].shape[0], parts[0].shape[1]
    zero = jnp.zeros((filters, plane), jnp.bfloat16)
    grad_ref[0] = zero
    grad_ref[depth + 1] = zero
    for number in range(count):
        for j in range(planes):
            grad_ref[1 + owner_ref[number] * planes + j] = parts[number][j]
    acc_ref[...] = jnp.zeros_like(acc_ref)

    def planes_step(turn, _):
        total = None
        for k in range(group):
            d = turn * group + k
            values = volume_ref[d].astype(jnp.float32)
            for number, (b, e) in enumerate(SHIFTS):
                moved = shifted(values, 1, b, e).astype(jnp.bfloat16)
                spread_ref[k, number * channels : (number + 1) * channels, :] = moved
            grads = grad_ref[pl.ds(d, 3)].reshape(3 * filters, plane)
            product = lax.dot_general(
                spread_ref[k], grads, (((1,), (1,)), ((), ())), preferred_element_type=jnp.float32
            )
            total = product if total is None else total + product
        acc_ref[...] += total
        return 0

    lax.fori_loop(0, depth // group, planes_step, 0)
    for r in range(3):
        for number in range(len(SHIFTS)):
            out_ref[(2 - r) * 9 + number] = acc_ref[
                number * channels : (number + 1) * channels, r * filters : (r + 1) * filters
            ]


def weight_grad(parts, owners, volume):
    depth, channels, plane = volume.shape
    filters = parts[0].shape[1]
    group = 4 if depth % 4 == 0 else 1
    turned = call(
        functools.partial(weight_grad_body, len(parts), group),
        struct((27, channels, filters), jnp.float32),
        (2 * 27 * filters * channels * plane * depth, 27 * channels * filters * 4 + volume.size * 6),
        in_specs=[SMEM] + [VMEM] * (1 + len(parts)),
        out_specs=VMEM,
        scratch_shapes=[
            pltpu.VMEM((depth + 2, filters, plane), jnp.bfloat16),
            pltpu.VMEM((group, 9 * channels, plane), jnp.bfloat16),
            pltpu.VMEM((9 * channels, 3 * filters), jnp.float32),
        ],
    )(jnp.stack(owners).astype(jnp.int32), volume, *parts)
    return jnp.transpose(turned, (0, 2, 1))


def channel_share(volume):
    return lax.all_to_all(volume, "slab", split_axis=1, concat_axis=0, tiled=True)


def shards(features, first_weight, second_weight, head_weight, labels):
    count = lax.axis_size("filt")
    all_in, first_in, last_in = assemble(exchanged(features, "filt"))
    before, after = neighbours(first_in, last_in)
    own = forward_own(all_in, first_weight)
    slope_first, hidden = forward_rest(before, after, first_weight, own)

    all_hidden, first_hidden, last_hidden = assemble(exchanged(hidden, "filt"))
    before, after = neighbours(first_hidden, last_hidden)
    own = forward_own(all_hidden, second_weight)
    slope_second, logits = forward_rest(before, after, second_weight, own, head_weight)

    share_in = channel_share(all_in)
    share_hidden = channel_share(all_hidden)

    second_out = loss_grad(exchanged(logits, "filt"), labels, head_weight, slope_second)
    before, after = neighbours(second_out[:1], second_out[-1:])
    own = backward_own(second_out, second_weight)
    kept, *sent = backward_rest(before, after, second_weight, own, count)
    parts = [kept] + [swap(part, "filt", 1 + number) for number, part in enumerate(sent)]
    first_out_grad = first_out(parts, slope_first)

    all_second = lax.all_gather(second_out, "slab", axis=0, tiled=True)
    second_grad = weight_grad([all_second], [jnp.int32(0)], share_hidden)
    first_grad = weight_grad(*every_plane(first_out_grad), share_in)
    return (first_grad, second_grad)


def solution(mesh):
    placed = (
        P("slab", "filt", None),
        P(None, "filt", None),
        P(None, "filt", None),
        P(None, "filt"),
        P("slab", None),
    )
    return jax.shard_map(
        shards,
        mesh=mesh,
        in_specs=placed,
        out_specs=(P(None, "filt", "slab"), P(None, "filt", "slab")),
        check_vma=False,
    )
```

```python
import functools

import jax
import jax.numpy as jnp
from jax import lax
from jax.experimental import pallas as pl
from jax.experimental.pallas import tpu as pltpu
from jax.sharding import PartitionSpec as P

WIDTH = 8
SHIFTS = [(b, e) for b in (-1, 0, 1) for e in (-1, 0, 1)]
LIMIT = 20 * 1024 * 1024
VMEM = pl.BlockSpec(memory_space=pltpu.VMEM)
SMEM = pl.BlockSpec(memory_space=pltpu.SMEM)


def swap(block, axis, step):
    count = lax.axis_size(axis)
    return lax.ppermute(block, axis, [(i, i ^ step) for i in range(count)])


def exchanged(block, axis):
    return [block] + [swap(block, axis, step) for step in range(1, lax.axis_size(axis))]


def neighbours(first, last):
    count = lax.axis_size("slab")
    before = lax.ppermute(last, "slab", [(i, i + 1) for i in range(count - 1)])
    after = lax.ppermute(first, "slab", [(i + 1, i) for i in range(count - 1)])
    return before, after


def every_plane(block):
    count = lax.axis_size("slab")
    me = lax.axis_index("slab")
    if count == 1:
        return [block], [me]
    other = swap(block, "slab", 1)
    steps = list(range(2, count, 2))
    far = [swap(block, "slab", step) for step in steps]
    crossed = [swap(part, "slab", 1) for part in far]
    blocks = [block, other] + far + crossed
    owners = [me, me ^ 1] + [me ^ step for step in steps] + [me ^ step ^ 1 for step in steps]
    return blocks, owners


def call(body, out_shape, cost, **options):
    flops, moved = cost
    return pl.pallas_call(
        body,
        out_shape=out_shape,
        cost_estimate=pl.CostEstimate(flops=flops, bytes_accessed=moved, transcendentals=0),
        compiler_params=pltpu.CompilerParams(vmem_limit_bytes=LIMIT),
        **options,
    )


def struct(shape, dtype):
    return jax.ShapeDtypeStruct(tuple(shape), dtype)


def inside(shape, axis, b, e):
    spot = lax.broadcasted_iota(jnp.int32, shape, axis)
    column = spot % WIDTH + e
    moved = spot + WIDTH * b
    return (column >= 0) & (column < WIDTH) & (moved >= 0) & (moved < shape[axis])


def shifted(values, axis, b, e):
    if b == 0 and e == 0:
        return values
    size = values.shape[axis]
    turned = pltpu.roll(values, (-(WIDTH * b + e)) % size, axis)
    return jnp.where(inside(values.shape, axis, b, e), turned, 0.0)


def fold_shifts(products):
    rows = products.shape[0] // len(SHIFTS)
    total = None
    for number, (b, e) in enumerate(SHIFTS):
        term = shifted(products[number * rows : (number + 1) * rows, :], 1, b, e)
        total = term if total is None else total + term
    return total


def dot(left, right):
    return jnp.dot(left, right, preferred_element_type=jnp.float32)


def assemble_body(count, shares, me_ref, *refs):
    parts, other_refs = refs[:count], refs[count:]
    whole_ref, first_ref, last_ref = other_refs[-4:-1] if shares else other_refs
    planes, size = parts[0].shape[0], parts[0].shape[1]
    for step in range(count):
        place = pl.ds(pl.multiple_of((me_ref[0] ^ step) * size, size), size)
        block = parts[step][...]
        whole_ref[:, place, :] = block
        first_ref[:, place, :] = block[:1]
        last_ref[:, place, :] = block[planes - 1 :]
    if shares:
        earlier_ref, share_ref = other_refs[0], other_refs[-1]
        rows = share_ref.shape[2]
        for slab in range(shares):
            share_ref[slab, :planes] = earlier_ref[:, slab * rows : (slab + 1) * rows, :]
            share_ref[slab, planes:] = whole_ref[:, slab * rows : (slab + 1) * rows, :]


def assemble(parts, earlier=None):
    planes, size, plane = parts[0].shape
    count = len(parts)
    channels = size * count
    me = lax.axis_index("filt").astype(jnp.int32).reshape(1)
    kind = parts[0].dtype
    outs = [struct((n, channels, plane), kind) for n in (planes, 1, 1)]
    shares = 0
    ins = [me, *parts]
    if earlier is not None:
        shares = lax.axis_size("slab")
        ins.append(earlier)
        outs.append(struct((shares, 2 * planes, channels // shares, plane), kind))
    return call(
        functools.partial(assemble_body, count, shares),
        outs,
        (0, 4 * planes * channels * plane),
        in_specs=[SMEM] + [VMEM] * (len(ins) - 1),
        out_specs=[VMEM] * len(outs),
    )(*ins)


def taps(weight_ref, a):
    block = weight_ref[9 * (a + 1) : 9 * (a + 2)]
    return block.reshape(block.shape[0] * block.shape[1], block.shape[2])


def forward_own_body(planes, volume_ref, weight_ref, out_ref, acc_ref):
    for a in (0, 1, -1):
        weight = taps(weight_ref, a)
        for j in range(planes):
            if 0 <= j + a < planes:
                product = dot(weight, volume_ref[j + a])
                acc_ref[j] = product if a == 0 else acc_ref[j] + product
    for j in range(planes):
        out_ref[j] = fold_shifts(acc_ref.at[j])


def forward_own(volume, weight):
    planes, channels, plane = volume.shape
    filters = weight.shape[1]
    return call(
        functools.partial(forward_own_body, planes),
        struct((planes, filters, plane), jnp.float32),
        (2 * 9 * filters * channels * plane * (3 * planes - 2), weight.size * 2),
        in_specs=[VMEM, VMEM],
        out_specs=VMEM,
        scratch_shapes=[pltpu.VMEM((planes, 9 * filters, plane), jnp.float32)],
    )(volume, weight)


def silu_and_slope(values):
    sig = 1.0 / (1.0 + jnp.exp(-values))
    return values * sig, sig * (1.0 + values * (1.0 - sig))


def forward_rest_body(planes, before_ref, after_ref, weight_ref, own_ref, *refs):
    head_ref = refs[0] if len(refs) == 4 else None
    slope_ref, made_ref, acc_ref = refs[-3:]
    acc_ref[0] = dot(taps(weight_ref, -1), before_ref[0])
    acc_ref[1] = dot(taps(weight_ref, 1), after_ref[0])
    for j in range(planes):
        total = own_ref[j]
        if j == 0:
            total = total + fold_shifts(acc_ref.at[0])
        if j == planes - 1:
            total = total + fold_shifts(acc_ref.at[1])
        value, slope = silu_and_slope(total)
        value = value.astype(jnp.bfloat16)
        slope_ref[j] = slope
        made_ref[j] = value if head_ref is None else dot(head_ref[...], value)


def forward_rest(before, after, weight, own, head=None):
    planes, filters, plane = own.shape
    channels = weight.shape[2]
    ins = [before, after, weight, own]
    if head is None:
        made = struct(own.shape, jnp.bfloat16)
    else:
        ins.append(head)
        made = struct((planes, head.shape[0], plane), jnp.float32)
    return call(
        functools.partial(forward_rest_body, planes),
        [struct(own.shape, jnp.float32), made],
        (2 * 9 * filters * channels * plane * 2, weight.size * 4 // 3),
        in_specs=[VMEM] * len(ins),
        out_specs=[VMEM] * 2,
        scratch_shapes=[pltpu.VMEM((2, 9 * filters, plane), jnp.float32)],
    )(*ins)


def loss_body(count, labels_ref, head_ref, slope_ref, *refs):
    parts, grad_ref = refs[:count], refs[count]
    for j in range(grad_ref.shape[0]):
        logits = parts[0][j]
        for part in parts[1:]:
            logits = logits + part[j]
        powers = jnp.exp(logits)
        likely = powers / jnp.sum(powers, axis=0, keepdims=True)
        classes = lax.broadcasted_iota(jnp.int32, logits.shape, 0)
        onehot = (labels_ref[j] == classes).astype(jnp.float32)
        logit_grad = (likely - onehot).astype(jnp.bfloat16).astype(jnp.float32)
        back = lax.dot_general(
            head_ref[...].astype(jnp.float32),
            logit_grad,
            (((0,), (0,)), ((), ())),
            preferred_element_type=jnp.float32,
        )
        grad_ref[j] = (back * slope_ref[j]).astype(jnp.bfloat16)


def loss_grad(parts, labels, head, slope):
    planes, plane = labels.shape
    return call(
        functools.partial(loss_body, len(parts)),
        struct(slope.shape, jnp.bfloat16),
        (2 * slope.size * head.shape[0], slope.size * 6),
        in_specs=[VMEM] * (3 + len(parts)),
        out_specs=VMEM,
    )(labels.reshape(planes, 1, plane), head, slope, *parts)


def spread_back(grad, spread_ref):
    filters = grad.shape[0]
    turned = grad.astype(jnp.float32).T
    for number, (b, e) in enumerate(SHIFTS):
        moved = shifted(turned, 0, -b, -e).astype(jnp.bfloat16)
        spread_ref[:, number * filters : (number + 1) * filters] = moved


def backward_own_body(planes, grad_ref, weight_ref, out_ref, spread_ref):
    for j in range(planes):
        spread_back(grad_ref[j], spread_ref.at[j])
    for a in (0, 1, -1):
        weight = taps(weight_ref, a)
        for j in range(planes):
            if 0 <= j - a < planes:
                product = dot(spread_ref[j - a], weight)
                out_ref[j] = product if a == 0 else out_ref[j] + product


def backward_own(grad, weight):
    planes, filters, plane = grad.shape
    channels = weight.shape[2]
    return call(
        functools.partial(backward_own_body, planes),
        struct((planes, plane, channels), jnp.float32),
        (2 * 9 * filters * channels * plane * (3 * planes - 2), weight.size * 2),
        in_specs=[VMEM, VMEM],
        out_specs=VMEM,
        scratch_shapes=[pltpu.VMEM((planes, plane, 9 * filters), jnp.bfloat16)],
    )(grad, weight)


def backward_rest_body(planes, count, me_ref, before_ref, after_ref, weight_ref, own_ref, *refs):
    kept_ref, sent, (spread_ref, total_ref) = refs[0], refs[1:count], refs[count:]
    size = kept_ref.shape[2]
    spread_back(before_ref[0], spread_ref.at[0])
    spread_back(after_ref[0], spread_ref.at[1])
    for j in range(planes):
        total = own_ref[j]
        if j == 0:
            total = total + dot(spread_ref[0], taps(weight_ref, 1))
        if j == planes - 1:
            total = total + dot(spread_ref[1], taps(weight_ref, -1))
        for block in range(count):
            total_ref[block, j] = total[:, block * size : (block + 1) * size]
    kept_ref[...] = total_ref[me_ref[0]]
    for number in range(1, count):
        sent[number - 1][...] = total_ref[me_ref[0] ^ number].astype(jnp.bfloat16)


def backward_rest(before, after, weight, own, count):
    planes, plane, channels = own.shape
    filters = weight.shape[1]
    size = channels // count
    me = lax.axis_index("filt").astype(jnp.int32).reshape(1)
    outs = [struct((planes, plane, size), jnp.float32)]
    outs += [struct((planes, plane, size), jnp.bfloat16)] * (count - 1)
    return call(
        functools.partial(backward_rest_body, planes, count),
        outs,
        (2 * 9 * filters * channels * plane * 2, weight.size * 4 // 3),
        in_specs=[SMEM] + [VMEM] * 4,
        out_specs=[VMEM] * count,
        scratch_shapes=[
            pltpu.VMEM((2, plane, 9 * filters), jnp.bfloat16),
            pltpu.VMEM((count, planes, plane, size), jnp.float32),
        ],
    )(me, before, after, weight, own)


def first_grad_body(count, slope_ref, *refs):
    parts, out_ref = refs[:count], refs[count]
    for j in range(out_ref.shape[0]):
        total = parts[0][j]
        for part in parts[1:]:
            total = total + part[j].astype(jnp.float32)
        out_ref[j] = (total.T * slope_ref[j]).astype(jnp.bfloat16)


def first_out(parts, slope):
    return call(
        functools.partial(first_grad_body, len(parts)),
        struct(slope.shape, jnp.bfloat16),
        (slope.size * 4, slope.size * 14),
        in_specs=[VMEM] * (1 + len(parts)),
        out_specs=VMEM,
    )(slope, *parts)


def weight_grad_body(count, offset, owner_ref, volume_ref, *refs):
    parts, (out_ref, grad_ref, spread_ref, acc_ref) = refs[:count], refs[count:]
    slabs, both, channels, plane = volume_ref.shape
    planes, filters = both // 2, parts[0].shape[1]
    depth = slabs * planes
    zero = jnp.zeros((filters, plane), jnp.bfloat16)
    grad_ref[0] = zero
    grad_ref[depth + 1] = zero
    for number in range(count):
        base = 1 + owner_ref[number] * planes
        for j in range(parts[number].shape[0]):
            grad_ref[base + j] = parts[number][j]
    acc_ref[...] = jnp.zeros_like(acc_ref)
    group = 2 if slabs % 2 == 0 else 1

    def slabs_step(turn, _):
        total = None
        for k in range(group):
            for j in range(planes):
                slab = turn * group + k
                values = volume_ref[slab, offset + j].astype(jnp.float32)
                for number, (b, e) in enumerate(SHIFTS):
                    moved = shifted(values, 1, b, e).astype(jnp.bfloat16)
                    spread_ref[k * planes + j, number * channels : (number + 1) * channels, :] = moved
                grads = grad_ref[pl.ds(slab * planes + j, 3)].reshape(3 * filters, plane)
                product = lax.dot_general(
                    spread_ref[k * planes + j],
                    grads,
                    (((1,), (1,)), ((), ())),
                    preferred_element_type=jnp.float32,
                )
                total = product if total is None else total + product
        acc_ref[...] += total
        return 0

    lax.fori_loop(0, slabs // group, slabs_step, 0)
    for r in range(3):
        for number in range(len(SHIFTS)):
            out_ref[(2 - r) * 9 + number] = acc_ref[
                number * channels : (number + 1) * channels, r * filters : (r + 1) * filters
            ]


def weight_grad(parts, owners, volume, offset):
    slabs, both, channels, plane = volume.shape
    filters = parts[0].shape[1]
    depth = slabs * both // 2
    turned = call(
        functools.partial(weight_grad_body, len(parts), offset),
        struct((27, channels, filters), jnp.float32),
        (2 * 27 * filters * channels * plane * depth, 27 * channels * filters * 4 + volume.size * 6),
        in_specs=[SMEM] + [VMEM] * (1 + len(parts)),
        out_specs=VMEM,
        scratch_shapes=[
            pltpu.VMEM((depth + 2, filters, plane), jnp.bfloat16),
            pltpu.VMEM((both, 9 * channels, plane), jnp.bfloat16),
            pltpu.VMEM((9 * channels, 3 * filters), jnp.float32),
        ],
    )(jnp.stack(owners).astype(jnp.int32), volume, *parts)
    return jnp.transpose(turned, (0, 2, 1))


def shards(features, first_weight, second_weight, head_weight, labels):
    planes = features.shape[0]
    count = lax.axis_size("filt")
    all_in, first_in, last_in = assemble(exchanged(features, "filt"))
    before, after = neighbours(first_in, last_in)
    own = forward_own(all_in, first_weight)
    slope_first, hidden = forward_rest(before, after, first_weight, own)

    all_hidden, first_hidden, last_hidden, share = assemble(exchanged(hidden, "filt"), all_in)
    before, after = neighbours(first_hidden, last_hidden)
    share = lax.all_to_all(share, "slab", split_axis=0, concat_axis=0, tiled=True)
    own = forward_own(all_hidden, second_weight)
    slope_second, logits = forward_rest(before, after, second_weight, own, head_weight)

    second_out = loss_grad(exchanged(logits, "filt"), labels, head_weight, slope_second)
    before, after = neighbours(second_out[:1], second_out[-1:])
    own = backward_own(second_out, second_weight)
    kept, *sent = backward_rest(before, after, second_weight, own, count)
    parts = [kept] + [swap(part, "filt", 1 + number) for number, part in enumerate(sent)]
    first_out_grad = first_out(parts, slope_first)

    all_second = lax.all_gather(second_out, "slab", axis=0, tiled=True)
    second_grad = weight_grad([all_second], [jnp.int32(0)], share, planes)
    first_grad = weight_grad(*every_plane(first_out_grad), share, 0)
    return (first_grad, second_grad)


def solution(mesh):
    placed = (
        P("slab", "filt", None),
        P(None, "filt", None),
        P(None, "filt", None),
        P(None, "filt"),
        P("slab", None),
    )
    return jax.shard_map(
        shards,
        mesh=mesh,
        in_specs=placed,
        out_specs=(P(None, "filt", "slab"), P(None, "filt", "slab")),
        check_vma=False,
    )
```

```python
import functools

import jax
import jax.numpy as jnp
from jax import lax
from jax.experimental import pallas as pl
from jax.experimental.pallas import tpu as pltpu
from jax.sharding import PartitionSpec as P

WIDTH = 8
SHIFTS = [(b, e) for b in (-1, 0, 1) for e in (-1, 0, 1)]
LIMIT = 20 * 1024 * 1024
VMEM = pl.BlockSpec(memory_space=pltpu.VMEM)
SMEM = pl.BlockSpec(memory_space=pltpu.SMEM)


def swap(block, axis, step):
    count = lax.axis_size(axis)
    return lax.ppermute(block, axis, [(i, i ^ step) for i in range(count)])


def exchanged(block, axis):
    return [block] + [swap(block, axis, step) for step in range(1, lax.axis_size(axis))]


def core():
    return lax.axis_index("slab").astype(jnp.int32) % 2


def halo(volume):
    count = lax.axis_size("slab")
    planes = volume.shape[0]
    other = swap(volume, "slab", 1)
    passed = lax.dynamic_slice_in_dim(other, (1 - core()) * (planes - 1), 1, 0)
    pairs = [(i, i + 2) for i in range(0, count - 2, 2)] + [(i, i - 2) for i in range(3, count, 2)]
    return other, lax.ppermute(passed, "slab", pairs)


def every_plane(block):
    count = lax.axis_size("slab")
    me = lax.axis_index("slab")
    if count == 1:
        return [block], [me]
    other = swap(block, "slab", 1)
    steps = list(range(2, count, 2))
    far = [swap(block, "slab", step) for step in steps]
    crossed = [swap(part, "slab", 1) for part in far]
    blocks = [block, other] + far + crossed
    owners = [me, me ^ 1] + [me ^ step for step in steps] + [me ^ step ^ 1 for step in steps]
    return blocks, owners


def call(body, out_shape, cost, **options):
    flops, moved = cost
    return pl.pallas_call(
        body,
        out_shape=out_shape,
        cost_estimate=pl.CostEstimate(flops=flops, bytes_accessed=moved, transcendentals=0),
        compiler_params=pltpu.CompilerParams(vmem_limit_bytes=LIMIT),
        **options,
    )


def struct(shape, dtype):
    return jax.ShapeDtypeStruct(tuple(shape), dtype)


def inside(shape, axis, b, e):
    spot = lax.broadcasted_iota(jnp.int32, shape, axis)
    column = spot % WIDTH + e
    moved = spot + WIDTH * b
    return (column >= 0) & (column < WIDTH) & (moved >= 0) & (moved < shape[axis])


def shifted(values, axis, b, e):
    if b == 0 and e == 0:
        return values
    size = values.shape[axis]
    turned = pltpu.roll(values, (-(WIDTH * b + e)) % size, axis)
    return jnp.where(inside(values.shape, axis, b, e), turned, 0.0)


def fold_shifts(products):
    rows = products.shape[0] // len(SHIFTS)
    total = None
    for number, (b, e) in enumerate(SHIFTS):
        term = shifted(products[number * rows : (number + 1) * rows, :], 1, b, e)
        total = term if total is None else total + term
    return total


def dot(left, right):
    return jnp.dot(left, right, preferred_element_type=jnp.float32)


def assemble_body(count, shares, me_ref, *refs):
    parts, other_refs = refs[:count], refs[count:]
    whole_ref = other_refs[1] if shares else other_refs[0]
    planes, size = parts[0].shape[0], parts[0].shape[1]
    for step in range(count):
        place = pl.ds(pl.multiple_of((me_ref[0] ^ step) * size, size), size)
        whole_ref[:, place, :] = parts[step][...]
    if shares:
        earlier_ref, share_ref = other_refs[0], other_refs[-1]
        rows = share_ref.shape[2]
        for slab in range(shares):
            share_ref[slab, :planes] = earlier_ref[:, slab * rows : (slab + 1) * rows, :]
            share_ref[slab, planes:] = whole_ref[:, slab * rows : (slab + 1) * rows, :]


def assemble(parts, earlier=None):
    planes, size, plane = parts[0].shape
    count = len(parts)
    channels = size * count
    me = lax.axis_index("filt").astype(jnp.int32).reshape(1)
    kind = parts[0].dtype
    outs = [struct((planes, channels, plane), kind)]
    shares = 0
    ins = [me, *parts]
    if earlier is not None:
        shares = lax.axis_size("slab")
        ins.append(earlier)
        outs.append(struct((shares, 2 * planes, channels // shares, plane), kind))
    return call(
        functools.partial(assemble_body, count, shares),
        outs,
        (0, 4 * planes * channels * plane),
        in_specs=[SMEM] + [VMEM] * (len(ins) - 1),
        out_specs=[VMEM] * len(outs),
    )(*ins)


def taps(weight_ref, number):
    block = weight_ref[pl.ds(9 * number, 9)]
    return block.reshape(block.shape[0] * block.shape[1], block.shape[2])


def forward_own_body(planes, core_ref, volume_ref, other_ref, weight_ref, out_ref, acc_ref):
    for a in (0, 1, -1):
        weight = taps(weight_ref, a + 1)
        for j in range(planes):
            if 0 <= j + a < planes:
                product = dot(weight, volume_ref[j + a])
                acc_ref[j] = product if a == 0 else acc_ref[j] + product
    up, last = core_ref[0], planes - 1
    place = (1 - up) * last
    acc_ref[place] = acc_ref[place] + dot(taps(weight_ref, 2 * (1 - up)), other_ref[up * last])
    for j in range(planes):
        out_ref[j] = fold_shifts(acc_ref.at[j])


def forward_own(volume, other, weight):
    planes, channels, plane = volume.shape
    filters = weight.shape[1]
    return call(
        functools.partial(forward_own_body, planes),
        struct((planes, filters, plane), jnp.float32),
        (2 * 9 * filters * channels * plane * (3 * planes - 1), weight.size * 2),
        in_specs=[SMEM] + [VMEM] * 3,
        out_specs=VMEM,
        scratch_shapes=[pltpu.VMEM((planes, 9 * filters, plane), jnp.float32)],
    )(core().reshape(1), volume, other, weight)


def silu_and_slope(values):
    sig = 1.0 / (1.0 + jnp.exp(-values))
    return values * sig, sig * (1.0 + values * (1.0 - sig))


def forward_rest_body(planes, core_ref, beyond_ref, weight_ref, own_ref, *refs):
    head_ref = refs[0] if len(refs) == 4 else None
    slope_ref, made_ref, acc_ref = refs[-3:]
    up = core_ref[0]
    place = up * (planes - 1)
    slope_ref[...] = own_ref[...]
    acc_ref[...] = dot(taps(weight_ref, 2 * up), beyond_ref[0])
    slope_ref[place] = slope_ref[place] + fold_shifts(acc_ref)
    for j in range(planes):
        value, slope = silu_and_slope(slope_ref[j])
        value = value.astype(jnp.bfloat16)
        slope_ref[j] = slope
        made_ref[j] = value if head_ref is None else dot(head_ref[...], value)


def forward_rest(beyond, weight, own, head=None):
    planes, filters, plane = own.shape
    channels = weight.shape[2]
    ins = [core().reshape(1), beyond, weight, own]
    if head is None:
        made = struct(own.shape, jnp.bfloat16)
    else:
        ins.append(head)
        made = struct((planes, head.shape[0], plane), jnp.float32)
    return call(
        functools.partial(forward_rest_body, planes),
        [struct(own.shape, jnp.float32), made],
        (2 * 9 * filters * channels * plane, weight.size * 2 // 3),
        in_specs=[SMEM] + [VMEM] * (len(ins) - 1),
        out_specs=[VMEM] * 2,
        scratch_shapes=[pltpu.VMEM((9 * filters, plane), jnp.float32)],
    )(*ins)


def loss_body(count, labels_ref, head_ref, slope_ref, *refs):
    parts, (grad_ref, copy_ref) = refs[:count], refs[count:]
    for j in range(grad_ref.shape[0]):
        logits = parts[0][j]
        for part in parts[1:]:
            logits = logits + part[j]
        powers = jnp.exp(logits)
        likely = powers / jnp.sum(powers, axis=0, keepdims=True)
        classes = lax.broadcasted_iota(jnp.int32, logits.shape, 0)
        onehot = (labels_ref[j] == classes).astype(jnp.float32)
        logit_grad = (likely - onehot).astype(jnp.bfloat16).astype(jnp.float32)
        back = lax.dot_general(
            head_ref[...].astype(jnp.float32),
            logit_grad,
            (((0,), (0,)), ((), ())),
            preferred_element_type=jnp.float32,
        )
        grad = (back * slope_ref[j]).astype(jnp.bfloat16)
        grad_ref[j] = grad
        copy_ref[j] = grad


def loss_grad(parts, labels, head, slope):
    planes, plane = labels.shape
    return call(
        functools.partial(loss_body, len(parts)),
        [struct(slope.shape, jnp.bfloat16)] * 2,
        (2 * slope.size * head.shape[0], slope.size * 6),
        in_specs=[VMEM] * (3 + len(parts)),
        out_specs=[VMEM] * 2,
    )(labels.reshape(planes, 1, plane), head, slope, *parts)


def spread_back(grad, spread_ref):
    filters = grad.shape[0]
    turned = grad.astype(jnp.float32).T
    for number, (b, e) in enumerate(SHIFTS):
        moved = shifted(turned, 0, -b, -e).astype(jnp.bfloat16)
        spread_ref[:, number * filters : (number + 1) * filters] = moved


def backward_own_body(planes, core_ref, grad_ref, other_ref, weight_ref, out_ref, spread_ref):
    up, last = core_ref[0], planes - 1
    for j in range(planes):
        spread_back(grad_ref[j], spread_ref.at[j])
    spread_back(other_ref[up * last], spread_ref.at[planes])
    for a in (0, 1, -1):
        weight = taps(weight_ref, a + 1)
        for j in range(planes):
            if 0 <= j - a < planes:
                product = dot(spread_ref[j - a], weight)
                out_ref[j] = product if a == 0 else out_ref[j] + product
    place = (1 - up) * last
    out_ref[place] = out_ref[place] + dot(spread_ref[planes], taps(weight_ref, 2 * up))


def backward_own(grad, other, weight):
    planes, filters, plane = grad.shape
    channels = weight.shape[2]
    return call(
        functools.partial(backward_own_body, planes),
        struct((planes, plane, channels), jnp.float32),
        (2 * 9 * filters * channels * plane * (3 * planes - 1), weight.size * 2),
        in_specs=[SMEM] + [VMEM] * 3,
        out_specs=VMEM,
        scratch_shapes=[pltpu.VMEM((planes + 1, plane, 9 * filters), jnp.bfloat16)],
    )(core().reshape(1), grad, other, weight)


def backward_rest_body(planes, count, me_ref, core_ref, beyond_ref, weight_ref, own_ref, *refs):
    kept_ref, sent, (spread_ref, total_ref) = refs[0], refs[1:count], refs[count:]
    size = kept_ref.shape[2]
    up = core_ref[0]
    place = up * (planes - 1)
    spread_back(beyond_ref[0], spread_ref)
    product = dot(spread_ref[...], taps(weight_ref, 2 * (1 - up)))
    for block in range(count):
        columns = slice(block * size, (block + 1) * size)
        for j in range(planes):
            total_ref[block, j] = own_ref[j, :, columns]
        total_ref[block, place] = total_ref[block, place] + product[:, columns]
    kept_ref[...] = total_ref[me_ref[0]]
    for number in range(1, count):
        sent[number - 1][...] = total_ref[me_ref[0] ^ number].astype(jnp.bfloat16)


def backward_rest(beyond, weight, own, count):
    planes, plane, channels = own.shape
    filters = weight.shape[1]
    size = channels // count
    me = lax.axis_index("filt").astype(jnp.int32).reshape(1)
    outs = [struct((planes, plane, size), jnp.float32)]
    outs += [struct((planes, plane, size), jnp.bfloat16)] * (count - 1)
    return call(
        functools.partial(backward_rest_body, planes, count),
        outs,
        (2 * 9 * filters * channels * plane, weight.size * 2 // 3),
        in_specs=[SMEM] * 2 + [VMEM] * 3,
        out_specs=[VMEM] * count,
        scratch_shapes=[
            pltpu.VMEM((plane, 9 * filters), jnp.bfloat16),
            pltpu.VMEM((count, planes, plane, size), jnp.float32),
        ],
    )(me, core().reshape(1), beyond, weight, own)


def first_grad_body(count, slope_ref, *refs):
    parts, out_ref = refs[:count], refs[count]
    for j in range(out_ref.shape[0]):
        total = parts[0][j]
        for part in parts[1:]:
            total = total + part[j].astype(jnp.float32)
        out_ref[j] = (total.T * slope_ref[j]).astype(jnp.bfloat16)


def first_out(parts, slope):
    return call(
        functools.partial(first_grad_body, len(parts)),
        struct(slope.shape, jnp.bfloat16),
        (slope.size * 4, slope.size * 14),
        in_specs=[VMEM] * (1 + len(parts)),
        out_specs=VMEM,
    )(slope, *parts)


def spread_body(offset, volume_ref, spread_ref):
    slabs, both, channels, plane = volume_ref.shape
    planes = both // 2

    def one(d, _):
        values = volume_ref[d // planes, offset + d % planes].astype(jnp.float32)
        place = pl.ds(pl.multiple_of(d * plane, plane), plane)
        for number, (b, e) in enumerate(SHIFTS):
            moved = shifted(values, 1, b, e).astype(jnp.bfloat16)
            spread_ref[number * channels : (number + 1) * channels, place] = moved
        return 0

    lax.fori_loop(0, slabs * planes, one, 0)


def spread(volume, offset):
    slabs, both, channels, plane = volume.shape
    depth = slabs * both // 2
    return call(
        functools.partial(spread_body, offset),
        struct((9 * channels, depth * plane), jnp.bfloat16),
        (9 * channels * depth * plane, 10 * channels * depth * plane),
        in_specs=[VMEM],
        out_specs=VMEM,
    )(volume)


def weight_grad_body(count, owner_ref, spread_ref, *refs):
    parts, (out_ref, grad_ref) = refs[:count], refs[count:]
    filters, plane = parts[0].shape[1:]
    channels = spread_ref.shape[0] // 9
    depth = spread_ref.shape[1] // plane
    planes = sum(part.shape[0] for part in parts) // count
    zero = jnp.zeros((filters, plane), jnp.bfloat16)
    grad_ref[: filters, (depth - 1) * plane :] = zero
    grad_ref[2 * filters :, : plane] = zero
    for number in range(count):
        for j in range(planes):
            d = owner_ref[number] * planes + j
            block = parts[number][j]
            for a in (-1, 0, 1):
                rows = slice((a + 1) * filters, (a + 2) * filters)

                @pl.when((d + a >= 0) & (d + a < depth))
                def _():
                    grad_ref[rows, pl.ds(pl.multiple_of((d + a) * plane, plane), plane)] = block

    product = lax.dot_general(
        spread_ref[...], grad_ref[...], (((1,), (1,)), ((), ())), preferred_element_type=jnp.float32
    )
    for r in range(3):
        for number in range(9):
            out_ref[r * 9 + number] = product[
                number * channels : (number + 1) * channels, r * filters : (r + 1) * filters
            ]


def weight_grad(parts, owners, spreads):
    channels, columns = spreads.shape[0] // 9, spreads.shape[1]
    filters = parts[0].shape[1]
    turned = call(
        functools.partial(weight_grad_body, len(parts)),
        struct((27, channels, filters), jnp.float32),
        (2 * 27 * filters * channels * columns, 27 * channels * filters * 4 + spreads.size * 2),
        in_specs=[SMEM] + [VMEM] * (1 + len(parts)),
        out_specs=VMEM,
        scratch_shapes=[pltpu.VMEM((3 * filters, columns), jnp.bfloat16)],
    )(jnp.stack(owners).astype(jnp.int32), spreads, *parts)
    return jnp.transpose(turned, (0, 2, 1))


def shards(features, first_weight, second_weight, head_weight, labels):
    planes = features.shape[0]
    count = lax.axis_size("filt")
    all_in, = assemble(exchanged(features, "filt"))
    other, beyond = halo(all_in)
    own = forward_own(all_in, other, first_weight)
    slope_first, hidden = forward_rest(beyond, first_weight, own)

    all_hidden, share = assemble(exchanged(hidden, "filt"), all_in)
    other, beyond = halo(all_hidden)
    share = lax.all_to_all(share, "slab", split_axis=0, concat_axis=0, tiled=True)
    own = forward_own(all_hidden, other, second_weight)
    slope_second, logits = forward_rest(beyond, second_weight, own, head_weight)

    second_out, second_copy = loss_grad(exchanged(logits, "filt"), labels, head_weight, slope_second)
    all_second = lax.all_gather(second_copy, "slab", axis=0, tiled=True)
    other, beyond = halo(second_out)
    own = backward_own(second_out, other, second_weight)
    kept, *sent = backward_rest(beyond, second_weight, own, count)
    parts = [kept] + [swap(part, "filt", 1 + number) for number, part in enumerate(sent)]
    first_out_grad = first_out(parts, slope_first)

    blocks, owners = every_plane(first_out_grad)
    second_grad = weight_grad([all_second], [jnp.int32(0)], spread(share, planes))
    first_grad = weight_grad(blocks, owners, spread(share, 0))
    return (first_grad, second_grad)


def solution(mesh):
    placed = (
        P("slab", "filt", None),
        P(None, "filt", None),
        P(None, "filt", None),
        P(None, "filt"),
        P("slab", None),
    )
    return jax.shard_map(
        shards,
        mesh=mesh,
        in_specs=placed,
        out_specs=(P(None, "filt", "slab"), P(None, "filt", "slab")),
        check_vma=False,
    )
```

```python
import functools

import jax
import jax.numpy as jnp
from jax import lax
from jax.experimental import pallas as pl
from jax.experimental.pallas import tpu as pltpu
from jax.sharding import PartitionSpec as P

WIDTH = 8
SHIFTS = [(b, e) for b in (-1, 0, 1) for e in (-1, 0, 1)]
LIMIT = 20 * 1024 * 1024
VMEM = pl.BlockSpec(memory_space=pltpu.VMEM)
SMEM = pl.BlockSpec(memory_space=pltpu.SMEM)
ANY = pl.BlockSpec(memory_space=pl.ANY)


def swap(block, axis, step):
    count = lax.axis_size(axis)
    return lax.ppermute(block, axis, [(i, i ^ step) for i in range(count)])


def exchanged(block, axis):
    return [block] + [swap(block, axis, step) for step in range(1, lax.axis_size(axis))]


def core():
    return lax.axis_index("slab").astype(jnp.int32) % 2


def halo(volume):
    count = lax.axis_size("slab")
    planes = volume.shape[0]
    other = swap(volume, "slab", 1)
    passed = lax.dynamic_slice_in_dim(other, (1 - core()) * (planes - 1), 1, 0)
    pairs = [(i, i + 2) for i in range(0, count - 2, 2)] + [(i, i - 2) for i in range(3, count, 2)]
    return other, lax.ppermute(passed, "slab", pairs)


def chips_apart(blocks):
    return [swap(block, "slab", 2 + 2 * number) for number, block in enumerate(blocks)]


def far_owners(side):
    me = lax.axis_index("slab").astype(jnp.int32)
    return [me ^ (2 * step) ^ side for step in range(lax.axis_size("slab") // 2)]


def call(body, out_shape, cost, *operands, in_specs, scratch_shapes=(), passed=(), after=()):
    flops, moved = cost
    single = not isinstance(out_shape, list)
    outs = [out_shape] if single else out_shape
    first, second = len(operands), len(operands) + len(passed) + len(after)
    third = second + len(outs)

    def inner(*refs):
        body(*refs[:first], *refs[second:third], *refs[third + len(passed) :])

    given = pl.pallas_call(
        inner,
        out_shape=[*outs, *(struct(array.shape, array.dtype) for array in passed)],
        cost_estimate=pl.CostEstimate(flops=flops, bytes_accessed=moved, transcendentals=0),
        compiler_params=pltpu.CompilerParams(vmem_limit_bytes=LIMIT),
        in_specs=[*in_specs] + [ANY] * (len(passed) + len(after)),
        out_specs=[VMEM] * len(outs) + [ANY] * len(passed),
        scratch_shapes=list(scratch_shapes),
        input_output_aliases={first + i: len(outs) + i for i in range(len(passed))},
    )(*operands, *passed, *after)
    if passed:
        return [*given[: len(outs)], list(given[len(outs) :])]
    return given[0] if single else list(given)


def struct(shape, dtype):
    return jax.ShapeDtypeStruct(tuple(shape), dtype)


TOKEN = struct((8, 128), jnp.float32)


def inside(shape, axis, b, e):
    spot = lax.broadcasted_iota(jnp.int32, shape, axis)
    column = spot % WIDTH + e
    moved = spot + WIDTH * b
    return (column >= 0) & (column < WIDTH) & (moved >= 0) & (moved < shape[axis])


def shifted(values, axis, b, e):
    if b == 0 and e == 0:
        return values
    size = values.shape[axis]
    turned = pltpu.roll(values, (-(WIDTH * b + e)) % size, axis)
    return jnp.where(inside(values.shape, axis, b, e), turned, 0.0)


def fold_shifts(products):
    rows = products.shape[0] // len(SHIFTS)
    total = None
    for number, (b, e) in enumerate(SHIFTS):
        term = shifted(products[number * rows : (number + 1) * rows, :], 1, b, e)
        total = term if total is None else total + term
    return total


def dot(left, right):
    return jnp.dot(left, right, preferred_element_type=jnp.float32)


def assemble_body(count, place_ref, *refs):
    parts, whole_ref, shares = refs[:count], refs[count], refs[count + 1 :]
    size = parts[0].shape[1]
    for step in range(count):
        place = pl.ds(pl.multiple_of((place_ref[0] ^ step) * size, size), size)
        whole_ref[:, place, :] = parts[step][...]
    rows = shares[0].shape[2]
    for step, share_ref in enumerate(shares):
        for side in range(2):
            begin = pl.multiple_of(((place_ref[1] ^ step) * 2 + side) * rows, rows)
            share_ref[side] = whole_ref[:, pl.ds(begin, rows), :]


def assemble(parts, after=()):
    planes, size, plane = parts[0].shape
    count, slabs = len(parts), lax.axis_size("slab")
    channels = size * count
    place = jnp.stack([lax.axis_index("filt"), lax.axis_index("slab") // 2]).astype(jnp.int32)
    kind = parts[0].dtype
    outs = [struct((planes, channels, plane), kind)]
    outs += [struct((2, planes, channels // slabs, plane), kind)] * (slabs // 2)
    whole, *shares = call(
        functools.partial(assemble_body, count),
        outs,
        (0, 4 * planes * channels * plane),
        place, *parts,
        in_specs=[SMEM] + [VMEM] * count,
        after=after,
    )
    return whole, shares


def pack_body(sides, count, core_ref, *refs):
    out_ref = refs[-1]
    row = 0
    for number in range(count):
        if number < sides:
            block = refs[number][1 - core_ref[0]]
        else:
            block = refs[number][...]
        rows = block.shape[0] * block.shape[1]
        out_ref[row : row + rows, :] = block.reshape(rows, block.shape[2])
        row += rows


def pack(shares, blocks, after=()):
    plane = blocks[0].shape[-1]
    total = sum(share.size // 2 for share in shares) + sum(block.size for block in blocks)
    count = len(shares) + len(blocks)
    return call(
        functools.partial(pack_body, len(shares), count),
        struct((total // plane, plane), blocks[0].dtype),
        (0, 4 * total),
        core().reshape(1), *shares, *blocks,
        in_specs=[SMEM] + [VMEM] * count,
        after=after,
    )


def taps(weight_ref, number):
    block = weight_ref[pl.ds(9 * number, 9)]
    return block.reshape(block.shape[0] * block.shape[1], block.shape[2])


def forward_own_body(planes, core_ref, volume_ref, other_ref, weight_ref, out_ref, acc_ref):
    for a in (0, 1, -1):
        weight = taps(weight_ref, a + 1)
        for j in range(planes):
            if 0 <= j + a < planes:
                product = dot(weight, volume_ref[j + a])
                acc_ref[j] = product if a == 0 else acc_ref[j] + product
    up, last = core_ref[0], planes - 1
    place = (1 - up) * last
    acc_ref[place] = acc_ref[place] + dot(taps(weight_ref, 2 * (1 - up)), other_ref[up * last])
    for j in range(planes):
        out_ref[j] = fold_shifts(acc_ref.at[j])


def forward_own(volume, other, weight, after=()):
    planes, channels, plane = volume.shape
    filters = weight.shape[1]
    return call(
        functools.partial(forward_own_body, planes),
        struct((planes, filters, plane), jnp.float32),
        (2 * 9 * filters * channels * plane * (3 * planes - 1), weight.size * 2),
        core().reshape(1), volume, other, weight,
        in_specs=[SMEM] + [VMEM] * 3,
        scratch_shapes=[pltpu.VMEM((planes, 9 * filters, plane), jnp.float32)],
        after=after,
    )


def silu_and_slope(values):
    sig = 1.0 / (1.0 + jnp.exp(-values))
    return values * sig, sig * (1.0 + values * (1.0 - sig))


def forward_rest_body(planes, core_ref, beyond_ref, weight_ref, own_ref, *refs):
    head_ref = refs[0] if len(refs) == 4 else None
    slope_ref, made_ref, acc_ref = refs[-3:]
    up = core_ref[0]
    place = up * (planes - 1)
    slope_ref[...] = own_ref[...]
    acc_ref[...] = dot(taps(weight_ref, 2 * up), beyond_ref[0])
    slope_ref[place] = slope_ref[place] + fold_shifts(acc_ref)
    for j in range(planes):
        value, slope = silu_and_slope(slope_ref[j])
        value = value.astype(jnp.bfloat16)
        slope_ref[j] = slope
        made_ref[j] = value if head_ref is None else dot(head_ref[...], value)


def forward_rest(beyond, weight, own, passed, head=None):
    planes, filters, plane = own.shape
    channels = weight.shape[2]
    ins = [core().reshape(1), beyond, weight, own]
    if head is None:
        made = struct(own.shape, jnp.bfloat16)
    else:
        ins.append(head)
        made = struct((planes, head.shape[0], plane), jnp.float32)
    return call(
        functools.partial(forward_rest_body, planes),
        [struct(own.shape, jnp.float32), made],
        (2 * 9 * filters * channels * plane, weight.size * 2 // 3),
        *ins,
        in_specs=[SMEM] + [VMEM] * (len(ins) - 1),
        scratch_shapes=[pltpu.VMEM((9 * filters, plane), jnp.float32)],
        passed=passed,
    )


def loss_body(count, labels_ref, head_ref, slope_ref, *refs):
    parts, grad_ref = refs[:count], refs[count]
    for j in range(grad_ref.shape[0]):
        logits = parts[0][j]
        for part in parts[1:]:
            logits = logits + part[j]
        powers = jnp.exp(logits)
        likely = powers / jnp.sum(powers, axis=0, keepdims=True)
        classes = lax.broadcasted_iota(jnp.int32, logits.shape, 0)
        onehot = (labels_ref[j] == classes).astype(jnp.float32)
        logit_grad = (likely - onehot).astype(jnp.bfloat16).astype(jnp.float32)
        back = lax.dot_general(
            head_ref[...].astype(jnp.float32),
            logit_grad,
            (((0,), (0,)), ((), ())),
            preferred_element_type=jnp.float32,
        )
        grad_ref[j] = (back * slope_ref[j]).astype(jnp.bfloat16)


def loss_grad(parts, labels, head, slope):
    planes, plane = labels.shape
    return call(
        functools.partial(loss_body, len(parts)),
        struct(slope.shape, jnp.bfloat16),
        (2 * slope.size * head.shape[0], slope.size * 6),
        labels.reshape(planes, 1, plane), head, slope, *parts,
        in_specs=[VMEM] * (3 + len(parts)),
    )


def spread_back(grad, spread_ref):
    filters = grad.shape[0]
    turned = grad.astype(jnp.float32).T
    for number, (b, e) in enumerate(SHIFTS):
        moved = shifted(turned, 0, -b, -e).astype(jnp.bfloat16)
        spread_ref[:, number * filters : (number + 1) * filters] = moved


def backward_own_body(planes, core_ref, grad_ref, other_ref, weight_ref, out_ref, spread_ref):
    up, last = core_ref[0], planes - 1
    for j in range(planes):
        spread_back(grad_ref[j], spread_ref.at[j])
    spread_back(other_ref[up * last], spread_ref.at[planes])
    for a in (0, 1, -1):
        weight = taps(weight_ref, a + 1)
        for j in range(planes):
            if 0 <= j - a < planes:
                product = dot(spread_ref[j - a], weight)
                out_ref[j] = product if a == 0 else out_ref[j] + product
    place = (1 - up) * last
    out_ref[place] = out_ref[place] + dot(spread_ref[planes], taps(weight_ref, 2 * up))


def backward_own(grad, other, weight, after=()):
    planes, filters, plane = grad.shape
    channels = weight.shape[2]
    return call(
        functools.partial(backward_own_body, planes),
        struct((planes, plane, channels), jnp.float32),
        (2 * 9 * filters * channels * plane * (3 * planes - 1), weight.size * 2),
        core().reshape(1), grad, other, weight,
        in_specs=[SMEM] + [VMEM] * 3,
        scratch_shapes=[pltpu.VMEM((planes + 1, plane, 9 * filters), jnp.bfloat16)],
        after=after,
    )


def backward_rest_body(planes, count, me_ref, core_ref, grad_ref, beyond_ref, weight_ref, own_ref, *refs):
    copy_ref, kept_ref, sent, (spread_ref, total_ref) = refs[0], refs[1], refs[2 : 1 + count], refs[1 + count :]
    copy_ref[...] = grad_ref[...]
    size = kept_ref.shape[2]
    up = core_ref[0]
    place = up * (planes - 1)
    spread_back(beyond_ref[0], spread_ref)
    product = dot(spread_ref[...], taps(weight_ref, 2 * (1 - up)))
    for block in range(count):
        columns = slice(block * size, (block + 1) * size)
        for j in range(planes):
            total_ref[block, j] = own_ref[j, :, columns]
        total_ref[block, place] = total_ref[block, place] + product[:, columns]
    kept_ref[...] = total_ref[me_ref[0]]
    for number in range(1, count):
        sent[number - 1][...] = total_ref[me_ref[0] ^ number].astype(jnp.bfloat16)


def backward_rest(grad, beyond, weight, own, count, after=()):
    planes, plane, channels = own.shape
    filters = weight.shape[1]
    size = channels // count
    me = lax.axis_index("filt").astype(jnp.int32).reshape(1)
    outs = [struct(grad.shape, grad.dtype), struct((planes, plane, size), jnp.float32)]
    outs += [struct((planes, plane, size), jnp.bfloat16)] * (count - 1)
    return call(
        functools.partial(backward_rest_body, planes, count),
        outs,
        (2 * 9 * filters * channels * plane, weight.size * 2 // 3),
        me, core().reshape(1), grad, beyond, weight, own,
        in_specs=[SMEM] * 2 + [VMEM] * 4,
        scratch_shapes=[
            pltpu.VMEM((plane, 9 * filters), jnp.bfloat16),
            pltpu.VMEM((count, planes, plane, size), jnp.float32),
        ],
        after=after,
    )


def first_grad_body(count, slope_ref, *refs):
    parts, out_ref = refs[:count], refs[count]
    for j in range(out_ref.shape[0]):
        total = parts[0][j]
        for part in parts[1:]:
            total = total + part[j].astype(jnp.float32)
        out_ref[j] = (total.T * slope_ref[j]).astype(jnp.bfloat16)


def first_out(parts, slope):
    return call(
        functools.partial(first_grad_body, len(parts)),
        struct(slope.shape, jnp.bfloat16),
        (slope.size * 4, slope.size * 14),
        slope, *parts,
        in_specs=[VMEM] * (1 + len(parts)),
    )


def spread_body(count, row, owner_ref, crossed_ref, *refs):
    shares, (spread_ref, token_ref) = refs[:count], refs[count:]
    _, planes, channels, plane = shares[0].shape
    token_ref[...] = jnp.zeros_like(token_ref)

    def one(values, d):
        values = values.astype(jnp.float32)
        place = pl.ds(pl.multiple_of(d * plane, plane), plane)
        for number, (b, e) in enumerate(SHIFTS):
            moved = shifted(values, 1, b, e).astype(jnp.bfloat16)
            spread_ref[number * channels : (number + 1) * channels, place] = moved

    for step in range(count):
        for j in range(planes):
            one(shares[step][owner_ref[0] % 2, j], owner_ref[step] * planes + j)
            begin = row + (step * planes + j) * channels
            one(crossed_ref[begin : begin + channels, :], (owner_ref[step] ^ 1) * planes + j)


def spread(shares, crossed, row):
    _, planes, channels, plane = shares[0].shape
    count = len(shares)
    depth = 2 * count * planes
    return call(
        functools.partial(spread_body, count, row),
        [struct((9 * channels, depth * plane), jnp.bfloat16), TOKEN],
        (9 * channels * depth * plane, 10 * channels * depth * plane),
        jnp.stack(far_owners(0)), crossed, *shares,
        in_specs=[SMEM] + [VMEM] * (1 + count),
    )


def weight_grad_body(count, row, has_other, owner_ref, spread_ref, crossed_ref, *refs):
    other_ref = refs[0] if has_other else None
    parts, (out_ref, token_ref, grad_ref) = refs[-3 - count : -3], refs[-3:]
    token_ref[...] = jnp.zeros_like(token_ref)
    planes, filters, plane = parts[0].shape
    channels = spread_ref.shape[0] // 9
    depth = spread_ref.shape[1] // plane
    zero = jnp.zeros((filters, plane), jnp.bfloat16)
    grad_ref[: filters, (depth - 1) * plane :] = zero
    grad_ref[2 * filters :, : plane] = zero

    def one(block, d):
        for a in (-1, 0, 1):

            @pl.when((d + a >= 0) & (d + a < depth))
            def _():
                place = pl.ds(pl.multiple_of((d + a) * plane, plane), plane)
                grad_ref[(a + 1) * filters : (a + 2) * filters, place] = block

    begin = row
    for step in range(count):
        for j in range(planes):
            one(parts[step][j], owner_ref[step] * planes + j)
            if has_other and step == 0:
                block = other_ref[j]
            else:
                block = crossed_ref[begin : begin + filters, :]
                begin += filters
            one(block, (owner_ref[step] ^ 1) * planes + j)

    product = lax.dot_general(
        spread_ref[...], grad_ref[...], (((1,), (1,)), ((), ())), preferred_element_type=jnp.float32
    )
    for r in range(3):
        for number in range(9):
            out_ref[r * 9 + number] = product[
                number * channels : (number + 1) * channels, r * filters : (r + 1) * filters
            ]


def weight_grad(spreads, blocks, crossed, row, other=None):
    channels, columns = spreads.shape[0] // 9, spreads.shape[1]
    filters = blocks[0].shape[1]
    count = len(blocks)
    blocks = ([] if other is None else [other]) + blocks
    return call(
        functools.partial(weight_grad_body, count, row, other is not None),
        [struct((27, channels, filters), jnp.float32), TOKEN],
        (2 * 27 * filters * channels * columns, 27 * channels * filters * 4 + spreads.size * 2),
        jnp.stack(far_owners(0)), spreads, crossed, *blocks,
        in_specs=[SMEM] + [VMEM] * (2 + len(blocks)),
        scratch_shapes=[pltpu.VMEM((3 * filters, columns), jnp.bfloat16)],
    )


def shards(features, first_weight, second_weight, head_weight, labels):
    count = lax.axis_size("filt")
    all_in, share_in = assemble(exchanged(features, "filt"))
    other, beyond = halo(all_in)
    own = forward_own(all_in, other, first_weight)
    slope_first, hidden, sent = forward_rest(beyond, first_weight, own, share_in[1:])

    hidden_parts = exchanged(hidden, "filt")
    share_in = [share_in[0]] + chips_apart(sent)
    all_hidden, share_hidden = assemble(hidden_parts, share_in[1:])
    other, beyond = halo(all_hidden)
    own = forward_own(all_hidden, other, second_weight)
    slope_second, logits, sent = forward_rest(beyond, second_weight, own, share_hidden[1:], head_weight)

    logits = exchanged(logits, "filt")
    share_hidden = [share_hidden[0]] + chips_apart(sent)
    second_out = loss_grad(logits, labels, head_weight, slope_second)
    second_other, beyond = halo(second_out)
    own = backward_own(second_out, second_other, second_weight)
    second_copy, kept, *sent = backward_rest(second_out, beyond, second_weight, own, count, share_hidden[1:])
    parts = [kept] + [swap(part, "filt", 1 + number) for number, part in enumerate(sent)]
    second_far = chips_apart([second_copy] * (lax.axis_size("slab") // 2 - 1))
    first_out_grad = first_out(parts, slope_first)

    first_blocks = [first_out_grad] + chips_apart([first_out_grad] * len(second_far))
    crossed = swap(pack(share_in + share_hidden, second_far, first_blocks[1:2]), "slab", 1)
    rows = sum(share.size // 2 for share in share_in) // features.shape[2]
    spread_hidden, _ = spread(share_hidden, crossed, rows)
    second_grad, second_token = weight_grad(spread_hidden, [second_out] + second_far, crossed, 2 * rows, second_other)
    spread_in, token = spread(share_in, crossed, 0)
    crossed = swap(pack([], first_blocks, [token, second_token]), "slab", 1)
    first_grad, _ = weight_grad(spread_in, first_blocks, crossed, 0)
    return jnp.transpose(first_grad, (0, 2, 1)), jnp.transpose(second_grad, (0, 2, 1))


def solution(mesh):
    placed = (
        P("slab", "filt", None),
        P(None, "filt", None),
        P(None, "filt", None),
        P(None, "filt"),
        P("slab", None),
    )
    return jax.shard_map(
        shards,
        mesh=mesh,
        in_specs=placed,
        out_specs=(P(None, "filt", "slab"), P(None, "filt", "slab")),
        check_vma=False,
    )
```

```python
import functools

import jax
import jax.numpy as jnp
from jax import lax
from jax.experimental import pallas as pl
from jax.experimental.pallas import tpu as pltpu
from jax.sharding import PartitionSpec as P

WIDTH = 8
SHIFTS = [(b, e) for b in (-1, 0, 1) for e in (-1, 0, 1)]
LIMIT = 20 * 1024 * 1024
VMEM = pl.BlockSpec(memory_space=pltpu.VMEM)
SMEM = pl.BlockSpec(memory_space=pltpu.SMEM)
ANY = pl.BlockSpec(memory_space=pl.ANY)


def swap(block, axis, step):
    count = lax.axis_size(axis)
    return lax.ppermute(block, axis, [(i, i ^ step) for i in range(count)])


def exchanged(block, axis):
    return [block] + [swap(block, axis, step) for step in range(1, lax.axis_size(axis))]


def core():
    return lax.axis_index("slab").astype(jnp.int32) % 2


def halo(volume):
    count = lax.axis_size("slab")
    planes = volume.shape[0]
    other = swap(volume, "slab", 1)
    passed = lax.dynamic_slice_in_dim(other, (1 - core()) * (planes - 1), 1, 0)
    pairs = [(i, i + 2) for i in range(0, count - 2, 2)] + [(i, i - 2) for i in range(3, count, 2)]
    return other, lax.ppermute(passed, "slab", pairs)


def chips_apart(blocks):
    return [swap(block, "slab", 2 + 2 * number) for number, block in enumerate(blocks)]


def far_owners(side):
    me = lax.axis_index("slab").astype(jnp.int32)
    return [me ^ (2 * step) ^ side for step in range(lax.axis_size("slab") // 2)]


def call(body, out_shape, cost, *operands, in_specs, scratch_shapes=(), passed=(), after=()):
    flops, moved = cost
    single = not isinstance(out_shape, list)
    outs = [out_shape] if single else out_shape
    first, second = len(operands), len(operands) + len(passed) + len(after)
    third = second + len(outs)

    def inner(*refs):
        body(*refs[:first], *refs[second:third], *refs[third + len(passed) :])

    given = pl.pallas_call(
        inner,
        out_shape=[*outs, *(struct(array.shape, array.dtype) for array in passed)],
        cost_estimate=pl.CostEstimate(flops=flops, bytes_accessed=moved, transcendentals=0),
        compiler_params=pltpu.CompilerParams(vmem_limit_bytes=LIMIT),
        in_specs=[*in_specs] + [ANY] * (len(passed) + len(after)),
        out_specs=[VMEM] * len(outs) + [ANY] * len(passed),
        scratch_shapes=list(scratch_shapes),
        input_output_aliases={first + i: len(outs) + i for i in range(len(passed))},
    )(*operands, *passed, *after)
    if passed:
        return [*given[: len(outs)], list(given[len(outs) :])]
    return given[0] if single else list(given)


def struct(shape, dtype):
    return jax.ShapeDtypeStruct(tuple(shape), dtype)


TOKEN = struct((8, 128), jnp.float32)


def stage_body(count, *refs):
    sources, targets, sems = refs[:count], refs[count : 2 * count], refs[2 * count]
    copies = [pltpu.make_async_copy(sources[i], targets[i], sems.at[i]) for i in range(count)]
    for copy in copies:
        copy.start()
    for copy in copies:
        copy.wait()


def stage(*arrays):
    count = len(arrays)
    return call(
        functools.partial(stage_body, count),
        [struct(array.shape, array.dtype) for array in arrays],
        (0, sum(4 * array.size for array in arrays)),
        *arrays,
        in_specs=[pl.BlockSpec(memory_space=pltpu.HBM)] * count,
        scratch_shapes=[pltpu.SemaphoreType.DMA((count,))],
    )


def inside(shape, axis, b, e):
    spot = lax.broadcasted_iota(jnp.int32, shape, axis)
    column = spot % WIDTH + e
    moved = spot + WIDTH * b
    return (column >= 0) & (column < WIDTH) & (moved >= 0) & (moved < shape[axis])


def shifted(values, axis, b, e):
    if b == 0 and e == 0:
        return values
    size = values.shape[axis]
    turned = pltpu.roll(values, (-(WIDTH * b + e)) % size, axis)
    return jnp.where(inside(values.shape, axis, b, e), turned, 0.0)


def fold_shifts(products):
    rows = products.shape[0] // len(SHIFTS)
    total = None
    for number, (b, e) in enumerate(SHIFTS):
        term = shifted(products[number * rows : (number + 1) * rows, :], 1, b, e)
        total = term if total is None else total + term
    return total


def dot(left, right):
    return jnp.dot(left, right, preferred_element_type=jnp.float32)


def assemble_body(count, place_ref, *refs):
    parts, whole_ref, shares = refs[:count], refs[count], refs[count + 1 :]
    size = parts[0].shape[1]
    for step in range(count):
        place = pl.ds(pl.multiple_of((place_ref[0] ^ step) * size, size), size)
        whole_ref[:, place, :] = parts[step][...]
    rows = shares[0].shape[2]
    for step, share_ref in enumerate(shares):
        for side in range(2):
            begin = pl.multiple_of(((place_ref[1] ^ step) * 2 + side) * rows, rows)
            share_ref[side] = whole_ref[:, pl.ds(begin, rows), :]


def assemble(parts, after=()):
    planes, size, plane = parts[0].shape
    count, slabs = len(parts), lax.axis_size("slab")
    channels = size * count
    place = jnp.stack([lax.axis_index("filt"), lax.axis_index("slab") // 2]).astype(jnp.int32)
    kind = parts[0].dtype
    outs = [struct((planes, channels, plane), kind)]
    outs += [struct((2, planes, channels // slabs, plane), kind)] * (slabs // 2)
    whole, *shares = call(
        functools.partial(assemble_body, count),
        outs,
        (0, 4 * planes * channels * plane),
        place, *parts,
        in_specs=[SMEM] + [VMEM] * count,
        after=after,
    )
    return whole, shares


def pack_body(sides, count, core_ref, *refs):
    out_ref = refs[-1]
    lanes = out_ref.shape[1]
    row = 0
    for number in range(sides):
        block = refs[number][1 - core_ref[0]]
        rows = block.shape[0] * block.shape[1]
        out_ref[row : row + rows, :] = block.reshape(rows, lanes)
        row += rows
    for number in range(sides, count):
        planes, plane, filters = refs[number].shape
        for j in range(planes):
            for begin in range(0, plane, filters):
                out_ref[row : row + filters, begin : begin + filters] = refs[number][j, begin : begin + filters, :]
            row += filters


def pack(shares, blocks, after=()):
    plane = blocks[0].shape[1]
    total = sum(share.size // 2 for share in shares) + sum(block.size for block in blocks)
    count = len(shares) + len(blocks)
    return call(
        functools.partial(pack_body, len(shares), count),
        struct((total // plane, plane), blocks[0].dtype),
        (0, 4 * total),
        core().reshape(1), *shares, *blocks,
        in_specs=[SMEM] + [VMEM] * count,
        after=after,
    )


def taps(weight_ref, number):
    block = weight_ref[pl.ds(9 * number, 9)]
    return block.reshape(block.shape[0] * block.shape[1], block.shape[2])


def forward_own_body(planes, core_ref, volume_ref, other_ref, weight_ref, out_ref, acc_ref):
    for a in (0, 1, -1):
        weight = taps(weight_ref, a + 1)
        for j in range(planes):
            if 0 <= j + a < planes:
                product = dot(weight, volume_ref[j + a])
                acc_ref[j] = product if a == 0 else acc_ref[j] + product
    up, last = core_ref[0], planes - 1
    place = (1 - up) * last
    acc_ref[place] = acc_ref[place] + dot(taps(weight_ref, 2 * (1 - up)), other_ref[up * last])
    for j in range(planes):
        out_ref[j] = fold_shifts(acc_ref.at[j])


def forward_own(volume, other, weight, after=()):
    planes, channels, plane = volume.shape
    filters = weight.shape[1]
    return call(
        functools.partial(forward_own_body, planes),
        struct((planes, filters, plane), jnp.float32),
        (2 * 9 * filters * channels * plane * (3 * planes - 1), weight.size * 2),
        core().reshape(1), volume, other, weight,
        in_specs=[SMEM] + [VMEM] * 3,
        scratch_shapes=[pltpu.VMEM((planes, 9 * filters, plane), jnp.float32)],
        after=after,
    )


def silu_and_slope(values):
    sig = 1.0 / (1.0 + jnp.exp(-values))
    return values * sig, sig * (1.0 + values * (1.0 - sig))


def forward_rest_body(planes, core_ref, beyond_ref, weight_ref, own_ref, *refs):
    head_ref = refs[0] if len(refs) == 5 else None
    slope_ref, made_ref, acc_ref, total_ref = refs[-4:]
    up = core_ref[0]
    place = up * (planes - 1)
    total_ref[...] = own_ref[...]
    acc_ref[...] = dot(taps(weight_ref, 2 * up), beyond_ref[0])
    total_ref[place] = total_ref[place] + fold_shifts(acc_ref)
    for j in range(planes):
        value, slope = silu_and_slope(total_ref[j])
        value = value.astype(jnp.bfloat16)
        slope_ref[j] = slope.T if head_ref is None else slope
        made_ref[j] = value if head_ref is None else dot(head_ref[...], value)


def forward_rest(beyond, weight, own, after, head=None):
    planes, filters, plane = own.shape
    channels = weight.shape[2]
    ins = [core().reshape(1), beyond, weight, own]
    slope = own.shape
    if head is None:
        slope = (planes, plane, filters)
        made = struct(own.shape, jnp.bfloat16)
    else:
        ins.append(head)
        made = struct((planes, head.shape[0], plane), jnp.float32)
    return call(
        functools.partial(forward_rest_body, planes),
        [struct(slope, jnp.float32), made],
        (2 * 9 * filters * channels * plane, weight.size * 2 // 3),
        *ins,
        in_specs=[SMEM] + [VMEM] * (len(ins) - 1),
        scratch_shapes=[
            pltpu.VMEM((9 * filters, plane), jnp.float32),
            pltpu.VMEM(own.shape, jnp.float32),
        ],
        after=after,
    )


def loss_body(count, labels_ref, head_ref, slope_ref, *refs):
    parts, grad_ref = refs[:count], refs[count]
    for j in range(grad_ref.shape[0]):
        logits = parts[0][j]
        for part in parts[1:]:
            logits = logits + part[j]
        powers = jnp.exp(logits)
        likely = powers / jnp.sum(powers, axis=0, keepdims=True)
        classes = lax.broadcasted_iota(jnp.int32, logits.shape, 0)
        onehot = (labels_ref[j] == classes).astype(jnp.float32)
        logit_grad = (likely - onehot).astype(jnp.bfloat16).astype(jnp.float32)
        back = lax.dot_general(
            head_ref[...].astype(jnp.float32),
            logit_grad,
            (((0,), (0,)), ((), ())),
            preferred_element_type=jnp.float32,
        )
        grad_ref[j] = (back * slope_ref[j]).T.astype(jnp.bfloat16)


def loss_grad(parts, labels, head, slope):
    planes, plane = labels.shape
    return call(
        functools.partial(loss_body, len(parts)),
        struct((planes, plane, slope.shape[1]), jnp.bfloat16),
        (2 * slope.size * head.shape[0], slope.size * 6),
        labels.reshape(planes, 1, plane), head, slope, *parts,
        in_specs=[VMEM] * (3 + len(parts)),
    )


def spread_back(grad, spread_ref):
    filters = grad.shape[1]
    turned = grad.astype(jnp.float32)
    for number, (b, e) in enumerate(SHIFTS):
        moved = shifted(turned, 0, -b, -e).astype(jnp.bfloat16)
        spread_ref[:, number * filters : (number + 1) * filters] = moved


def backward_own_body(planes, core_ref, grad_ref, other_ref, weight_ref, out_ref, spread_ref):
    up, last = core_ref[0], planes - 1
    for j in range(planes):
        spread_back(grad_ref[j], spread_ref.at[j])
    spread_back(other_ref[up * last], spread_ref.at[planes])
    for a in (0, 1, -1):
        weight = taps(weight_ref, a + 1)
        for j in range(planes):
            if 0 <= j - a < planes:
                product = dot(spread_ref[j - a], weight)
                out_ref[j] = product if a == 0 else out_ref[j] + product
    place = (1 - up) * last
    out_ref[place] = out_ref[place] + dot(spread_ref[planes], taps(weight_ref, 2 * up))


def backward_own(grad, other, weight, after=()):
    planes, plane, filters = grad.shape
    channels = weight.shape[2]
    return call(
        functools.partial(backward_own_body, planes),
        struct((planes, plane, channels), jnp.float32),
        (2 * 9 * filters * channels * plane * (3 * planes - 1), weight.size * 2),
        core().reshape(1), grad, other, weight,
        in_specs=[SMEM] + [VMEM] * 3,
        scratch_shapes=[pltpu.VMEM((planes + 1, plane, 9 * filters), jnp.bfloat16)],
        after=after,
    )


def backward_rest_body(planes, count, steps, me_ref, chip_ref, core_ref, weight_ref, own_ref, *refs):
    near, refs = refs[: len(steps)], refs[len(steps) :]
    kept_ref, sent, (edge_ref, spread_ref, total_ref) = refs[0], refs[1:count], refs[count:]
    size = kept_ref.shape[2]
    up = core_ref[0]
    place = up * (planes - 1)
    edge_ref[...] = jnp.zeros_like(edge_ref)
    for number, step in enumerate(steps):

        @pl.when(chip_ref[0] == step)
        def _():
            edge_ref[...] = near[number][(1 - up) * (planes - 1)]

    spread_back(edge_ref[...], spread_ref)
    product = dot(spread_ref[...], taps(weight_ref, 2 * (1 - up)))
    for block in range(count):
        columns = slice(block * size, (block + 1) * size)
        for j in range(planes):
            total_ref[block, j] = own_ref[j, :, columns]
        total_ref[block, place] = total_ref[block, place] + product[:, columns]
    kept_ref[...] = total_ref[me_ref[0]]
    for number in range(1, count):
        sent[number - 1][...] = total_ref[me_ref[0] ^ number].astype(jnp.bfloat16)


def backward_rest(far, weight, own, count):
    planes, plane, channels = own.shape
    filters = weight.shape[1]
    size = channels // count
    me = lax.axis_index("filt").astype(jnp.int32)
    chips = len(far) + 1
    chip = lax.axis_index("slab").astype(jnp.int32) // 2
    other = chip + 2 * core() - 1
    step = jnp.where((other >= 0) & (other < chips), chip ^ other, 0)
    steps = [1 << bits for bits in range(1, chips.bit_length())]
    steps = [step - 1 for step in steps if step <= chips]
    outs = [struct((planes, plane, size), jnp.float32)]
    outs += [struct((planes, plane, size), jnp.bfloat16)] * (count - 1)
    return call(
        functools.partial(backward_rest_body, planes, count, steps),
        outs,
        (2 * 9 * filters * channels * plane, weight.size * 2 // 3),
        me.reshape(1), step.reshape(1), core().reshape(1), weight, own, *[far[step - 1] for step in steps],
        in_specs=[SMEM] * 3 + [VMEM] * (2 + len(steps)),
        scratch_shapes=[
            pltpu.VMEM((plane, filters), jnp.bfloat16),
            pltpu.VMEM((plane, 9 * filters), jnp.bfloat16),
            pltpu.VMEM((count, planes, plane, size), jnp.float32),
        ],
    )


def first_grad_body(count, slope_ref, *refs):
    parts, out_ref = refs[:count], refs[count]
    for j in range(out_ref.shape[0]):
        total = parts[0][j]
        for part in parts[1:]:
            total = total + part[j].astype(jnp.float32)
        out_ref[j] = (total * slope_ref[j]).astype(jnp.bfloat16)


def first_out(parts, slope):
    return call(
        functools.partial(first_grad_body, len(parts)),
        struct(slope.shape, jnp.bfloat16),
        (slope.size * 4, slope.size * 14),
        slope, *parts,
        in_specs=[VMEM] * (1 + len(parts)),
    )


def spread_body(count, row, owner_ref, crossed_ref, *refs):
    shares, (spread_ref, token_ref) = refs[:count], refs[count:]
    _, planes, channels, plane = shares[0].shape
    token_ref[...] = jnp.zeros_like(token_ref)

    def one(values, d):
        values = values.astype(jnp.float32)
        place = pl.ds(pl.multiple_of(d * plane, plane), plane)
        for number, (b, e) in enumerate(SHIFTS):
            moved = shifted(values, 1, b, e).astype(jnp.bfloat16)
            spread_ref[number * channels : (number + 1) * channels, place] = moved

    for step in range(count):
        for j in range(planes):
            one(shares[step][owner_ref[0] % 2, j], owner_ref[step] * planes + j)
            begin = row + (step * planes + j) * channels
            one(crossed_ref[begin : begin + channels, :], (owner_ref[step] ^ 1) * planes + j)


def spread(shares, crossed, row):
    _, planes, channels, plane = shares[0].shape
    count = len(shares)
    depth = 2 * count * planes
    return call(
        functools.partial(spread_body, count, row),
        [struct((9 * channels, depth * plane), jnp.bfloat16), TOKEN],
        (9 * channels * depth * plane, 10 * channels * depth * plane),
        jnp.stack(far_owners(0)), crossed, *shares,
        in_specs=[SMEM] + [VMEM] * (1 + count),
    )


def weight_grad_body(count, row, owner_ref, spread_ref, crossed_ref, *refs):
    parts, (out_ref, token_ref, grad_ref) = refs[:count], refs[count:]
    token_ref[...] = jnp.zeros_like(token_ref)
    planes, plane, filters = parts[0].shape
    channels = spread_ref.shape[0] // 9
    depth = spread_ref.shape[1] // plane
    zero = jnp.zeros((plane, filters), jnp.bfloat16)
    grad_ref[depth * plane : (depth + 1) * plane, : filters] = zero
    grad_ref[plane : 2 * plane, 2 * filters :] = zero

    def one(block, d, begin):
        rows = block.shape[0]
        for a in (-1, 0, 1):
            place = pl.ds(pl.multiple_of((d + a + 1) * plane + begin, rows), rows)
            grad_ref[place, (a + 1) * filters : (a + 2) * filters] = block

    for number in range(count):
        for j in range(planes):
            one(parts[number][j], owner_ref[number] * planes + j, 0)
    for number in range(count, owner_ref.shape[0]):
        for j in range(planes):
            for begin in range(0, plane, filters):
                block = crossed_ref[row : row + filters, begin : begin + filters]
                one(block, owner_ref[number] * planes + j, begin)
            row += filters

    product = dot(spread_ref[...], grad_ref[plane : (depth + 1) * plane, :])
    for r in range(3):
        for number in range(9):
            out_ref[r * 9 + number] = product[
                number * channels : (number + 1) * channels, r * filters : (r + 1) * filters
            ]


def weight_grad(spreads, blocks, owners, crossed, row):
    channels, columns = spreads.shape[0] // 9, spreads.shape[1]
    _, plane, filters = blocks[0].shape
    return call(
        functools.partial(weight_grad_body, len(blocks), row),
        [struct((27, channels, filters), jnp.float32), TOKEN],
        (2 * 27 * filters * channels * columns, 27 * channels * filters * 4 + spreads.size * 2),
        jnp.stack(owners), spreads, crossed, *blocks,
        in_specs=[SMEM] + [VMEM] * (2 + len(blocks)),
        scratch_shapes=[pltpu.VMEM((columns + 2 * plane, 3 * filters), jnp.bfloat16)],
    )


def shards(features, first_weight, second_weight, head_weight, labels):
    count = lax.axis_size("filt")
    chips = lax.axis_size("slab") // 2
    near, first_weight, head_weight = stage(features, first_weight, head_weight)
    all_in, share_in = assemble([near] + exchanged(features, "filt")[1:])
    other, beyond = halo(all_in)
    share_in = [share_in[0]] + chips_apart(share_in[1:])
    own = forward_own(all_in, other, first_weight)
    slope_first, hidden = forward_rest(beyond, first_weight, own, share_in[1:])

    all_hidden, share_hidden = assemble(exchanged(hidden, "filt"))
    other, beyond = halo(all_hidden)
    share_hidden = [share_hidden[0]] + chips_apart(share_hidden[1:])
    own = forward_own(all_hidden, other, second_weight)
    slope_second, logits = forward_rest(beyond, second_weight, own, share_hidden[1:], head_weight)

    second_out = loss_grad(exchanged(logits, "filt"), labels, head_weight, slope_second)
    second_other = swap(second_out, "slab", 1)
    second_far = chips_apart([second_other] * (chips - 1))
    own = backward_own(second_out, second_other, second_weight)
    kept, *sent = backward_rest(second_far, second_weight, own, count)
    parts = [kept] + [swap(part, "filt", 1 + number) for number, part in enumerate(sent)]
    first_out_grad = first_out(parts, slope_first)

    here, there = far_owners(0), far_owners(1)
    first_blocks = [first_out_grad] + chips_apart([first_out_grad] * (chips - 1))
    crossed = swap(pack(share_in + share_hidden, second_far, parts[1:2]), "slab", 1)
    rows = sum(share.size // 2 for share in share_in) // features.shape[2]
    spread_hidden, _ = spread(share_hidden, crossed, rows)
    second_grad, second_token = weight_grad(
        spread_hidden,
        [second_out, second_other] + second_far,
        [here[0], there[0]] + there[1:] + here[1:],
        crossed,
        2 * rows,
    )
    spread_in, token = spread(share_in, crossed, 0)
    crossed = swap(pack([], first_blocks, [token, second_token]), "slab", 1)
    first_grad, _ = weight_grad(spread_in, first_blocks, here + there, crossed, 0)
    return jnp.transpose(first_grad, (0, 2, 1)), jnp.transpose(second_grad, (0, 2, 1))


def solution(mesh):
    placed = (
        P("slab", "filt", None),
        P(None, "filt", None),
        P(None, "filt", None),
        P(None, "filt"),
        P("slab", None),
    )
    return jax.shard_map(
        shards,
        mesh=mesh,
        in_specs=placed,
        out_specs=(P(None, "filt", "slab"), P(None, "filt", "slab")),
        check_vma=False,
    )
```

```python
import functools

import jax
import jax.numpy as jnp
from jax import lax
from jax.experimental import pallas as pl
from jax.experimental.pallas import tpu as pltpu
from jax.sharding import PartitionSpec as P

WIDTH = 8
SHIFTS = [(b, e) for b in (-1, 0, 1) for e in (-1, 0, 1)]
LIMIT = 20 * 1024 * 1024
VMEM = pl.BlockSpec(memory_space=pltpu.VMEM)
ANY = pl.BlockSpec(memory_space=pl.ANY)


def swap(block, axis, step):
    count = lax.axis_size(axis)
    return lax.ppermute(block, axis, [(i, i ^ step) for i in range(count)])


def exchanged(block, axis):
    return [block] + [swap(block, axis, step) for step in range(1, lax.axis_size(axis))]


def halo(volume):
    count = lax.axis_size("slab")
    other = swap(volume, "slab", 1)
    passed = edge(other)
    pairs = [(i, i + 2) for i in range(0, count - 2, 2)] + [(i, i - 2) for i in range(3, count, 2)]
    return other, lax.ppermute(passed, "slab", pairs)


def chips_apart(blocks):
    return [swap(block, "slab", 2 + 2 * number) for number, block in enumerate(blocks)]


def call(body, out_shape, cost, *operands, in_specs, scratch_shapes=(), passed=(), after=()):
    flops, moved = cost
    single = not isinstance(out_shape, list)
    outs = [out_shape] if single else out_shape
    first, second = len(operands), len(operands) + len(passed) + len(after)
    third = second + len(outs)

    def inner(*refs):
        body(*refs[:first], *refs[second:third], *refs[third + len(passed) :])

    given = pl.pallas_call(
        inner,
        out_shape=[*outs, *(struct(array.shape, array.dtype) for array in passed)],
        cost_estimate=pl.CostEstimate(flops=flops, bytes_accessed=moved, transcendentals=0),
        compiler_params=pltpu.CompilerParams(vmem_limit_bytes=LIMIT),
        in_specs=[*in_specs] + [ANY] * (len(passed) + len(after)),
        out_specs=[VMEM] * len(outs) + [ANY] * len(passed),
        scratch_shapes=list(scratch_shapes),
        input_output_aliases={first + i: len(outs) + i for i in range(len(passed))},
    )(*operands, *passed, *after)
    if passed:
        return [*given[: len(outs)], list(given[len(outs) :])]
    return given[0] if single else list(given)


def struct(shape, dtype):
    return jax.ShapeDtypeStruct(tuple(shape), dtype)


def here(axis):
    return lax.axis_index(axis).astype(jnp.int32)


def core():
    return lax.rem(here("slab"), 2)


def far_owners(side):
    me = here("slab")
    return [me ^ (2 * step) ^ side for step in range(lax.axis_size("slab") // 2)]


TOKEN = struct((8, 128), jnp.float32)


def stage_body(count, *refs):
    sources, targets, sems = refs[:count], refs[count : 2 * count], refs[2 * count]
    copies = [pltpu.make_async_copy(sources[i], targets[i], sems.at[i]) for i in range(count)]
    for copy in copies:
        copy.start()
    for copy in copies:
        copy.wait()


def stage(*arrays):
    count = len(arrays)
    return call(
        functools.partial(stage_body, count),
        [struct(array.shape, array.dtype) for array in arrays],
        (0, sum(4 * array.size for array in arrays)),
        *arrays,
        in_specs=[pl.BlockSpec(memory_space=pltpu.HBM)] * count,
        scratch_shapes=[pltpu.SemaphoreType.DMA((count,))],
    )


def inside(shape, axis, b, e):
    spot = lax.broadcasted_iota(jnp.int32, shape, axis)
    column = spot % WIDTH + e
    moved = spot + WIDTH * b
    return (column >= 0) & (column < WIDTH) & (moved >= 0) & (moved < shape[axis])


def shifted(values, axis, b, e):
    if b == 0 and e == 0:
        return values
    size = values.shape[axis]
    turned = pltpu.roll(values, (-(WIDTH * b + e)) % size, axis)
    return jnp.where(inside(values.shape, axis, b, e), turned, 0.0)


def fold_shifts(products):
    rows = products.shape[0] // len(SHIFTS)
    total = None
    for number, (b, e) in enumerate(SHIFTS):
        term = shifted(products[number * rows : (number + 1) * rows, :], 1, b, e)
        total = term if total is None else total + term
    return total


def dot(left, right):
    return jnp.dot(left, right, preferred_element_type=jnp.float32)


def edge_body(other_ref, out_ref):
    out_ref[0] = other_ref[(1 - core()) * (other_ref.shape[0] - 1)]


def edge(other):
    shape = (1, *other.shape[1:])
    return call(edge_body, struct(shape, other.dtype), (0, other.size), other, in_specs=[VMEM])


def assemble_body(count, *refs):
    parts, whole_ref, shares = refs[:count], refs[count], refs[count + 1 :]
    size = parts[0].shape[1]
    me, chip = here("filt"), here("slab") // 2
    for step in range(count):
        place = pl.ds(pl.multiple_of((me ^ step) * size, size), size)
        whole_ref[:, place, :] = parts[step][...]
    rows = shares[0].shape[2]
    for step, share_ref in enumerate(shares):
        for side in range(2):
            begin = pl.multiple_of(((chip ^ step) * 2 + side) * rows, rows)
            share_ref[side] = whole_ref[:, pl.ds(begin, rows), :]


def assemble(parts, after=()):
    planes, size, plane = parts[0].shape
    count, slabs = len(parts), lax.axis_size("slab")
    channels = size * count
    kind = parts[0].dtype
    outs = [struct((planes, channels, plane), kind)]
    outs += [struct((2, planes, channels // slabs, plane), kind)] * (slabs // 2)
    whole, *shares = call(
        functools.partial(assemble_body, count),
        outs,
        (0, 4 * planes * channels * plane),
        *parts,
        in_specs=[VMEM] * count,
        after=after,
    )
    return whole, shares


def pack_body(sides, count, *refs):
    out_ref = refs[-1]
    lanes = out_ref.shape[1]
    row = 0
    for number in range(sides):
        block = refs[number][1 - core()]
        rows = block.shape[0] * block.shape[1]
        out_ref[row : row + rows, :] = block.reshape(rows, lanes)
        row += rows
    for number in range(sides, count):
        planes, plane, filters = refs[number].shape
        for j in range(planes):
            for begin in range(0, plane, filters):
                out_ref[row : row + filters, begin : begin + filters] = refs[number][j, begin : begin + filters, :]
            row += filters


def pack(shares, blocks, after=()):
    plane = blocks[0].shape[1]
    total = sum(share.size // 2 for share in shares) + sum(block.size for block in blocks)
    count = len(shares) + len(blocks)
    return call(
        functools.partial(pack_body, len(shares), count),
        struct((total // plane, plane), blocks[0].dtype),
        (0, 4 * total),
        *shares, *blocks,
        in_specs=[VMEM] * count,
        after=after,
    )


def taps(weight_ref, number):
    block = weight_ref[pl.ds(9 * number, 9)]
    return block.reshape(block.shape[0] * block.shape[1], block.shape[2])


def forward_own_body(planes, volume_ref, other_ref, weight_ref, out_ref, acc_ref):
    for a in (0, 1, -1):
        weight = taps(weight_ref, a + 1)
        for j in range(planes):
            if 0 <= j + a < planes:
                product = dot(weight, volume_ref[j + a])
                acc_ref[j] = product if a == 0 else acc_ref[j] + product
    up, last = core(), planes - 1
    place = (1 - up) * last
    acc_ref[place] = acc_ref[place] + dot(taps(weight_ref, 2 * (1 - up)), other_ref[up * last])
    for j in range(planes):
        out_ref[j] = fold_shifts(acc_ref.at[j])


def forward_own(volume, other, weight, after=()):
    planes, channels, plane = volume.shape
    filters = weight.shape[1]
    return call(
        functools.partial(forward_own_body, planes),
        struct((planes, filters, plane), jnp.float32),
        (2 * 9 * filters * channels * plane * (3 * planes - 1), weight.size * 2),
        volume, other, weight,
        in_specs=[VMEM] * 3,
        scratch_shapes=[pltpu.VMEM((planes, 9 * filters, plane), jnp.float32)],
        after=after,
    )


def silu_and_slope(values):
    sig = 1.0 / (1.0 + jnp.exp(-values))
    return values * sig, sig * (1.0 + values * (1.0 - sig))


def forward_rest_body(planes, beyond_ref, weight_ref, own_ref, *refs):
    head_ref = refs[0] if len(refs) == 5 else None
    slope_ref, made_ref, acc_ref, total_ref = refs[-4:]
    up = core()
    place = up * (planes - 1)
    total_ref[...] = own_ref[...]
    acc_ref[...] = dot(taps(weight_ref, 2 * up), beyond_ref[0])
    total_ref[place] = total_ref[place] + fold_shifts(acc_ref)
    for j in range(planes):
        value, slope = silu_and_slope(total_ref[j])
        value = value.astype(jnp.bfloat16)
        slope_ref[j] = slope.T if head_ref is None else slope
        made_ref[j] = value if head_ref is None else dot(head_ref[...], value)


def forward_rest(beyond, weight, own, after, head=None):
    planes, filters, plane = own.shape
    channels = weight.shape[2]
    ins = [beyond, weight, own]
    slope = own.shape
    if head is None:
        slope = (planes, plane, filters)
        made = struct(own.shape, jnp.bfloat16)
    else:
        ins.append(head)
        made = struct((planes, head.shape[0], plane), jnp.float32)
    return call(
        functools.partial(forward_rest_body, planes),
        [struct(slope, jnp.float32), made],
        (2 * 9 * filters * channels * plane, weight.size * 2 // 3),
        *ins,
        in_specs=[VMEM] * len(ins),
        scratch_shapes=[
            pltpu.VMEM((9 * filters, plane), jnp.float32),
            pltpu.VMEM(own.shape, jnp.float32),
        ],
        after=after,
    )


def loss_body(count, labels_ref, head_ref, slope_ref, *refs):
    parts, grad_ref = refs[:count], refs[count]
    for j in range(grad_ref.shape[0]):
        logits = parts[0][j]
        for part in parts[1:]:
            logits = logits + part[j]
        powers = jnp.exp(logits)
        likely = powers / jnp.sum(powers, axis=0, keepdims=True)
        classes = lax.broadcasted_iota(jnp.int32, logits.shape, 0)
        onehot = (labels_ref[j : j + 1, :] == classes).astype(jnp.float32)
        logit_grad = (likely - onehot).astype(jnp.bfloat16).astype(jnp.float32)
        back = lax.dot_general(
            head_ref[...].astype(jnp.float32),
            logit_grad,
            (((0,), (0,)), ((), ())),
            preferred_element_type=jnp.float32,
        )
        grad_ref[j] = (back * slope_ref[j]).T.astype(jnp.bfloat16)


def loss_grad(parts, labels, head, slope):
    planes, plane = labels.shape
    return call(
        functools.partial(loss_body, len(parts)),
        struct((planes, plane, slope.shape[1]), jnp.bfloat16),
        (2 * slope.size * head.shape[0], slope.size * 6),
        labels, head, slope, *parts,
        in_specs=[VMEM] * (3 + len(parts)),
    )


def spread_back(grad, spread_ref):
    filters = grad.shape[1]
    turned = grad.astype(jnp.float32)
    for number, (b, e) in enumerate(SHIFTS):
        moved = shifted(turned, 0, -b, -e).astype(jnp.bfloat16)
        spread_ref[:, number * filters : (number + 1) * filters] = moved


def backward_own_body(planes, grad_ref, other_ref, weight_ref, out_ref, spread_ref):
    up, last = core(), planes - 1
    for j in range(planes):
        spread_back(grad_ref[j], spread_ref.at[j])
    spread_back(other_ref[up * last], spread_ref.at[planes])
    for a in (0, 1, -1):
        weight = taps(weight_ref, a + 1)
        for j in range(planes):
            if 0 <= j - a < planes:
                product = dot(spread_ref[j - a], weight)
                out_ref[j] = product if a == 0 else out_ref[j] + product
    place = (1 - up) * last
    out_ref[place] = out_ref[place] + dot(spread_ref[planes], taps(weight_ref, 2 * up))


def backward_own(grad, other, weight, after=()):
    planes, plane, filters = grad.shape
    channels = weight.shape[2]
    return call(
        functools.partial(backward_own_body, planes),
        struct((planes, plane, channels), jnp.float32),
        (2 * 9 * filters * channels * plane * (3 * planes - 1), weight.size * 2),
        grad, other, weight,
        in_specs=[VMEM] * 3,
        scratch_shapes=[pltpu.VMEM((planes + 1, plane, 9 * filters), jnp.bfloat16)],
        after=after,
    )


def backward_rest_body(planes, count, chips, steps, weight_ref, own_ref, *refs):
    near, refs = refs[: len(steps)], refs[len(steps) :]
    kept_ref, sent, (edge_ref, spread_ref, total_ref) = refs[0], refs[1:count], refs[count:]
    size = kept_ref.shape[2]
    up = core()
    place = up * (planes - 1)
    me, chip = here("filt"), here("slab") // 2
    other = chip + 2 * up - 1
    edge_ref[...] = jnp.zeros_like(edge_ref)
    for number, step in enumerate(steps):

        @pl.when((other >= 0) & (other < chips) & (chip ^ other == step))
        def _():
            edge_ref[...] = near[number][(1 - up) * (planes - 1)]

    spread_back(edge_ref[...], spread_ref)
    product = dot(spread_ref[...], taps(weight_ref, 2 * (1 - up)))
    for block in range(count):
        columns = slice(block * size, (block + 1) * size)
        for j in range(planes):
            total_ref[block, j] = own_ref[j, :, columns]
        total_ref[block, place] = total_ref[block, place] + product[:, columns]
    kept_ref[...] = total_ref[me]
    for number in range(1, count):
        sent[number - 1][...] = total_ref[me ^ number].astype(jnp.bfloat16)


def backward_rest(far, weight, own, count):
    planes, plane, channels = own.shape
    filters = weight.shape[1]
    size = channels // count
    chips = len(far) + 1
    steps = [1 << bits for bits in range(1, chips.bit_length())]
    steps = [step - 1 for step in steps if step <= chips]
    outs = [struct((planes, plane, size), jnp.float32)]
    outs += [struct((planes, plane, size), jnp.bfloat16)] * (count - 1)
    return call(
        functools.partial(backward_rest_body, planes, count, chips, steps),
        outs,
        (2 * 9 * filters * channels * plane, weight.size * 2 // 3),
        weight, own, *[far[step - 1] for step in steps],
        in_specs=[VMEM] * (2 + len(steps)),
        scratch_shapes=[
            pltpu.VMEM((plane, filters), jnp.bfloat16),
            pltpu.VMEM((plane, 9 * filters), jnp.bfloat16),
            pltpu.VMEM((count, planes, plane, size), jnp.float32),
        ],
    )


def first_grad_body(count, slope_ref, *refs):
    parts, out_ref = refs[:count], refs[count]
    for j in range(out_ref.shape[0]):
        total = parts[0][j]
        for part in parts[1:]:
            total = total + part[j].astype(jnp.float32)
        out_ref[j] = (total * slope_ref[j]).astype(jnp.bfloat16)


def first_out(parts, slope):
    return call(
        functools.partial(first_grad_body, len(parts)),
        struct(slope.shape, jnp.bfloat16),
        (slope.size * 4, slope.size * 14),
        slope, *parts,
        in_specs=[VMEM] * (1 + len(parts)),
    )


def spread_body(count, row, crossed_ref, *refs):
    shares, (spread_ref, token_ref) = refs[:count], refs[count:]
    _, planes, channels, plane = shares[0].shape
    token_ref[...] = jnp.zeros_like(token_ref)

    def one(values, d):
        values = values.astype(jnp.float32)
        place = pl.ds(pl.multiple_of(d * plane, plane), plane)
        for number, (b, e) in enumerate(SHIFTS):
            moved = shifted(values, 1, b, e).astype(jnp.bfloat16)
            spread_ref[number * channels : (number + 1) * channels, place] = moved

    owners, side = far_owners(0), core()
    for step in range(count):
        for j in range(planes):
            one(shares[step][side, j], owners[step] * planes + j)
            begin = row + (step * planes + j) * channels
            one(crossed_ref[begin : begin + channels, :], (owners[step] ^ 1) * planes + j)


def spread(shares, crossed, row):
    _, planes, channels, plane = shares[0].shape
    count = len(shares)
    depth = 2 * count * planes
    return call(
        functools.partial(spread_body, count, row),
        [struct((9 * channels, depth * plane), jnp.bfloat16), TOKEN],
        (9 * channels * depth * plane, 10 * channels * depth * plane),
        crossed, *shares,
        in_specs=[VMEM] * (1 + count),
    )


def weight_grad_body(count, row, second, spread_ref, crossed_ref, *refs):
    parts, (out_ref, token_ref, grad_ref) = refs[:count], refs[count:]
    token_ref[...] = jnp.zeros_like(token_ref)
    planes, plane, filters = parts[0].shape
    channels = spread_ref.shape[0] // 9
    depth = spread_ref.shape[1] // plane
    zero = jnp.zeros((plane, filters), jnp.bfloat16)
    grad_ref[depth * plane : (depth + 1) * plane, : filters] = zero
    grad_ref[plane : 2 * plane, 2 * filters :] = zero

    def one(block, d, begin):
        rows = block.shape[0]
        for a in (-1, 0, 1):
            place = pl.ds(pl.multiple_of((d + a + 1) * plane + begin, rows), rows)
            grad_ref[place, (a + 1) * filters : (a + 2) * filters] = block

    near, far = far_owners(0), far_owners(1)
    owners = [near[0], *far, *near[1:]] if second else near + far
    for number in range(count):
        for j in range(planes):
            one(parts[number][j], owners[number] * planes + j, 0)
    for number in range(count, len(owners)):
        for j in range(planes):
            for begin in range(0, plane, filters):
                block = crossed_ref[row : row + filters, begin : begin + filters]
                one(block, owners[number] * planes + j, begin)
            row += filters

    product = dot(spread_ref[...], grad_ref[plane : (depth + 1) * plane, :])
    for r in range(3):
        for number in range(9):
            out_ref[r * 9 + number] = product[
                number * channels : (number + 1) * channels, r * filters : (r + 1) * filters
            ]


def weight_grad(spreads, blocks, crossed, row, second):
    channels, columns = spreads.shape[0] // 9, spreads.shape[1]
    _, plane, filters = blocks[0].shape
    return call(
        functools.partial(weight_grad_body, len(blocks), row, second),
        [struct((27, channels, filters), jnp.float32), TOKEN],
        (2 * 27 * filters * channels * columns, 27 * channels * filters * 4 + spreads.size * 2),
        spreads, crossed, *blocks,
        in_specs=[VMEM] * (2 + len(blocks)),
        scratch_shapes=[pltpu.VMEM((columns + 2 * plane, 3 * filters), jnp.bfloat16)],
    )


def shards(features, first_weight, second_weight, head_weight, labels):
    count = lax.axis_size("filt")
    chips = lax.axis_size("slab") // 2
    near, first_weight, head_weight = stage(features, first_weight, head_weight)
    all_in, share_in = assemble([near] + exchanged(features, "filt")[1:])
    other, beyond = halo(all_in)
    share_in = [share_in[0]] + chips_apart(share_in[1:])
    own = forward_own(all_in, other, first_weight)
    slope_first, hidden = forward_rest(beyond, first_weight, own, share_in[1:])

    all_hidden, share_hidden = assemble(exchanged(hidden, "filt"))
    other, beyond = halo(all_hidden)
    share_hidden = [share_hidden[0]] + chips_apart(share_hidden[1:])
    own = forward_own(all_hidden, other, second_weight)
    slope_second, logits = forward_rest(beyond, second_weight, own, share_hidden[1:], head_weight)

    second_out = loss_grad(exchanged(logits, "filt"), labels, head_weight, slope_second)
    second_other = swap(second_out, "slab", 1)
    second_far = chips_apart([second_other] * (chips - 1))
    own = backward_own(second_out, second_other, second_weight)
    kept, *sent = backward_rest(second_far, second_weight, own, count)
    parts = [kept] + [swap(part, "filt", 1 + number) for number, part in enumerate(sent)]
    first_out_grad = first_out(parts, slope_first)

    first_blocks = [first_out_grad] + chips_apart([first_out_grad] * (chips - 1))
    crossed = swap(pack(share_in + share_hidden, second_far, parts[1:2]), "slab", 1)
    rows = sum(share.size // 2 for share in share_in) // features.shape[2]
    spread_hidden, _ = spread(share_hidden, crossed, rows)
    blocks = [second_out, second_other] + second_far
    second_grad, second_token = weight_grad(spread_hidden, blocks, crossed, 2 * rows, True)
    spread_in, token = spread(share_in, crossed, 0)
    crossed = swap(pack([], first_blocks, [token, second_token]), "slab", 1)
    first_grad, _ = weight_grad(spread_in, first_blocks, crossed, 0, False)
    return jnp.transpose(first_grad, (0, 2, 1)), jnp.transpose(second_grad, (0, 2, 1))


def solution(mesh):
    placed = (
        P("slab", "filt", None),
        P(None, "filt", None),
        P(None, "filt", None),
        P(None, "filt"),
        P("slab", None),
    )
    return jax.shard_map(
        shards,
        mesh=mesh,
        in_specs=placed,
        out_specs=(P(None, "filt", "slab"), P(None, "filt", "slab")),
        check_vma=False,
    )
```

```python
import functools

import jax
import jax.numpy as jnp
from jax import lax
from jax.experimental import pallas as pl
from jax.experimental.pallas import tpu as pltpu
from jax.sharding import PartitionSpec as P

WIDTH = 8
SHIFTS = [(b, e) for b in (-1, 0, 1) for e in (-1, 0, 1)]
LIMIT = 20 * 1024 * 1024
VMEM = pl.BlockSpec(memory_space=pltpu.VMEM)
ANY = pl.BlockSpec(memory_space=pl.ANY)


def swap(block, axis, step):
    count = lax.axis_size(axis)
    return lax.ppermute(block, axis, [(i, i ^ step) for i in range(count)])


def exchanged(block, axis):
    return [block] + [swap(block, axis, step) for step in range(1, lax.axis_size(axis))]


def halo(volume):
    count = lax.axis_size("slab")
    other = swap(volume, "slab", 1)
    passed = edge(other)
    pairs = [(i, i + 2) for i in range(0, count - 2, 2)] + [(i, i - 2) for i in range(3, count, 2)]
    return other, lax.ppermute(passed, "slab", pairs)


def chips_apart(blocks):
    return [swap(block, "slab", 2 + 2 * number) for number, block in enumerate(blocks)]


def call(body, out_shape, cost, *operands, in_specs, scratch_shapes=(), passed=(), after=()):
    flops, moved = cost
    single = not isinstance(out_shape, list)
    outs = [out_shape] if single else out_shape
    first, second = len(operands), len(operands) + len(passed) + len(after)
    third = second + len(outs)

    def inner(*refs):
        body(*refs[:first], *refs[second:third], *refs[third + len(passed) :])

    given = pl.pallas_call(
        inner,
        out_shape=[*outs, *(struct(array.shape, array.dtype) for array in passed)],
        cost_estimate=pl.CostEstimate(flops=flops, bytes_accessed=moved, transcendentals=0),
        compiler_params=pltpu.CompilerParams(vmem_limit_bytes=LIMIT),
        in_specs=[*in_specs] + [ANY] * (len(passed) + len(after)),
        out_specs=[VMEM] * len(outs) + [ANY] * len(passed),
        scratch_shapes=list(scratch_shapes),
        input_output_aliases={first + i: len(outs) + i for i in range(len(passed))},
    )(*operands, *passed, *after)
    if passed:
        return [*given[: len(outs)], list(given[len(outs) :])]
    return given[0] if single else list(given)


def struct(shape, dtype):
    return jax.ShapeDtypeStruct(tuple(shape), dtype)


def here(axis):
    return lax.axis_index(axis).astype(jnp.int32)


def core():
    return lax.rem(here("slab"), 2)


def far_owners(side):
    me = here("slab")
    return [me ^ (2 * step) ^ side for step in range(lax.axis_size("slab") // 2)]


TOKEN = struct((8, 128), jnp.float32)


def stage_body(count, *refs):
    sources, targets, sems = refs[:count], refs[count : 2 * count], refs[2 * count]
    copies = [pltpu.make_async_copy(sources[i], targets[i], sems.at[i]) for i in range(count)]
    for copy in copies:
        copy.start()
    for copy in copies:
        copy.wait()


def stage(*arrays):
    count = len(arrays)
    return call(
        functools.partial(stage_body, count),
        [struct(array.shape, array.dtype) for array in arrays],
        (0, sum(4 * array.size for array in arrays)),
        *arrays,
        in_specs=[pl.BlockSpec(memory_space=pltpu.HBM)] * count,
        scratch_shapes=[pltpu.SemaphoreType.DMA((count,))],
    )


def inside(shape, axis, b, e):
    spot = lax.broadcasted_iota(jnp.int32, shape, axis)
    column = spot % WIDTH + e
    moved = spot + WIDTH * b
    return (column >= 0) & (column < WIDTH) & (moved >= 0) & (moved < shape[axis])


def shifted(values, axis, b, e):
    if b == 0 and e == 0:
        return values
    size = values.shape[axis]
    turned = pltpu.roll(values, (-(WIDTH * b + e)) % size, axis)
    return jnp.where(inside(values.shape, axis, b, e), turned, 0.0)


def fold_shifts(products):
    rows = products.shape[0] // len(SHIFTS)
    total = None
    for number, (b, e) in enumerate(SHIFTS):
        term = shifted(products[number * rows : (number + 1) * rows, :], 1, b, e)
        total = term if total is None else total + term
    return total


def dot(left, right):
    return jnp.dot(left, right, preferred_element_type=jnp.float32)


def edge_body(other_ref, out_ref):
    out_ref[0] = other_ref[(1 - core()) * (other_ref.shape[0] - 1)]


def edge(other):
    shape = (1, *other.shape[1:])
    return call(edge_body, struct(shape, other.dtype), (0, other.size), other, in_specs=[VMEM])


def halves(rows):
    return 2 if rows % 32 == 0 and lax.axis_size("filt") % 2 == 0 else 1


def assemble_body(count, split, *refs):
    parts, whole_ref, shares = refs[:count], refs[count], refs[count + 1 :]
    size = parts[0].shape[1]
    me, chip = here("filt"), here("slab") // 2
    for step in range(count):
        place = pl.ds(pl.multiple_of((me ^ step) * size, size), size)
        whole_ref[:, place, :] = parts[step][...]
    rows = shares[0].shape[2]
    for step, share_ref in enumerate(shares):
        for side in range(2):
            begin = (((chip ^ step) * 2 + side) * split + lax.rem(me, split)) * rows
            share_ref[side] = whole_ref[:, pl.ds(pl.multiple_of(begin, rows), rows), :]


def assemble(parts):
    planes, size, plane = parts[0].shape
    count, slabs = len(parts), lax.axis_size("slab")
    channels = size * count
    split = halves(channels // slabs)
    kind = parts[0].dtype
    outs = [struct((planes, channels, plane), kind)]
    outs += [struct((2, planes, channels // slabs // split, plane), kind)] * (slabs // 2)
    whole, *shares = call(
        functools.partial(assemble_body, count, split),
        outs,
        (0, 4 * planes * channels * plane),
        *parts,
        in_specs=[VMEM] * count,
    )
    return whole, shares


def crossing_body(count, *refs):
    planes = refs[0].shape[1]
    for step in range(count):
        for j in range(planes):
            refs[count][step * planes + j] = refs[step][1 - core(), j]


def collect_body(count, crossed_ref, *refs):
    owners, side = far_owners(0), core()
    planes = refs[0].shape[1]
    for step in range(count):
        for j in range(planes):
            refs[count][owners[step] * planes + j] = refs[step][side, j]
            refs[count][(owners[step] ^ 1) * planes + j] = crossed_ref[step * planes + j]


def collected(shares, after=()):
    count = len(shares)
    _, planes, rows, plane = shares[0].shape
    kind, size = shares[0].dtype, shares[0].size * count
    crossing = call(
        functools.partial(crossing_body, count),
        struct((count * planes, rows, plane), kind),
        (0, 2 * size),
        *shares,
        in_specs=[VMEM] * count,
        after=after,
    )
    return call(
        functools.partial(collect_body, count),
        struct((2 * count * planes, rows, plane), kind),
        (0, 4 * size),
        swap(crossing, "slab", 1), *shares,
        in_specs=[VMEM] * (1 + count),
    )


def both_halves(volume, split):
    return [volume] + ([swap(volume, "filt", 1)] if split == 2 else [])


def pack_body(count, *refs):
    out_ref = refs[count]
    row = 0
    for number in range(count):
        planes, plane, filters = refs[number].shape
        for j in range(planes):
            for begin in range(0, plane, filters):
                out_ref[row : row + filters, begin : begin + filters] = refs[number][j, begin : begin + filters, :]
            row += filters


def pack(blocks, after=()):
    plane = blocks[0].shape[1]
    total = sum(block.size for block in blocks)
    return call(
        functools.partial(pack_body, len(blocks)),
        struct((total // plane, plane), blocks[0].dtype),
        (0, 4 * total),
        *blocks,
        in_specs=[VMEM] * len(blocks),
        after=after,
    )


def taps(weight_ref, number):
    block = weight_ref[pl.ds(9 * number, 9)]
    return block.reshape(block.shape[0] * block.shape[1], block.shape[2])


def forward_own_body(planes, volume_ref, other_ref, weight_ref, out_ref, acc_ref):
    for a in (0, 1, -1):
        weight = taps(weight_ref, a + 1)
        for j in range(planes):
            if 0 <= j + a < planes:
                product = dot(weight, volume_ref[j + a])
                acc_ref[j] = product if a == 0 else acc_ref[j] + product
    up, last = core(), planes - 1
    place = (1 - up) * last
    acc_ref[place] = acc_ref[place] + dot(taps(weight_ref, 2 * (1 - up)), other_ref[up * last])
    for j in range(planes):
        out_ref[j] = fold_shifts(acc_ref.at[j])


def forward_own(volume, other, weight, after=()):
    planes, channels, plane = volume.shape
    filters = weight.shape[1]
    return call(
        functools.partial(forward_own_body, planes),
        struct((planes, filters, plane), jnp.float32),
        (2 * 9 * filters * channels * plane * (3 * planes - 1), weight.size * 2),
        volume, other, weight,
        in_specs=[VMEM] * 3,
        scratch_shapes=[pltpu.VMEM((planes, 9 * filters, plane), jnp.float32)],
        after=after,
    )


def silu_and_slope(values):
    sig = 1.0 / (1.0 + jnp.exp(-values))
    return values * sig, sig * (1.0 + values * (1.0 - sig))


def forward_rest_body(planes, beyond_ref, weight_ref, own_ref, *refs):
    head_ref = refs[0] if len(refs) == 5 else None
    slope_ref, made_ref, acc_ref, total_ref = refs[-4:]
    up = core()
    place = up * (planes - 1)
    total_ref[...] = own_ref[...]
    acc_ref[...] = dot(taps(weight_ref, 2 * up), beyond_ref[0])
    total_ref[place] = total_ref[place] + fold_shifts(acc_ref)
    for j in range(planes):
        value, slope = silu_and_slope(total_ref[j])
        value = value.astype(jnp.bfloat16)
        slope_ref[j] = slope.T if head_ref is None else slope
        made_ref[j] = value if head_ref is None else dot(head_ref[...], value)


def forward_rest(beyond, weight, own, after, head=None):
    planes, filters, plane = own.shape
    channels = weight.shape[2]
    ins = [beyond, weight, own]
    slope = own.shape
    if head is None:
        slope = (planes, plane, filters)
        made = struct(own.shape, jnp.bfloat16)
    else:
        ins.append(head)
        made = struct((planes, head.shape[0], plane), jnp.float32)
    return call(
        functools.partial(forward_rest_body, planes),
        [struct(slope, jnp.float32), made],
        (2 * 9 * filters * channels * plane, weight.size * 2 // 3),
        *ins,
        in_specs=[VMEM] * len(ins),
        scratch_shapes=[
            pltpu.VMEM((9 * filters, plane), jnp.float32),
            pltpu.VMEM(own.shape, jnp.float32),
        ],
        after=after,
    )


def loss_body(count, labels_ref, head_ref, slope_ref, *refs):
    parts, grad_ref = refs[:count], refs[count]
    for j in range(grad_ref.shape[0]):
        logits = parts[0][j]
        for part in parts[1:]:
            logits = logits + part[j]
        powers = jnp.exp(logits)
        likely = powers / jnp.sum(powers, axis=0, keepdims=True)
        classes = lax.broadcasted_iota(jnp.int32, logits.shape, 0)
        onehot = (labels_ref[j : j + 1, :] == classes).astype(jnp.float32)
        logit_grad = (likely - onehot).astype(jnp.bfloat16).astype(jnp.float32)
        back = lax.dot_general(
            head_ref[...].astype(jnp.float32),
            logit_grad,
            (((0,), (0,)), ((), ())),
            preferred_element_type=jnp.float32,
        )
        grad_ref[j] = (back * slope_ref[j]).T.astype(jnp.bfloat16)


def loss_grad(parts, labels, head, slope, after):
    planes, plane = labels.shape
    return call(
        functools.partial(loss_body, len(parts)),
        struct((planes, plane, slope.shape[1]), jnp.bfloat16),
        (2 * slope.size * head.shape[0], slope.size * 6),
        labels, head, slope, *parts,
        in_specs=[VMEM] * (3 + len(parts)),
        after=after,
    )


def spread_back(grad, spread_ref):
    filters = grad.shape[1]
    turned = grad.astype(jnp.float32)
    for number, (b, e) in enumerate(SHIFTS):
        moved = shifted(turned, 0, -b, -e).astype(jnp.bfloat16)
        spread_ref[:, number * filters : (number + 1) * filters] = moved


def backward_own_body(planes, grad_ref, other_ref, weight_ref, out_ref, spread_ref):
    up, last = core(), planes - 1
    for j in range(planes):
        spread_back(grad_ref[j], spread_ref.at[j])
    spread_back(other_ref[up * last], spread_ref.at[planes])
    for a in (0, 1, -1):
        weight = taps(weight_ref, a + 1)
        for j in range(planes):
            if 0 <= j - a < planes:
                product = dot(spread_ref[j - a], weight)
                out_ref[j] = product if a == 0 else out_ref[j] + product
    place = (1 - up) * last
    out_ref[place] = out_ref[place] + dot(spread_ref[planes], taps(weight_ref, 2 * up))


def backward_own(grad, other, weight, after=()):
    planes, plane, filters = grad.shape
    channels = weight.shape[2]
    return call(
        functools.partial(backward_own_body, planes),
        struct((planes, plane, channels), jnp.float32),
        (2 * 9 * filters * channels * plane * (3 * planes - 1), weight.size * 2),
        grad, other, weight,
        in_specs=[VMEM] * 3,
        scratch_shapes=[pltpu.VMEM((planes + 1, plane, 9 * filters), jnp.bfloat16)],
        after=after,
    )


def backward_rest_body(planes, count, grad_ref, beyond_ref, weight_ref, own_ref, *refs):
    copy_ref, kept_ref, sent, (spread_ref, total_ref) = refs[0], refs[1], refs[2 : 1 + count], refs[1 + count :]
    copy_ref[...] = grad_ref[...]
    size = kept_ref.shape[2]
    up, me = core(), here("filt")
    place = up * (planes - 1)
    spread_back(beyond_ref[0], spread_ref)
    product = dot(spread_ref[...], taps(weight_ref, 2 * (1 - up)))
    for block in range(count):
        columns = slice(block * size, (block + 1) * size)
        for j in range(planes):
            total_ref[block, j] = own_ref[j, :, columns]
        total_ref[block, place] = total_ref[block, place] + product[:, columns]
    kept_ref[...] = total_ref[me]
    for number in range(1, count):
        sent[number - 1][...] = total_ref[me ^ number].astype(jnp.bfloat16)


def backward_rest(grad, beyond, weight, own, count, after):
    planes, plane, channels = own.shape
    filters = weight.shape[1]
    size = channels // count
    outs = [struct(grad.shape, grad.dtype), struct((planes, plane, size), jnp.float32)]
    outs += [struct((planes, plane, size), jnp.bfloat16)] * (count - 1)
    return call(
        functools.partial(backward_rest_body, planes, count),
        outs,
        (2 * 9 * filters * channels * plane, weight.size * 2 // 3),
        grad, beyond, weight, own,
        in_specs=[VMEM] * 4,
        scratch_shapes=[
            pltpu.VMEM((plane, 9 * filters), jnp.bfloat16),
            pltpu.VMEM((count, planes, plane, size), jnp.float32),
        ],
        after=after,
    )


def first_grad_body(count, slope_ref, *refs):
    parts, out_ref = refs[:count], refs[count]
    for j in range(out_ref.shape[0]):
        total = parts[0][j]
        for part in parts[1:]:
            total = total + part[j].astype(jnp.float32)
        out_ref[j] = (total * slope_ref[j]).astype(jnp.bfloat16)


def first_out(parts, slope, after):
    return call(
        functools.partial(first_grad_body, len(parts)),
        struct(slope.shape, jnp.bfloat16),
        (slope.size * 4, slope.size * 14),
        slope, *parts,
        in_specs=[VMEM] * (1 + len(parts)),
        after=after,
    )


def spread_body(split, *refs):
    spread_ref, token_ref = refs[split:]
    token_ref[...] = jnp.zeros_like(token_ref)
    depth, rows, plane = refs[0].shape
    me = lax.rem(here("filt"), split)
    for d in range(depth):
        for half in range(split):
            values = refs[half][d].astype(jnp.float32)
            for number, (b, e) in enumerate(SHIFTS):
                begin = (number * split + (me ^ half)) * rows
                moved = shifted(values, 1, b, e).astype(jnp.bfloat16)
                spread_ref[pl.ds(pl.multiple_of(begin, rows), rows), d * plane : (d + 1) * plane] = moved


def spread(halved):
    split = len(halved)
    depth, rows, plane = halved[0].shape
    channels = split * rows
    return call(
        functools.partial(spread_body, split),
        [struct((9 * channels, depth * plane), jnp.bfloat16), TOKEN],
        (9 * channels * depth * plane, 10 * channels * depth * plane),
        *halved,
        in_specs=[VMEM] * split,
    )


def weight_grad_body(count, second, spread_ref, crossed_ref, *refs):
    parts, (out_ref, token_ref, grad_ref) = refs[:count], refs[count:]
    token_ref[...] = jnp.zeros_like(token_ref)
    planes, plane, filters = parts[0].shape
    channels = spread_ref.shape[0] // 9
    depth = spread_ref.shape[1] // plane
    zero = jnp.zeros((plane, filters), jnp.bfloat16)
    grad_ref[depth * plane : (depth + 1) * plane, : filters] = zero
    grad_ref[plane : 2 * plane, 2 * filters :] = zero

    def one(block, d, begin):
        rows = block.shape[0]
        for a in (-1, 0, 1):
            place = pl.ds(pl.multiple_of((d + a + 1) * plane + begin, rows), rows)
            grad_ref[place, (a + 1) * filters : (a + 2) * filters] = block

    near, far = far_owners(0), far_owners(1)
    owners = [near[0], far[0], *near[1:], *far[1:]] if second else near + far
    row = 0
    for number in range(count):
        for j in range(planes):
            one(parts[number][j], owners[number] * planes + j, 0)
    for number in range(count, len(owners)):
        for j in range(planes):
            for begin in range(0, plane, filters):
                block = crossed_ref[row : row + filters, begin : begin + filters]
                one(block, owners[number] * planes + j, begin)
            row += filters

    product = dot(spread_ref[...], grad_ref[plane : (depth + 1) * plane, :])
    for r in range(3):
        for number in range(9):
            out_ref[r * 9 + number] = product[
                number * channels : (number + 1) * channels, r * filters : (r + 1) * filters
            ]


def weight_grad(spreads, blocks, crossed, second):
    channels, columns = spreads.shape[0] // 9, spreads.shape[1]
    _, plane, filters = blocks[0].shape
    return call(
        functools.partial(weight_grad_body, len(blocks), second),
        [struct((27, channels, filters), jnp.float32), TOKEN],
        (2 * 27 * filters * channels * columns, 27 * channels * filters * 4 + spreads.size * 2),
        spreads, crossed, *blocks,
        in_specs=[VMEM] * (2 + len(blocks)),
        scratch_shapes=[pltpu.VMEM((columns + 2 * plane, 3 * filters), jnp.bfloat16)],
    )


def shards(features, first_weight, second_weight, head_weight, labels):
    count = lax.axis_size("filt")
    chips = lax.axis_size("slab") // 2
    split = halves(features.shape[1] * count // lax.axis_size("slab"))
    near, first_weight, head_weight = stage(features, first_weight, head_weight)
    all_in, share_in = assemble([near] + exchanged(features, "filt")[1:])
    other, beyond = halo(all_in)
    share_in = [share_in[0]] + chips_apart(share_in[1:])
    own = forward_own(all_in, other, first_weight)
    slope_first, hidden = forward_rest(beyond, first_weight, own, share_in[1:])

    all_hidden, share_hidden = assemble(exchanged(hidden, "filt"))
    other, beyond = halo(all_hidden)
    share_hidden = [share_hidden[0]] + chips_apart(share_hidden[1:])
    halved_in = both_halves(collected(share_in), split)
    own = forward_own(all_hidden, other, second_weight)
    due = share_hidden[1:] + halved_in
    slope_second, logits = forward_rest(beyond, second_weight, own, due, head_weight)

    halved_hidden = both_halves(collected(share_hidden, [logits]), split)
    second_out = loss_grad(exchanged(logits, "filt"), labels, head_weight, slope_second, halved_hidden[:1])
    second_other, beyond = halo(second_out)
    own = backward_own(second_out, second_other, second_weight)
    second_copy, kept, *sent = backward_rest(second_out, beyond, second_weight, own, count, halved_hidden)
    parts = [kept] + [swap(part, "filt", 1 + number) for number, part in enumerate(sent)]
    second_far = chips_apart([second_copy] * (chips - 1))
    spread_in, token = spread(halved_in)
    first_out_grad = first_out(parts, slope_first, [token])

    first_blocks = [first_out_grad] + chips_apart([first_out_grad] * (chips - 1))
    crossed = swap(pack(second_far, first_blocks[1:2]), "slab", 1)
    spread_hidden, _ = spread(halved_hidden)
    second_grad, token = weight_grad(spread_hidden, [second_out, second_other] + second_far, crossed, True)
    crossed = swap(pack(first_blocks, [token]), "slab", 1)
    first_grad, _ = weight_grad(spread_in, first_blocks, crossed, False)
    return jnp.transpose(first_grad, (0, 2, 1)), jnp.transpose(second_grad, (0, 2, 1))


def solution(mesh):
    placed = (
        P("slab", "filt", None),
        P(None, "filt", None),
        P(None, "filt", None),
        P(None, "filt"),
        P("slab", None),
    )
    return jax.shard_map(
        shards,
        mesh=mesh,
        in_specs=placed,
        out_specs=(P(None, "filt", "slab"), P(None, "filt", "slab")),
        check_vma=False,
    )
```

```python
import functools

import jax
import jax.numpy as jnp
from jax import lax
from jax.experimental import pallas as pl
from jax.experimental.pallas import tpu as pltpu
from jax.sharding import PartitionSpec as P

WIDTH = 8
SHIFTS = [(b, e) for b in (-1, 0, 1) for e in (-1, 0, 1)]
LIMIT = 20 * 1024 * 1024
VMEM = pl.BlockSpec(memory_space=pltpu.VMEM)
ANY = pl.BlockSpec(memory_space=pl.ANY)


def swap(block, axis, step):
    count = lax.axis_size(axis)
    return lax.ppermute(block, axis, [(i, i ^ step) for i in range(count)])


def exchanged(block, axis):
    return [block] + [swap(block, axis, step) for step in range(1, lax.axis_size(axis))]


def halo(volume):
    count = lax.axis_size("slab")
    other = swap(volume, "slab", 1)
    passed = edge(other)
    pairs = [(i, i + 2) for i in range(0, count - 2, 2)] + [(i, i - 2) for i in range(3, count, 2)]
    return other, lax.ppermute(passed, "slab", pairs)


def chips_apart(blocks):
    return [swap(block, "slab", 2 + 2 * number) for number, block in enumerate(blocks)]


def call(body, out_shape, cost, *operands, in_specs, scratch_shapes=(), passed=(), after=()):
    flops, moved = cost
    single = not isinstance(out_shape, list)
    outs = [out_shape] if single else out_shape
    first, second = len(operands), len(operands) + len(passed) + len(after)
    third = second + len(outs)

    def inner(*refs):
        body(*refs[:first], *refs[second:third], *refs[third + len(passed) :])

    given = pl.pallas_call(
        inner,
        out_shape=[*outs, *(struct(array.shape, array.dtype) for array in passed)],
        cost_estimate=pl.CostEstimate(flops=flops, bytes_accessed=moved, transcendentals=0),
        compiler_params=pltpu.CompilerParams(vmem_limit_bytes=LIMIT),
        in_specs=[*in_specs] + [ANY] * (len(passed) + len(after)),
        out_specs=[VMEM] * len(outs) + [ANY] * len(passed),
        scratch_shapes=list(scratch_shapes),
        input_output_aliases={first + i: len(outs) + i for i in range(len(passed))},
    )(*operands, *passed, *after)
    if passed:
        return [*given[: len(outs)], list(given[len(outs) :])]
    return given[0] if single else list(given)


def struct(shape, dtype):
    return jax.ShapeDtypeStruct(tuple(shape), dtype)


def here(axis):
    return lax.axis_index(axis).astype(jnp.int32)


def core():
    return lax.rem(here("slab"), 2)


def far_owners(side):
    me = here("slab")
    return [me ^ (2 * step) ^ side for step in range(lax.axis_size("slab") // 2)]


TOKEN = struct((8, 128), jnp.float32)


def stage_body(count, *refs):
    sources, targets, sems = refs[:count], refs[count : 2 * count], refs[2 * count]
    copies = [pltpu.make_async_copy(sources[i], targets[i], sems.at[i]) for i in range(count)]
    for copy in copies:
        copy.start()
    for copy in copies:
        copy.wait()


def stage(*arrays):
    count = len(arrays)
    return call(
        functools.partial(stage_body, count),
        [struct(array.shape, array.dtype) for array in arrays],
        (0, sum(4 * array.size for array in arrays)),
        *arrays,
        in_specs=[pl.BlockSpec(memory_space=pltpu.HBM)] * count,
        scratch_shapes=[pltpu.SemaphoreType.DMA((count,))],
    )


def inside(shape, axis, b, e):
    spot = lax.broadcasted_iota(jnp.int32, shape, axis)
    column = spot % WIDTH + e
    moved = spot + WIDTH * b
    return (column >= 0) & (column < WIDTH) & (moved >= 0) & (moved < shape[axis])


def shifted(values, axis, b, e):
    if b == 0 and e == 0:
        return values
    size = values.shape[axis]
    turned = pltpu.roll(values, (-(WIDTH * b + e)) % size, axis)
    return jnp.where(inside(values.shape, axis, b, e), turned, 0.0)


def fold_shifts(products):
    rows = products.shape[0] // len(SHIFTS)
    total = None
    for number, (b, e) in enumerate(SHIFTS):
        term = shifted(products[number * rows : (number + 1) * rows, :], 1, b, e)
        total = term if total is None else total + term
    return total


def dot(left, right):
    return jnp.dot(left, right, preferred_element_type=jnp.float32)


def edge_body(other_ref, out_ref):
    out_ref[0] = other_ref[(1 - core()) * (other_ref.shape[0] - 1)]


def edge(other):
    shape = (1, *other.shape[1:])
    return call(edge_body, struct(shape, other.dtype), (0, other.size), other, in_specs=[VMEM])


def halves(rows):
    return 2 if rows % 32 == 0 and lax.axis_size("filt") % 2 == 0 else 1


def assemble_body(count, split, *refs):
    parts, whole_ref, shares = refs[:count], refs[count], refs[count + 1 :]
    size = parts[0].shape[1]
    me, chip = here("filt"), here("slab") // 2
    for step in range(count):
        place = pl.ds(pl.multiple_of((me ^ step) * size, size), size)
        whole_ref[:, place, :] = parts[step][...]
    rows = shares[0].shape[2]
    for step, share_ref in enumerate(shares):
        for side in range(2):
            begin = (((chip ^ step) * 2 + side) * split + lax.rem(me, split)) * rows
            share_ref[side] = whole_ref[:, pl.ds(pl.multiple_of(begin, rows), rows), :]


def assemble(parts, after=()):
    planes, size, plane = parts[0].shape
    count, slabs = len(parts), lax.axis_size("slab")
    channels = size * count
    split = halves(channels // slabs)
    kind = parts[0].dtype
    outs = [struct((planes, channels, plane), kind)]
    outs += [struct((2, planes, channels // slabs // split, plane), kind)] * (slabs // 2)
    whole, *shares = call(
        functools.partial(assemble_body, count, split),
        outs,
        (0, 4 * planes * channels * plane),
        *parts,
        in_specs=[VMEM] * count,
        after=after,
    )
    return whole, shares


def crossing_body(count, *refs):
    planes = refs[0].shape[1]
    for step in range(count):
        for j in range(planes):
            refs[count][step * planes + j] = refs[step][1 - core(), j]


def collect_body(count, crossed_ref, *refs):
    owners, side = far_owners(0), core()
    planes = refs[0].shape[1]
    for step in range(count):
        for j in range(planes):
            refs[count][owners[step] * planes + j] = refs[step][side, j]
            refs[count][(owners[step] ^ 1) * planes + j] = crossed_ref[step * planes + j]


def collected(shares, after=()):
    count = len(shares)
    _, planes, rows, plane = shares[0].shape
    kind, size = shares[0].dtype, shares[0].size * count
    crossing = call(
        functools.partial(crossing_body, count),
        struct((count * planes, rows, plane), kind),
        (0, 2 * size),
        *shares,
        in_specs=[VMEM] * count,
        after=after,
    )
    return call(
        functools.partial(collect_body, count),
        struct((2 * count * planes, rows, plane), kind),
        (0, 4 * size),
        swap(crossing, "slab", 1), *shares,
        in_specs=[VMEM] * (1 + count),
    )


def both_halves(volume, split):
    return [volume] + ([swap(volume, "filt", 1)] if split == 2 else [])


def pack_body(count, *refs):
    out_ref = refs[count]
    row = 0
    for number in range(count):
        planes, plane, filters = refs[number].shape
        for j in range(planes):
            for begin in range(0, plane, filters):
                out_ref[row : row + filters, begin : begin + filters] = refs[number][j, begin : begin + filters, :]
            row += filters


def pack(blocks, after=()):
    plane = blocks[0].shape[1]
    total = sum(block.size for block in blocks)
    return call(
        functools.partial(pack_body, len(blocks)),
        struct((total // plane, plane), blocks[0].dtype),
        (0, 4 * total),
        *blocks,
        in_specs=[VMEM] * len(blocks),
        after=after,
    )


def taps(weight_ref, number):
    block = weight_ref[pl.ds(9 * number, 9)]
    return block.reshape(block.shape[0] * block.shape[1], block.shape[2])


def forward_own_body(planes, volume_ref, other_ref, weight_ref, out_ref, acc_ref):
    for a in (0, 1, -1):
        weight = taps(weight_ref, a + 1)
        for j in range(planes):
            if 0 <= j + a < planes:
                product = dot(weight, volume_ref[j + a])
                acc_ref[j] = product if a == 0 else acc_ref[j] + product
    up, last = core(), planes - 1
    place = (1 - up) * last
    acc_ref[place] = acc_ref[place] + dot(taps(weight_ref, 2 * (1 - up)), other_ref[up * last])
    for j in range(planes):
        out_ref[j] = fold_shifts(acc_ref.at[j])


def forward_own(volume, other, weight, after=()):
    planes, channels, plane = volume.shape
    filters = weight.shape[1]
    return call(
        functools.partial(forward_own_body, planes),
        struct((planes, filters, plane), jnp.float32),
        (2 * 9 * filters * channels * plane * (3 * planes - 1), weight.size * 2),
        volume, other, weight,
        in_specs=[VMEM] * 3,
        scratch_shapes=[pltpu.VMEM((planes, 9 * filters, plane), jnp.float32)],
        after=after,
    )


def silu_and_slope(values):
    sig = 1.0 / (1.0 + jnp.exp(-values))
    return values * sig, sig * (1.0 + values * (1.0 - sig))


def forward_rest_body(planes, beyond_ref, weight_ref, own_ref, *refs):
    head_ref = refs[0] if len(refs) == 5 else None
    slope_ref, made_ref, acc_ref, total_ref = refs[-4:]
    up = core()
    place = up * (planes - 1)
    total_ref[...] = own_ref[...]
    acc_ref[...] = dot(taps(weight_ref, 2 * up), beyond_ref[0])
    total_ref[place] = total_ref[place] + fold_shifts(acc_ref)
    for j in range(planes):
        value, slope = silu_and_slope(total_ref[j])
        value = value.astype(jnp.bfloat16)
        slope_ref[j] = slope.T if head_ref is None else slope
        made_ref[j] = value if head_ref is None else dot(head_ref[...], value)


def forward_rest(beyond, weight, own, after, head=None):
    planes, filters, plane = own.shape
    channels = weight.shape[2]
    ins = [beyond, weight, own]
    slope = own.shape
    if head is None:
        slope = (planes, plane, filters)
        made = struct(own.shape, jnp.bfloat16)
    else:
        ins.append(head)
        made = struct((planes, head.shape[0], plane), jnp.float32)
    return call(
        functools.partial(forward_rest_body, planes),
        [struct(slope, jnp.float32), made],
        (2 * 9 * filters * channels * plane, weight.size * 2 // 3),
        *ins,
        in_specs=[VMEM] * len(ins),
        scratch_shapes=[
            pltpu.VMEM((9 * filters, plane), jnp.float32),
            pltpu.VMEM(own.shape, jnp.float32),
        ],
        after=after,
    )


def loss_body(count, labels_ref, head_ref, slope_ref, *refs):
    parts, grad_ref = refs[:count], refs[count]
    for j in range(grad_ref.shape[0]):
        logits = parts[0][j]
        for part in parts[1:]:
            logits = logits + part[j]
        powers = jnp.exp(logits)
        likely = powers / jnp.sum(powers, axis=0, keepdims=True)
        classes = lax.broadcasted_iota(jnp.int32, logits.shape, 0)
        onehot = (labels_ref[j : j + 1, :] == classes).astype(jnp.float32)
        logit_grad = (likely - onehot).astype(jnp.bfloat16).astype(jnp.float32)
        back = lax.dot_general(
            head_ref[...].astype(jnp.float32),
            logit_grad,
            (((0,), (0,)), ((), ())),
            preferred_element_type=jnp.float32,
        )
        grad_ref[j] = (back * slope_ref[j]).T.astype(jnp.bfloat16)


def loss_grad(parts, labels, head, slope, after):
    planes, plane = labels.shape
    return call(
        functools.partial(loss_body, len(parts)),
        struct((planes, plane, slope.shape[1]), jnp.bfloat16),
        (2 * slope.size * head.shape[0], slope.size * 6),
        labels, head, slope, *parts,
        in_specs=[VMEM] * (3 + len(parts)),
        after=after,
    )


def spread_back(grad, spread_ref):
    filters = grad.shape[1]
    turned = grad.astype(jnp.float32)
    for number, (b, e) in enumerate(SHIFTS):
        moved = shifted(turned, 0, -b, -e).astype(jnp.bfloat16)
        spread_ref[:, number * filters : (number + 1) * filters] = moved


def backward_own_body(planes, grad_ref, other_ref, weight_ref, out_ref, spread_ref):
    up, last = core(), planes - 1
    for j in range(planes):
        spread_back(grad_ref[j], spread_ref.at[j])
    spread_back(other_ref[up * last], spread_ref.at[planes])
    for a in (0, 1, -1):
        weight = taps(weight_ref, a + 1)
        for j in range(planes):
            if 0 <= j - a < planes:
                product = dot(spread_ref[j - a], weight)
                out_ref[j] = product if a == 0 else out_ref[j] + product
    place = (1 - up) * last
    out_ref[place] = out_ref[place] + dot(spread_ref[planes], taps(weight_ref, 2 * up))


def backward_own(grad, other, weight, after=()):
    planes, plane, filters = grad.shape
    channels = weight.shape[2]
    return call(
        functools.partial(backward_own_body, planes),
        struct((planes, plane, channels), jnp.float32),
        (2 * 9 * filters * channels * plane * (3 * planes - 1), weight.size * 2),
        grad, other, weight,
        in_specs=[VMEM] * 3,
        scratch_shapes=[pltpu.VMEM((planes + 1, plane, 9 * filters), jnp.bfloat16)],
        after=after,
    )


def near_steps(chips):
    return [step for step in range(1, chips) if step & (step + 1) == 0]


def backward_rest_body(planes, count, chips, steps, other_ref, weight_ref, own_ref, *refs):
    near, refs = refs[: len(steps)], refs[len(steps) :]
    copy_ref, kept_ref, sent = refs[0], refs[1], refs[2 : 1 + count]
    edge_ref, spread_ref, total_ref = refs[1 + count :]
    copy_ref[...] = other_ref[...]
    size = kept_ref.shape[2]
    up, me, chip = core(), here("filt"), here("slab") // 2
    place = up * (planes - 1)
    beyond = chip + 2 * up - 1
    edge_ref[...] = jnp.zeros_like(edge_ref)
    for number, step in enumerate(steps):

        @pl.when((beyond >= 0) & (beyond < chips) & (chip ^ beyond == step))
        def _():
            edge_ref[...] = near[number][(1 - up) * (planes - 1)]

    spread_back(edge_ref[...], spread_ref)
    product = dot(spread_ref[...], taps(weight_ref, 2 * (1 - up)))
    for block in range(count):
        columns = slice(block * size, (block + 1) * size)
        for j in range(planes):
            total_ref[block, j] = own_ref[j, :, columns]
        total_ref[block, place] = total_ref[block, place] + product[:, columns]
    kept_ref[...] = total_ref[me]
    for number in range(1, count):
        sent[number - 1][...] = total_ref[me ^ number].astype(jnp.bfloat16)


def backward_rest(other, far, weight, own, count, after):
    planes, plane, channels = own.shape
    filters = weight.shape[1]
    size = channels // count
    chips = lax.axis_size("slab") // 2
    outs = [struct(other.shape, other.dtype), struct((planes, plane, size), jnp.float32)]
    outs += [struct((planes, plane, size), jnp.bfloat16)] * (count - 1)
    return call(
        functools.partial(backward_rest_body, planes, count, chips, near_steps(chips)),
        outs,
        (2 * 9 * filters * channels * plane, weight.size * 2 // 3),
        other, weight, own, *far,
        in_specs=[VMEM] * (3 + len(far)),
        scratch_shapes=[
            pltpu.VMEM((plane, filters), jnp.bfloat16),
            pltpu.VMEM((plane, 9 * filters), jnp.bfloat16),
            pltpu.VMEM((count, planes, plane, size), jnp.float32),
        ],
        after=after,
    )


def first_grad_body(count, slope_ref, *refs):
    parts, out_ref = refs[:count], refs[count]
    for j in range(out_ref.shape[0]):
        total = parts[0][j]
        for part in parts[1:]:
            total = total + part[j].astype(jnp.float32)
        out_ref[j] = (total * slope_ref[j]).astype(jnp.bfloat16)


def first_out(parts, slope, after):
    return call(
        functools.partial(first_grad_body, len(parts)),
        struct(slope.shape, jnp.bfloat16),
        (slope.size * 4, slope.size * 14),
        slope, *parts,
        in_specs=[VMEM] * (1 + len(parts)),
        after=after,
    )


def spread_body(split, *refs):
    spread_ref, token_ref = refs[split:]
    token_ref[...] = jnp.zeros_like(token_ref)
    depth, rows, plane = refs[0].shape
    me = lax.rem(here("filt"), split)
    for d in range(depth):
        for half in range(split):
            values = refs[half][d].astype(jnp.float32)
            for number, (b, e) in enumerate(SHIFTS):
                begin = (number * split + (me ^ half)) * rows
                moved = shifted(values, 1, b, e).astype(jnp.bfloat16)
                spread_ref[pl.ds(pl.multiple_of(begin, rows), rows), d * plane : (d + 1) * plane] = moved


def spread(halved):
    split = len(halved)
    depth, rows, plane = halved[0].shape
    channels = split * rows
    return call(
        functools.partial(spread_body, split),
        [struct((9 * channels, depth * plane), jnp.bfloat16), TOKEN],
        (9 * channels * depth * plane, 10 * channels * depth * plane),
        *halved,
        in_specs=[VMEM] * split,
    )


def weight_grad_body(count, second, spread_ref, crossed_ref, *refs):
    parts, (out_ref, token_ref, grad_ref) = refs[:count], refs[count:]
    token_ref[...] = jnp.zeros_like(token_ref)
    planes, plane, filters = parts[0].shape
    channels = spread_ref.shape[0] // 9
    depth = spread_ref.shape[1] // plane
    zero = jnp.zeros((plane, filters), jnp.bfloat16)
    grad_ref[depth * plane : (depth + 1) * plane, : filters] = zero
    grad_ref[plane : 2 * plane, 2 * filters :] = zero

    def one(block, d, begin):
        rows = block.shape[0]
        for a in (-1, 0, 1):
            place = pl.ds(pl.multiple_of((d + a + 1) * plane + begin, rows), rows)
            grad_ref[place, (a + 1) * filters : (a + 2) * filters] = block

    near, far = far_owners(0), far_owners(1)
    owners = [near[0], far[0], *far[1:], *near[1:]] if second else near + far
    row = 0
    for number in range(count):
        for j in range(planes):
            one(parts[number][j], owners[number] * planes + j, 0)
    for number in range(count, len(owners)):
        for j in range(planes):
            for begin in range(0, plane, filters):
                block = crossed_ref[row : row + filters, begin : begin + filters]
                one(block, owners[number] * planes + j, begin)
            row += filters

    product = dot(spread_ref[...], grad_ref[plane : (depth + 1) * plane, :])
    for r in range(3):
        for number in range(9):
            out_ref[r * 9 + number] = product[
                number * channels : (number + 1) * channels, r * filters : (r + 1) * filters
            ]


def weight_grad(spreads, blocks, crossed, second):
    channels, columns = spreads.shape[0] // 9, spreads.shape[1]
    _, plane, filters = blocks[0].shape
    return call(
        functools.partial(weight_grad_body, len(blocks), second),
        [struct((27, channels, filters), jnp.float32), TOKEN],
        (2 * 27 * filters * channels * columns, 27 * channels * filters * 4 + spreads.size * 2),
        spreads, crossed, *blocks,
        in_specs=[VMEM] * (2 + len(blocks)),
        scratch_shapes=[pltpu.VMEM((columns + 2 * plane, 3 * filters), jnp.bfloat16)],
    )


def shards(features, first_weight, second_weight, head_weight, labels):
    count = lax.axis_size("filt")
    chips = lax.axis_size("slab") // 2
    split = halves(features.shape[1] * count // lax.axis_size("slab"))
    near, first_weight, head_weight = stage(features, first_weight, head_weight)
    all_in, share_in = assemble([near] + exchanged(features, "filt")[1:])
    other, beyond = halo(all_in)
    share_in = [share_in[0]] + chips_apart(share_in[1:])
    own = forward_own(all_in, other, first_weight)
    slope_first, hidden = forward_rest(beyond, first_weight, own, share_in[1:])

    halved_in = collected(share_in, [hidden])
    all_hidden, share_hidden = assemble(exchanged(hidden, "filt"), [halved_in])
    other, beyond = halo(all_hidden)
    share_hidden = [share_hidden[0]] + chips_apart(share_hidden[1:])
    halved_in = both_halves(halved_in, split)
    own = forward_own(all_hidden, other, second_weight)
    due = share_hidden[1:] + halved_in
    slope_second, logits = forward_rest(beyond, second_weight, own, due, head_weight)

    halved_hidden = both_halves(collected(share_hidden, [logits]), split)
    second_out = loss_grad(exchanged(logits, "filt"), labels, head_weight, slope_second, halved_hidden[:1])
    second_other = swap(second_out, "slab", 1)
    near = {step: swap(second_other, "slab", 2 * step) for step in near_steps(chips)}
    own = backward_own(second_out, second_other, second_weight)
    passed, kept, *sent = backward_rest(second_other, list(near.values()), second_weight, own, count, halved_hidden)
    parts = [kept] + [swap(part, "filt", 1 + number) for number, part in enumerate(sent)]
    second_far = [near[step] if step in near else swap(passed, "slab", 2 * step) for step in range(1, chips)]
    spread_in, token_in = spread(halved_in)
    spread_hidden, token_hidden = spread(halved_hidden)
    first_out_grad = first_out(parts, slope_first, [token_in, token_hidden, *second_far])

    first_blocks = [first_out_grad] + chips_apart([first_out_grad] * (chips - 1))
    crossed = swap(pack(second_far, [first_out_grad]), "slab", 1)
    second_grad, token = weight_grad(spread_hidden, [second_out, second_other] + second_far, crossed, True)
    crossed = swap(pack(first_blocks, [token]), "slab", 1)
    first_grad, _ = weight_grad(spread_in, first_blocks, crossed, False)
    return jnp.transpose(first_grad, (0, 2, 1)), jnp.transpose(second_grad, (0, 2, 1))


def solution(mesh):
    placed = (
        P("slab", "filt", None),
        P(None, "filt", None),
        P(None, "filt", None),
        P(None, "filt"),
        P("slab", None),
    )
    return jax.shard_map(
        shards,
        mesh=mesh,
        in_specs=placed,
        out_specs=(P(None, "filt", "slab"), P(None, "filt", "slab")),
        check_vma=False,
    )
```

```python
import functools

import jax
import jax.numpy as jnp
from jax import lax
from jax.experimental import pallas as pl
from jax.experimental.pallas import tpu as pltpu
from jax.sharding import PartitionSpec as P

WIDTH = 8
SHIFTS = [(b, e) for b in (-1, 0, 1) for e in (-1, 0, 1)]
LIMIT = 20 * 1024 * 1024
VMEM = pl.BlockSpec(memory_space=pltpu.VMEM)
ANY = pl.BlockSpec(memory_space=pl.ANY)


def swap(block, axis, step):
    count = lax.axis_size(axis)
    return lax.ppermute(block, axis, [(i, i ^ step) for i in range(count)])


def exchanged(block, axis):
    return [block] + [swap(block, axis, step) for step in range(1, lax.axis_size(axis))]


def halo(volume):
    count = lax.axis_size("slab")
    other = swap(volume, "slab", 1)
    passed = edge(other)
    pairs = [(i, i + 2) for i in range(0, count - 2, 2)] + [(i, i - 2) for i in range(3, count, 2)]
    return other, lax.ppermute(passed, "slab", pairs)


def chips_apart(blocks):
    return [swap(block, "slab", 2 + 2 * number) for number, block in enumerate(blocks)]


def every_chip(block):
    blocks = [block]
    for step in range(1, lax.axis_size("slab") // 2):
        low = step & -step
        blocks.append(swap(blocks[step ^ low], "slab", 2 * low))
    return blocks


def call(body, out_shape, cost, *operands, in_specs, scratch_shapes=(), passed=(), after=()):
    flops, moved = cost
    single = not isinstance(out_shape, list)
    outs = [out_shape] if single else out_shape
    first, second = len(operands), len(operands) + len(passed) + len(after)
    third = second + len(outs)

    def inner(*refs):
        body(*refs[:first], *refs[second:third], *refs[third + len(passed) :])

    given = pl.pallas_call(
        inner,
        out_shape=[*outs, *(struct(array.shape, array.dtype) for array in passed)],
        cost_estimate=pl.CostEstimate(flops=flops, bytes_accessed=moved, transcendentals=0),
        compiler_params=pltpu.CompilerParams(vmem_limit_bytes=LIMIT),
        in_specs=[*in_specs] + [ANY] * (len(passed) + len(after)),
        out_specs=[VMEM] * len(outs) + [ANY] * len(passed),
        scratch_shapes=list(scratch_shapes),
        input_output_aliases={first + i: len(outs) + i for i in range(len(passed))},
    )(*operands, *passed, *after)
    if passed:
        return [*given[: len(outs)], list(given[len(outs) :])]
    return given[0] if single else list(given)


def struct(shape, dtype):
    return jax.ShapeDtypeStruct(tuple(shape), dtype)


def here(axis):
    return lax.axis_index(axis).astype(jnp.int32)


def core():
    return lax.rem(here("slab"), 2)


def far_owners(side):
    me = here("slab")
    return [me ^ (2 * step) ^ side for step in range(lax.axis_size("slab") // 2)]


TOKEN = struct((8, 128), jnp.float32)


def stage_body(count, *refs):
    sources, targets, sems = refs[:count], refs[count : 2 * count], refs[2 * count]
    copies = [pltpu.make_async_copy(sources[i], targets[i], sems.at[i]) for i in range(count)]
    for copy in copies:
        copy.start()
    for copy in copies:
        copy.wait()


def stage(*arrays):
    count = len(arrays)
    return call(
        functools.partial(stage_body, count),
        [struct(array.shape, array.dtype) for array in arrays],
        (0, sum(4 * array.size for array in arrays)),
        *arrays,
        in_specs=[pl.BlockSpec(memory_space=pltpu.HBM)] * count,
        scratch_shapes=[pltpu.SemaphoreType.DMA((count,))],
    )


def inside(shape, axis, b, e):
    spot = lax.broadcasted_iota(jnp.int32, shape, axis)
    column = spot % WIDTH + e
    moved = spot + WIDTH * b
    return (column >= 0) & (column < WIDTH) & (moved >= 0) & (moved < shape[axis])


def shifted(values, axis, b, e):
    if b == 0 and e == 0:
        return values
    size = values.shape[axis]
    turned = pltpu.roll(values, (-(WIDTH * b + e)) % size, axis)
    return jnp.where(inside(values.shape, axis, b, e), turned, 0.0)


def fold_shifts(products):
    rows = products.shape[0] // len(SHIFTS)
    total = None
    for number, (b, e) in enumerate(SHIFTS):
        term = shifted(products[number * rows : (number + 1) * rows, :], 1, b, e)
        total = term if total is None else total + term
    return total


def dot(left, right):
    return jnp.dot(left, right, preferred_element_type=jnp.float32)


def edge_body(other_ref, out_ref):
    out_ref[0] = other_ref[(1 - core()) * (other_ref.shape[0] - 1)]


def edge(other):
    shape = (1, *other.shape[1:])
    return call(edge_body, struct(shape, other.dtype), (0, other.size), other, in_specs=[VMEM])


def halves(rows):
    return 2 if rows % 32 == 0 and lax.axis_size("filt") % 2 == 0 else 1


def assemble_body(count, split, *refs):
    parts, whole_ref, shares = refs[:count], refs[count], refs[count + 1 :]
    size = parts[0].shape[1]
    me, chip = here("filt"), here("slab") // 2
    for step in range(count):
        place = pl.ds(pl.multiple_of((me ^ step) * size, size), size)
        whole_ref[:, place, :] = parts[step][...]
    rows = shares[0].shape[2]
    for step, share_ref in enumerate(shares):
        for side in range(2):
            begin = (((chip ^ step) * 2 + side) * split + lax.rem(me, split)) * rows
            share_ref[side] = whole_ref[:, pl.ds(pl.multiple_of(begin, rows), rows), :]


def assemble(parts, after=()):
    planes, size, plane = parts[0].shape
    count, slabs = len(parts), lax.axis_size("slab")
    channels = size * count
    split = halves(channels // slabs)
    kind = parts[0].dtype
    outs = [struct((planes, channels, plane), kind)]
    outs += [struct((2, planes, channels // slabs // split, plane), kind)] * (slabs // 2)
    whole, *shares = call(
        functools.partial(assemble_body, count, split),
        outs,
        (0, 4 * planes * channels * plane),
        *parts,
        in_specs=[VMEM] * count,
        after=after,
    )
    return whole, shares


def crossing_body(count, *refs):
    planes = refs[0].shape[1]
    for step in range(count):
        for j in range(planes):
            refs[count][step * planes + j] = refs[step][1 - core(), j]


def collect_body(count, crossed_ref, *refs):
    owners, side = far_owners(0), core()
    planes = refs[0].shape[1]
    for step in range(count):
        for j in range(planes):
            refs[count][owners[step] * planes + j] = refs[step][side, j]
            refs[count][(owners[step] ^ 1) * planes + j] = crossed_ref[step * planes + j]


def collected(shares, after=()):
    count = len(shares)
    _, planes, rows, plane = shares[0].shape
    kind, size = shares[0].dtype, shares[0].size * count
    crossing = call(
        functools.partial(crossing_body, count),
        struct((count * planes, rows, plane), kind),
        (0, 2 * size),
        *shares,
        in_specs=[VMEM] * count,
        after=after,
    )
    return call(
        functools.partial(collect_body, count),
        struct((2 * count * planes, rows, plane), kind),
        (0, 4 * size),
        swap(crossing, "slab", 1), *shares,
        in_specs=[VMEM] * (1 + count),
    )


def both_halves(volume, split):
    return [volume] + ([swap(volume, "filt", 1)] if split == 2 else [])


def pack_body(count, *refs):
    out_ref = refs[count]
    row = 0
    for number in range(count):
        planes, plane, filters = refs[number].shape
        for j in range(planes):
            for begin in range(0, plane, filters):
                out_ref[row : row + filters, begin : begin + filters] = refs[number][j, begin : begin + filters, :]
            row += filters


def pack(blocks, after=()):
    plane = blocks[0].shape[1]
    total = sum(block.size for block in blocks)
    return call(
        functools.partial(pack_body, len(blocks)),
        struct((total // plane, plane), blocks[0].dtype),
        (0, 4 * total),
        *blocks,
        in_specs=[VMEM] * len(blocks),
        after=after,
    )


def taps(weight_ref, number):
    block = weight_ref[pl.ds(9 * number, 9)]
    return block.reshape(block.shape[0] * block.shape[1], block.shape[2])


def forward_own_body(planes, volume_ref, other_ref, weight_ref, out_ref, acc_ref):
    for a in (0, 1, -1):
        weight = taps(weight_ref, a + 1)
        for j in range(planes):
            if 0 <= j + a < planes:
                product = dot(weight, volume_ref[j + a])
                acc_ref[j] = product if a == 0 else acc_ref[j] + product
    up, last = core(), planes - 1
    place = (1 - up) * last
    acc_ref[place] = acc_ref[place] + dot(taps(weight_ref, 2 * (1 - up)), other_ref[up * last])
    for j in range(planes):
        out_ref[j] = fold_shifts(acc_ref.at[j])


def forward_own(volume, other, weight, after=()):
    planes, channels, plane = volume.shape
    filters = weight.shape[1]
    return call(
        functools.partial(forward_own_body, planes),
        struct((planes, filters, plane), jnp.float32),
        (2 * 9 * filters * channels * plane * (3 * planes - 1), weight.size * 2),
        volume, other, weight,
        in_specs=[VMEM] * 3,
        scratch_shapes=[pltpu.VMEM((planes, 9 * filters, plane), jnp.float32)],
        after=after,
    )


def silu_and_slope(values):
    sig = 1.0 / (1.0 + jnp.exp(-values))
    return values * sig, sig * (1.0 + values * (1.0 - sig))


def forward_rest_body(planes, beyond_ref, weight_ref, own_ref, *refs):
    head_ref = refs[0] if len(refs) == 5 else None
    slope_ref, made_ref, acc_ref, total_ref = refs[-4:]
    up = core()
    place = up * (planes - 1)
    total_ref[...] = own_ref[...]
    acc_ref[...] = dot(taps(weight_ref, 2 * up), beyond_ref[0])
    total_ref[place] = total_ref[place] + fold_shifts(acc_ref)
    for j in range(planes):
        value, slope = silu_and_slope(total_ref[j])
        value = value.astype(jnp.bfloat16)
        slope_ref[j] = slope.T if head_ref is None else slope
        made_ref[j] = value if head_ref is None else dot(head_ref[...], value)


def forward_rest(beyond, weight, own, after, head=None):
    planes, filters, plane = own.shape
    channels = weight.shape[2]
    ins = [beyond, weight, own]
    slope = own.shape
    if head is None:
        slope = (planes, plane, filters)
        made = struct(own.shape, jnp.bfloat16)
    else:
        ins.append(head)
        made = struct((planes, head.shape[0], plane), jnp.float32)
    return call(
        functools.partial(forward_rest_body, planes),
        [struct(slope, jnp.float32), made],
        (2 * 9 * filters * channels * plane, weight.size * 2 // 3),
        *ins,
        in_specs=[VMEM] * len(ins),
        scratch_shapes=[
            pltpu.VMEM((9 * filters, plane), jnp.float32),
            pltpu.VMEM(own.shape, jnp.float32),
        ],
        after=after,
    )


def add_body(left_ref, right_ref, out_ref):
    out_ref[...] = left_ref[...] + right_ref[...]


def butterfly(term, axis):
    count = lax.axis_size(axis)
    terms = [term]
    step = 1
    while step < count:
        if len(terms) == 2:
            shape = struct(term.shape, term.dtype)
            terms = [call(add_body, shape, (term.size, 12 * term.size), *terms, in_specs=[VMEM] * 2)]
        terms = [terms[0], swap(terms[0], axis, step)]
        step *= 2
    return terms


def loss_body(count, labels_ref, head_ref, slope_ref, *refs):
    parts, grad_ref = refs[:count], refs[count]
    for j in range(grad_ref.shape[0]):
        logits = parts[0][j]
        for part in parts[1:]:
            logits = logits + part[j]
        powers = jnp.exp(logits)
        likely = powers / jnp.sum(powers, axis=0, keepdims=True)
        classes = lax.broadcasted_iota(jnp.int32, logits.shape, 0)
        onehot = (labels_ref[j : j + 1, :] == classes).astype(jnp.float32)
        logit_grad = (likely - onehot).astype(jnp.bfloat16).astype(jnp.float32)
        back = lax.dot_general(
            head_ref[...].astype(jnp.float32),
            logit_grad,
            (((0,), (0,)), ((), ())),
            preferred_element_type=jnp.float32,
        )
        grad_ref[j] = (back * slope_ref[j]).T.astype(jnp.bfloat16)


def loss_grad(parts, labels, head, slope, after):
    planes, plane = labels.shape
    return call(
        functools.partial(loss_body, len(parts)),
        struct((planes, plane, slope.shape[1]), jnp.bfloat16),
        (2 * slope.size * head.shape[0], slope.size * 6),
        labels, head, slope, *parts,
        in_specs=[VMEM] * (3 + len(parts)),
        after=after,
    )


def spread_back(grad, spread_ref):
    filters = grad.shape[1]
    turned = grad.astype(jnp.float32)
    for number, (b, e) in enumerate(SHIFTS):
        moved = shifted(turned, 0, -b, -e).astype(jnp.bfloat16)
        spread_ref[:, number * filters : (number + 1) * filters] = moved


def backward_own_body(planes, grad_ref, other_ref, weight_ref, out_ref, spread_ref):
    up, last = core(), planes - 1
    for j in range(planes):
        spread_back(grad_ref[j], spread_ref.at[j])
    spread_back(other_ref[up * last], spread_ref.at[planes])
    for a in (0, 1, -1):
        weight = taps(weight_ref, a + 1)
        for j in range(planes):
            if 0 <= j - a < planes:
                product = dot(spread_ref[j - a], weight)
                out_ref[j] = product if a == 0 else out_ref[j] + product
    place = (1 - up) * last
    out_ref[place] = out_ref[place] + dot(spread_ref[planes], taps(weight_ref, 2 * up))


def backward_own(grad, other, weight, after=()):
    planes, plane, filters = grad.shape
    channels = weight.shape[2]
    return call(
        functools.partial(backward_own_body, planes),
        struct((planes, plane, channels), jnp.float32),
        (2 * 9 * filters * channels * plane * (3 * planes - 1), weight.size * 2),
        grad, other, weight,
        in_specs=[VMEM] * 3,
        scratch_shapes=[pltpu.VMEM((planes + 1, plane, 9 * filters), jnp.bfloat16)],
        after=after,
    )


def backward_rest_body(planes, count, beyond_ref, weight_ref, own_ref, *refs):
    kept_ref, sent, (spread_ref, total_ref) = refs[0], refs[1:count], refs[count:]
    size = kept_ref.shape[2]
    up, me = core(), here("filt")
    place = up * (planes - 1)
    spread_back(beyond_ref[0], spread_ref)
    product = dot(spread_ref[...], taps(weight_ref, 2 * (1 - up)))
    for block in range(count):
        columns = slice(block * size, (block + 1) * size)
        for j in range(planes):
            total_ref[block, j] = own_ref[j, :, columns]
        total_ref[block, place] = total_ref[block, place] + product[:, columns]
    kept_ref[...] = total_ref[me]
    for number in range(1, count):
        sent[number - 1][...] = total_ref[me ^ number].astype(jnp.bfloat16)


def backward_rest(beyond, weight, own, count, after):
    planes, plane, channels = own.shape
    filters = weight.shape[1]
    size = channels // count
    outs = [struct((planes, plane, size), jnp.float32)]
    outs += [struct((planes, plane, size), jnp.bfloat16)] * (count - 1)
    return call(
        functools.partial(backward_rest_body, planes, count),
        outs,
        (2 * 9 * filters * channels * plane, weight.size * 2 // 3),
        beyond, weight, own,
        in_specs=[VMEM] * 3,
        scratch_shapes=[
            pltpu.VMEM((plane, 9 * filters), jnp.bfloat16),
            pltpu.VMEM((count, planes, plane, size), jnp.float32),
        ],
        after=after,
    )


def first_grad_body(count, slope_ref, *refs):
    parts, out_ref = refs[:count], refs[count]
    for j in range(out_ref.shape[0]):
        total = parts[0][j]
        for part in parts[1:]:
            total = total + part[j].astype(jnp.float32)
        out_ref[j] = (total * slope_ref[j]).astype(jnp.bfloat16)


def first_out(parts, slope, after):
    return call(
        functools.partial(first_grad_body, len(parts)),
        struct(slope.shape, jnp.bfloat16),
        (slope.size * 4, slope.size * 14),
        slope, *parts,
        in_specs=[VMEM] * (1 + len(parts)),
        after=after,
    )


def spread_body(split, *refs):
    spread_ref, token_ref = refs[split:]
    token_ref[...] = jnp.zeros_like(token_ref)
    depth, rows, plane = refs[0].shape
    me = lax.rem(here("filt"), split)
    for d in range(depth):
        for half in range(split):
            values = refs[half][d].astype(jnp.float32)
            for number, (b, e) in enumerate(SHIFTS):
                begin = (number * split + (me ^ half)) * rows
                moved = shifted(values, 1, b, e).astype(jnp.bfloat16)
                spread_ref[pl.ds(pl.multiple_of(begin, rows), rows), d * plane : (d + 1) * plane] = moved


def spread(halved):
    split = len(halved)
    depth, rows, plane = halved[0].shape
    channels = split * rows
    return call(
        functools.partial(spread_body, split),
        [struct((9 * channels, depth * plane), jnp.bfloat16), TOKEN],
        (9 * channels * depth * plane, 10 * channels * depth * plane),
        *halved,
        in_specs=[VMEM] * split,
    )


def weight_grad_body(count, second, spread_ref, crossed_ref, *refs):
    parts, (out_ref, token_ref, grad_ref) = refs[:count], refs[count:]
    token_ref[...] = jnp.zeros_like(token_ref)
    planes, plane, filters = parts[0].shape
    channels = spread_ref.shape[0] // 9
    depth = spread_ref.shape[1] // plane
    zero = jnp.zeros((plane, filters), jnp.bfloat16)
    grad_ref[depth * plane : (depth + 1) * plane, : filters] = zero
    grad_ref[plane : 2 * plane, 2 * filters :] = zero

    def one(block, d, begin):
        rows = block.shape[0]
        for a in (-1, 0, 1):
            place = pl.ds(pl.multiple_of((d + a + 1) * plane + begin, rows), rows)
            grad_ref[place, (a + 1) * filters : (a + 2) * filters] = block

    near, far = far_owners(0), far_owners(1)
    owners = [near[0], far[0], *near[1:], *far[1:]] if second else near + far
    row = 0
    for number in range(count):
        for j in range(planes):
            one(parts[number][j], owners[number] * planes + j, 0)
    for number in range(count, len(owners)):
        for j in range(planes):
            for begin in range(0, plane, filters):
                block = crossed_ref[row : row + filters, begin : begin + filters]
                one(block, owners[number] * planes + j, begin)
            row += filters

    product = dot(spread_ref[...], grad_ref[plane : (depth + 1) * plane, :])
    for r in range(3):
        for number in range(9):
            out_ref[r * 9 + number] = product[
                number * channels : (number + 1) * channels, r * filters : (r + 1) * filters
            ]


def weight_grad(spreads, blocks, crossed, second):
    channels, columns = spreads.shape[0] // 9, spreads.shape[1]
    _, plane, filters = blocks[0].shape
    return call(
        functools.partial(weight_grad_body, len(blocks), second),
        [struct((27, channels, filters), jnp.float32), TOKEN],
        (2 * 27 * filters * channels * columns, 27 * channels * filters * 4 + spreads.size * 2),
        spreads, crossed, *blocks,
        in_specs=[VMEM] * (2 + len(blocks)),
        scratch_shapes=[pltpu.VMEM((columns + 2 * plane, 3 * filters), jnp.bfloat16)],
    )


def shards(features, first_weight, second_weight, head_weight, labels):
    count = lax.axis_size("filt")
    chips = lax.axis_size("slab") // 2
    split = halves(features.shape[1] * count // lax.axis_size("slab"))
    near, first_weight, head_weight = stage(features, first_weight, head_weight)
    all_in, share_in = assemble([near] + exchanged(features, "filt")[1:])
    other, beyond = halo(all_in)
    share_in = [share_in[0]] + chips_apart(share_in[1:])
    own = forward_own(all_in, other, first_weight)
    slope_first, hidden = forward_rest(beyond, first_weight, own, share_in[1:])

    halved_in = collected(share_in, [hidden])
    all_hidden, share_hidden = assemble(exchanged(hidden, "filt"), [halved_in])
    other, beyond = halo(all_hidden)
    share_hidden = [share_hidden[0]] + chips_apart(share_hidden[1:])
    halved_in = both_halves(halved_in, split)
    own = forward_own(all_hidden, other, second_weight)
    due = share_hidden[1:] + halved_in
    slope_second, logits = forward_rest(beyond, second_weight, own, due, head_weight)

    halved_hidden = both_halves(collected(share_hidden, [logits]), split)
    second_out = loss_grad(butterfly(logits, "filt"), labels, head_weight, slope_second, halved_hidden[:1])
    second_other, beyond = halo(second_out)
    second_far = every_chip(second_out)[1:]
    own = backward_own(second_out, second_other, second_weight)
    due = halved_hidden + second_far[chips // 2 - 1 : chips // 2]
    kept, *sent = backward_rest(beyond, second_weight, own, count, due)
    parts = [kept] + [swap(part, "filt", 1 + number) for number, part in enumerate(sent)]
    spread_in, token_in = spread(halved_in)
    spread_hidden, token_hidden = spread(halved_hidden)
    first_out_grad = first_out(parts, slope_first, [token_in, token_hidden, *second_far])

    first_blocks = every_chip(first_out_grad)
    crossed = swap(pack(second_far, [first_out_grad]), "slab", 1)
    second_grad, token = weight_grad(spread_hidden, [second_out, second_other] + second_far, crossed, True)
    crossed = swap(pack(first_blocks, [token]), "slab", 1)
    first_grad, _ = weight_grad(spread_in, first_blocks, crossed, False)
    return jnp.transpose(first_grad, (0, 2, 1)), jnp.transpose(second_grad, (0, 2, 1))


def solution(mesh):
    placed = (
        P("slab", "filt", None),
        P(None, "filt", None),
        P(None, "filt", None),
        P(None, "filt"),
        P("slab", None),
    )
    return jax.shard_map(
        shards,
        mesh=mesh,
        in_specs=placed,
        out_specs=(P(None, "filt", "slab"), P(None, "filt", "slab")),
        check_vma=False,
    )
```

```python
import functools

import jax
import jax.numpy as jnp
from jax import lax
from jax.experimental import pallas as pl
from jax.experimental.pallas import tpu as pltpu
from jax.sharding import PartitionSpec as P

WIDTH = 8
SHIFTS = [(b, e) for b in (-1, 0, 1) for e in (-1, 0, 1)]
LIMIT = 20 * 1024 * 1024
VMEM = pl.BlockSpec(memory_space=pltpu.VMEM)
ANY = pl.BlockSpec(memory_space=pl.ANY)


def swap(block, axis, step):
    count = lax.axis_size(axis)
    return lax.ppermute(block, axis, [(i, i ^ step) for i in range(count)])


def exchanged(block, axis):
    return [block] + [swap(block, axis, step) for step in range(1, lax.axis_size(axis))]


def halo(volume, own):
    count = lax.axis_size("slab")
    other = swap(volume, "slab", 1)
    passed = edge(other, own)
    pairs = [(i, i + 2) for i in range(0, count - 2, 2)] + [(i, i - 2) for i in range(3, count, 2)]
    return other, lax.ppermute(passed, "slab", pairs)


def chips_apart(blocks):
    return [swap(block, "slab", 2 + 2 * number) for number, block in enumerate(blocks)]


def every_chip(block):
    blocks = [block]
    for step in range(1, lax.axis_size("slab") // 2):
        low = step & -step
        blocks.append(swap(blocks[step ^ low], "slab", 2 * low))
    return blocks


def call(body, out_shape, cost, *operands, in_specs, scratch_shapes=(), passed=(), after=()):
    flops, moved = cost
    single = not isinstance(out_shape, list)
    outs = [out_shape] if single else out_shape
    first, second = len(operands), len(operands) + len(passed) + len(after)
    third = second + len(outs)

    def inner(*refs):
        body(*refs[:first], *refs[second:third], *refs[third + len(passed) :])

    given = pl.pallas_call(
        inner,
        out_shape=[*outs, *(struct(array.shape, array.dtype) for array in passed)],
        cost_estimate=pl.CostEstimate(flops=flops, bytes_accessed=moved, transcendentals=0),
        compiler_params=pltpu.CompilerParams(vmem_limit_bytes=LIMIT),
        in_specs=[*in_specs] + [ANY] * (len(passed) + len(after)),
        out_specs=[VMEM] * len(outs) + [ANY] * len(passed),
        scratch_shapes=list(scratch_shapes),
        input_output_aliases={first + i: len(outs) + i for i in range(len(passed))},
    )(*operands, *passed, *after)
    if passed:
        return [*given[: len(outs)], list(given[len(outs) :])]
    return given[0] if single else list(given)


def struct(shape, dtype):
    return jax.ShapeDtypeStruct(tuple(shape), dtype)


def here(axis):
    return lax.axis_index(axis).astype(jnp.int32)


def core():
    return lax.rem(here("slab"), 2)


def far_owners(side):
    me = here("slab")
    return [me ^ (2 * step) ^ side for step in range(lax.axis_size("slab") // 2)]


TOKEN = struct((8, 128), jnp.float32)


def stage_body(count, *refs):
    sources, targets, sems = refs[:count], refs[count : 2 * count], refs[2 * count]
    copies = [pltpu.make_async_copy(sources[i], targets[i], sems.at[i]) for i in range(count)]
    for copy in copies:
        copy.start()
    for copy in copies:
        copy.wait()


def stage(*arrays):
    count = len(arrays)
    return call(
        functools.partial(stage_body, count),
        [struct(array.shape, array.dtype) for array in arrays],
        (0, sum(4 * array.size for array in arrays)),
        *arrays,
        in_specs=[pl.BlockSpec(memory_space=pltpu.HBM)] * count,
        scratch_shapes=[pltpu.SemaphoreType.DMA((count,))],
    )


def inside(shape, axis, b, e):
    spot = lax.broadcasted_iota(jnp.int32, shape, axis)
    column = spot % WIDTH + e
    moved = spot + WIDTH * b
    return (column >= 0) & (column < WIDTH) & (moved >= 0) & (moved < shape[axis])


def shifted(values, axis, b, e):
    if b == 0 and e == 0:
        return values
    size = values.shape[axis]
    turned = pltpu.roll(values, (-(WIDTH * b + e)) % size, axis)
    return jnp.where(inside(values.shape, axis, b, e), turned, 0.0)


def fold_shifts(products):
    rows = products.shape[0] // len(SHIFTS)
    total = None
    for number, (b, e) in enumerate(SHIFTS):
        term = shifted(products[number * rows : (number + 1) * rows, :], 1, b, e)
        total = term if total is None else total + term
    return total


def dot(left, right):
    return jnp.dot(left, right, preferred_element_type=jnp.float32)


def edge_body(other_ref, out_ref):
    out_ref[0] = other_ref[(1 - core()) * (other_ref.shape[0] - 1)]


def edge(other, own):
    shape = (1, *other.shape[1:])
    return call(edge_body, struct(shape, other.dtype), (0, other.size), other, in_specs=[VMEM], after=[own])


def halves(rows):
    return 2 if rows % 32 == 0 and lax.axis_size("filt") % 2 == 0 else 1


def assemble_body(count, split, *refs):
    parts, whole_ref, shares = refs[:count], refs[count], refs[count + 1 :]
    size = parts[0].shape[1]
    me, chip = here("filt"), here("slab") // 2
    for step in range(count):
        place = pl.ds(pl.multiple_of((me ^ step) * size, size), size)
        whole_ref[:, place, :] = parts[step][...]
    rows = shares[0].shape[2]
    for step, share_ref in enumerate(shares):
        for side in range(2):
            begin = (((chip ^ step) * 2 + side) * split + lax.rem(me, split)) * rows
            share_ref[side] = whole_ref[:, pl.ds(pl.multiple_of(begin, rows), rows), :]


def assemble(parts, after=()):
    planes, size, plane = parts[0].shape
    count, slabs = len(parts), lax.axis_size("slab")
    channels = size * count
    split = halves(channels // slabs)
    kind = parts[0].dtype
    outs = [struct((planes, channels, plane), kind)]
    outs += [struct((2, planes, channels // slabs // split, plane), kind)] * (slabs // 2)
    whole, *shares = call(
        functools.partial(assemble_body, count, split),
        outs,
        (0, 4 * planes * channels * plane),
        *parts,
        in_specs=[VMEM] * count,
        after=after,
    )
    return whole, shares


def crossing_body(count, *refs):
    planes = refs[0].shape[1]
    for step in range(count):
        for j in range(planes):
            refs[count][step * planes + j] = refs[step][1 - core(), j]


def collect_body(count, crossed_ref, *refs):
    owners, side = far_owners(0), core()
    planes = refs[0].shape[1]
    for step in range(count):
        for j in range(planes):
            refs[count][owners[step] * planes + j] = refs[step][side, j]
            refs[count][(owners[step] ^ 1) * planes + j] = crossed_ref[step * planes + j]


def collected(shares, after, later=()):
    count = len(shares)
    _, planes, rows, plane = shares[0].shape
    kind, size = shares[0].dtype, shares[0].size * count
    crossing = call(
        functools.partial(crossing_body, count),
        struct((count * planes, rows, plane), kind),
        (0, 2 * size),
        *shares,
        in_specs=[VMEM] * count,
        after=after,
    )
    return call(
        functools.partial(collect_body, count),
        struct((2 * count * planes, rows, plane), kind),
        (0, 4 * size),
        swap(crossing, "slab", 1), *shares,
        in_specs=[VMEM] * (1 + count),
        after=later,
    )


def both_halves(volume, split):
    return [volume] + ([swap(volume, "filt", 1)] if split == 2 else [])


def pack_body(count, *refs):
    out_ref = refs[count]
    row = 0
    for number in range(count):
        planes, plane, filters = refs[number].shape
        for j in range(planes):
            for begin in range(0, plane, filters):
                out_ref[row : row + filters, begin : begin + filters] = refs[number][j, begin : begin + filters, :]
            row += filters


def pack(blocks, after=()):
    plane = blocks[0].shape[1]
    total = sum(block.size for block in blocks)
    return call(
        functools.partial(pack_body, len(blocks)),
        struct((total // plane, plane), blocks[0].dtype),
        (0, 4 * total),
        *blocks,
        in_specs=[VMEM] * len(blocks),
        after=after,
    )


def taps(weight_ref, number):
    block = weight_ref[pl.ds(9 * number, 9)]
    return block.reshape(block.shape[0] * block.shape[1], block.shape[2])


def forward_own_body(planes, volume_ref, weight_ref, out_ref, acc_ref):
    for a in (0, 1, -1):
        weight = taps(weight_ref, a + 1)
        for j in range(planes):
            if 0 <= j + a < planes:
                product = dot(weight, volume_ref[j + a])
                acc_ref[j] = product if a == 0 else acc_ref[j] + product
    for j in range(planes):
        out_ref[j] = fold_shifts(acc_ref.at[j])


def forward_own(volume, weight):
    planes, channels, plane = volume.shape
    filters = weight.shape[1]
    return call(
        functools.partial(forward_own_body, planes),
        struct((planes, filters, plane), jnp.float32),
        (2 * 9 * filters * channels * plane * (3 * planes - 2), weight.size * 2),
        volume, weight,
        in_specs=[VMEM] * 2,
        scratch_shapes=[pltpu.VMEM((planes, 9 * filters, plane), jnp.float32)],
    )


def forward_other_body(planes, other_ref, weight_ref, own_ref, out_ref, acc_ref):
    up, last = core(), planes - 1
    place = (1 - up) * last
    acc_ref[...] = dot(taps(weight_ref, 2 * (1 - up)), other_ref[up * last])
    out_ref[...] = own_ref[...]
    out_ref[place] = out_ref[place] + fold_shifts(acc_ref)


def forward_other(other, weight, own, passed):
    planes, filters, plane = own.shape
    return call(
        functools.partial(forward_other_body, planes),
        [struct(own.shape, jnp.float32)],
        (2 * weight.size // 3 * plane, weight.size * 2 // 3),
        other, weight, own,
        in_specs=[VMEM] * 3,
        scratch_shapes=[pltpu.VMEM((9 * filters, plane), jnp.float32)],
        passed=passed,
    )


def silu_and_slope(values):
    sig = 1.0 / (1.0 + jnp.exp(-values))
    return values * sig, sig * (1.0 + values * (1.0 - sig))


def forward_rest_body(planes, beyond_ref, weight_ref, own_ref, *refs):
    head_ref = refs[0] if len(refs) == 5 else None
    slope_ref, made_ref, acc_ref, total_ref = refs[-4:]
    up = core()
    place = up * (planes - 1)
    total_ref[...] = own_ref[...]
    acc_ref[...] = dot(taps(weight_ref, 2 * up), beyond_ref[0])
    total_ref[place] = total_ref[place] + fold_shifts(acc_ref)
    for j in range(planes):
        value, slope = silu_and_slope(total_ref[j])
        value = value.astype(jnp.bfloat16)
        slope_ref[j] = slope.T if head_ref is None else slope
        made_ref[j] = value if head_ref is None else dot(head_ref[...], value)


def forward_rest(beyond, weight, own, after, head=None):
    planes, filters, plane = own.shape
    channels = weight.shape[2]
    ins = [beyond, weight, own]
    slope = own.shape
    if head is None:
        slope = (planes, plane, filters)
        made = struct(own.shape, jnp.bfloat16)
    else:
        ins.append(head)
        made = struct((planes, head.shape[0], plane), jnp.float32)
    return call(
        functools.partial(forward_rest_body, planes),
        [struct(slope, jnp.float32), made],
        (2 * 9 * filters * channels * plane, weight.size * 2 // 3),
        *ins,
        in_specs=[VMEM] * len(ins),
        scratch_shapes=[
            pltpu.VMEM((9 * filters, plane), jnp.float32),
            pltpu.VMEM(own.shape, jnp.float32),
        ],
        after=after,
    )


def loss_body(count, labels_ref, head_ref, slope_ref, *refs):
    parts, grad_ref = refs[:count], refs[count]
    for j in range(grad_ref.shape[0]):
        logits = parts[0][j]
        for part in parts[1:]:
            logits = logits + part[j]
        powers = jnp.exp(logits)
        likely = powers / jnp.sum(powers, axis=0, keepdims=True)
        classes = lax.broadcasted_iota(jnp.int32, logits.shape, 0)
        onehot = (labels_ref[j : j + 1, :] == classes).astype(jnp.float32)
        logit_grad = (likely - onehot).astype(jnp.bfloat16).astype(jnp.float32)
        back = lax.dot_general(
            head_ref[...].astype(jnp.float32),
            logit_grad,
            (((0,), (0,)), ((), ())),
            preferred_element_type=jnp.float32,
        )
        grad_ref[j] = (back * slope_ref[j]).T.astype(jnp.bfloat16)


def loss_grad(parts, labels, head, slope, after):
    planes, plane = labels.shape
    return call(
        functools.partial(loss_body, len(parts)),
        struct((planes, plane, slope.shape[1]), jnp.bfloat16),
        (2 * slope.size * head.shape[0], slope.size * 6),
        labels, head, slope, *parts,
        in_specs=[VMEM] * (3 + len(parts)),
        after=after,
    )


def spread_back(grad, spread_ref):
    filters = grad.shape[1]
    turned = grad.astype(jnp.float32)
    for number, (b, e) in enumerate(SHIFTS):
        moved = shifted(turned, 0, -b, -e).astype(jnp.bfloat16)
        spread_ref[:, number * filters : (number + 1) * filters] = moved


def backward_own_body(planes, grad_ref, weight_ref, out_ref, spread_ref):
    for j in range(planes):
        spread_back(grad_ref[j], spread_ref.at[j])
    for a in (0, 1, -1):
        weight = taps(weight_ref, a + 1)
        for j in range(planes):
            if 0 <= j - a < planes:
                product = dot(spread_ref[j - a], weight)
                out_ref[j] = product if a == 0 else out_ref[j] + product


def backward_own(grad, weight):
    planes, plane, filters = grad.shape
    channels = weight.shape[2]
    return call(
        functools.partial(backward_own_body, planes),
        struct((planes, plane, channels), jnp.float32),
        (2 * 9 * filters * channels * plane * (3 * planes - 2), weight.size * 2),
        grad, weight,
        in_specs=[VMEM] * 2,
        scratch_shapes=[pltpu.VMEM((planes, plane, 9 * filters), jnp.bfloat16)],
    )


def backward_other_body(planes, other_ref, weight_ref, own_ref, out_ref, spread_ref):
    up, last = core(), planes - 1
    place = (1 - up) * last
    spread_back(other_ref[up * last], spread_ref)
    out_ref[...] = own_ref[...]
    out_ref[place] = out_ref[place] + dot(spread_ref[...], taps(weight_ref, 2 * up))


def backward_other(other, weight, own):
    planes, plane, _ = own.shape
    filters = weight.shape[1]
    return call(
        functools.partial(backward_other_body, planes),
        struct(own.shape, jnp.float32),
        (2 * weight.size // 3 * plane, weight.size * 2 // 3),
        other, weight, own,
        in_specs=[VMEM] * 3,
        scratch_shapes=[pltpu.VMEM((plane, 9 * filters), jnp.bfloat16)],
    )


def backward_rest_body(planes, count, beyond_ref, weight_ref, own_ref, *refs):
    kept_ref, sent, (spread_ref, total_ref) = refs[0], refs[1:count], refs[count:]
    size = kept_ref.shape[2]
    up, me = core(), here("filt")
    place = up * (planes - 1)
    spread_back(beyond_ref[0], spread_ref)
    product = dot(spread_ref[...], taps(weight_ref, 2 * (1 - up)))
    for block in range(count):
        columns = slice(block * size, (block + 1) * size)
        for j in range(planes):
            total_ref[block, j] = own_ref[j, :, columns]
        total_ref[block, place] = total_ref[block, place] + product[:, columns]
    kept_ref[...] = total_ref[me]
    for number in range(1, count):
        sent[number - 1][...] = total_ref[me ^ number].astype(jnp.bfloat16)


def backward_rest(beyond, weight, own, count, after):
    planes, plane, channels = own.shape
    filters = weight.shape[1]
    size = channels // count
    outs = [struct((planes, plane, size), jnp.float32)]
    outs += [struct((planes, plane, size), jnp.bfloat16)] * (count - 1)
    return call(
        functools.partial(backward_rest_body, planes, count),
        outs,
        (2 * 9 * filters * channels * plane, weight.size * 2 // 3),
        beyond, weight, own,
        in_specs=[VMEM] * 3,
        scratch_shapes=[
            pltpu.VMEM((plane, 9 * filters), jnp.bfloat16),
            pltpu.VMEM((count, planes, plane, size), jnp.float32),
        ],
        after=after,
    )


def first_grad_body(count, slope_ref, *refs):
    parts, out_ref = refs[:count], refs[count]
    for j in range(out_ref.shape[0]):
        total = parts[0][j]
        for part in parts[1:]:
            total = total + part[j].astype(jnp.float32)
        out_ref[j] = (total * slope_ref[j]).astype(jnp.bfloat16)


def first_out(parts, slope, after):
    return call(
        functools.partial(first_grad_body, len(parts)),
        struct(slope.shape, jnp.bfloat16),
        (slope.size * 4, slope.size * 14),
        slope, *parts,
        in_specs=[VMEM] * (1 + len(parts)),
        after=after,
    )


def spread_body(split, *refs):
    spread_ref, token_ref = refs[split:]
    token_ref[...] = jnp.zeros_like(token_ref)
    depth, rows, plane = refs[0].shape
    me = lax.rem(here("filt"), split)
    for d in range(depth):
        for half in range(split):
            values = refs[half][d].astype(jnp.float32)
            for number, (b, e) in enumerate(SHIFTS):
                begin = (number * split + (me ^ half)) * rows
                moved = shifted(values, 1, b, e).astype(jnp.bfloat16)
                spread_ref[pl.ds(pl.multiple_of(begin, rows), rows), d * plane : (d + 1) * plane] = moved


def spread(halved):
    split = len(halved)
    depth, rows, plane = halved[0].shape
    channels = split * rows
    return call(
        functools.partial(spread_body, split),
        [struct((9 * channels, depth * plane), jnp.bfloat16), TOKEN],
        (9 * channels * depth * plane, 10 * channels * depth * plane),
        *halved,
        in_specs=[VMEM] * split,
    )


def weight_grad_body(count, second, spread_ref, crossed_ref, *refs):
    parts, grad_ref = refs[:count], refs[-1]
    if second:
        carried_ref, out_ref, token_ref, copy_ref = refs[count:-1]
        copy_ref[...] = carried_ref[...]
    else:
        out_ref, token_ref = refs[count:-1]
    token_ref[...] = jnp.zeros_like(token_ref)
    planes, plane, filters = parts[0].shape
    channels = spread_ref.shape[0] // 9
    depth = spread_ref.shape[1] // plane
    zero = jnp.zeros((plane, filters), jnp.bfloat16)
    grad_ref[depth * plane : (depth + 1) * plane, : filters] = zero
    grad_ref[plane : 2 * plane, 2 * filters :] = zero

    def one(block, d, begin):
        rows = block.shape[0]
        for a in (-1, 0, 1):
            place = pl.ds(pl.multiple_of((d + a + 1) * plane + begin, rows), rows)
            grad_ref[place, (a + 1) * filters : (a + 2) * filters] = block

    near, far = far_owners(0), far_owners(1)
    owners = [near[0], far[0], *near[1:], *far[1:]] if second else near + far
    row = 0
    for number in range(count):
        for j in range(planes):
            one(parts[number][j], owners[number] * planes + j, 0)
    for number in range(count, len(owners)):
        for j in range(planes):
            for begin in range(0, plane, filters):
                block = crossed_ref[row : row + filters, begin : begin + filters]
                one(block, owners[number] * planes + j, begin)
            row += filters

    product = dot(spread_ref[...], grad_ref[plane : (depth + 1) * plane, :])
    for r in range(3):
        for number in range(9):
            out_ref[r * 9 + number] = product[
                number * channels : (number + 1) * channels, r * filters : (r + 1) * filters
            ]


def weight_grad(spreads, blocks, crossed, carried=()):
    channels, columns = spreads.shape[0] // 9, spreads.shape[1]
    _, plane, filters = blocks[0].shape
    return call(
        functools.partial(weight_grad_body, len(blocks), len(carried) > 0),
        [struct((27, channels, filters), jnp.float32), TOKEN, *(struct(block.shape, block.dtype) for block in carried)],
        (2 * 27 * filters * channels * columns, 27 * channels * filters * 4 + spreads.size * 2),
        spreads, crossed, *blocks, *carried,
        in_specs=[VMEM] * (2 + len(blocks) + len(carried)),
        scratch_shapes=[pltpu.VMEM((columns + 2 * plane, 3 * filters), jnp.bfloat16)],
    )


def shards(features, first_weight, second_weight, head_weight, labels):
    count = lax.axis_size("filt")
    chips = lax.axis_size("slab") // 2
    split = halves(features.shape[1] * count // lax.axis_size("slab"))
    near, first_weight, head_weight = stage(features, first_weight, head_weight)
    all_in, share_in = assemble([near] + exchanged(features, "filt")[1:])
    own = forward_own(all_in, first_weight)
    other, beyond = halo(all_in, own)
    own, passed = forward_other(other, first_weight, own, share_in[1:2])
    share_in = [share_in[0]] + chips_apart(passed + share_in[2:])
    slope_first, hidden = forward_rest(beyond, first_weight, own, share_in[1:])

    halved_in = collected(share_in, [hidden])
    all_hidden, share_hidden = assemble(exchanged(hidden, "filt"), [halved_in])
    own = forward_own(all_hidden, second_weight)
    other, beyond = halo(all_hidden, own)
    own, passed = forward_other(other, second_weight, own, share_hidden[1:2])
    share_hidden = [share_hidden[0]] + chips_apart(passed + share_hidden[2:])
    halved_in = both_halves(halved_in, split)
    due = share_hidden[1:] + halved_in
    slope_second, logits = forward_rest(beyond, second_weight, own, due, head_weight)

    logits_parts = exchanged(logits, "filt")
    halved_hidden = both_halves(collected(share_hidden, [logits], logits_parts[1:]), split)
    second_out = loss_grad(logits_parts, labels, head_weight, slope_second, [])
    own = backward_own(second_out, second_weight)
    second_other, beyond = halo(second_out, own)
    second_far = every_chip(second_out)[1:]
    own = backward_other(second_other, second_weight, own)
    due = halved_hidden + second_far[chips // 2 - 1 : chips // 2]
    kept, *sent = backward_rest(beyond, second_weight, own, count, due)
    parts = [kept] + [swap(part, "filt", 1 + number) for number, part in enumerate(sent)]
    spread_in, token_in = spread(halved_in)
    spread_hidden, token_hidden = spread(halved_hidden)
    first_out_grad = first_out(parts, slope_first, [token_in, token_hidden, *second_far])

    crossed = swap(pack(second_far, [first_out_grad]), "slab", 1)
    second_blocks = [second_out, second_other] + second_far
    second_grad, token, passed = weight_grad(spread_hidden, second_blocks, crossed, [first_out_grad])
    first_blocks = [first_out_grad] + chips_apart([passed] + [first_out_grad] * (chips - 2))
    crossed = swap(pack(first_blocks, [token]), "slab", 1)
    first_grad, _ = weight_grad(spread_in, first_blocks, crossed)
    return jnp.transpose(first_grad, (0, 2, 1)), jnp.transpose(second_grad, (0, 2, 1))


def solution(mesh):
    placed = (
        P("slab", "filt", None),
        P(None, "filt", None),
        P(None, "filt", None),
        P(None, "filt"),
        P("slab", None),
    )
    return jax.shard_map(
        shards,
        mesh=mesh,
        in_specs=placed,
        out_specs=(P(None, "filt", "slab"), P(None, "filt", "slab")),
        check_vma=False,
    )
```

```python
import functools

import jax
import jax.numpy as jnp
from jax import lax
from jax.experimental import pallas as pl
from jax.experimental.pallas import tpu as pltpu
from jax.sharding import PartitionSpec as P

WIDTH = 8
SHIFTS = [(b, e) for b in (-1, 0, 1) for e in (-1, 0, 1)]
LIMIT = 20 * 1024 * 1024
VMEM = pl.BlockSpec(memory_space=pltpu.VMEM)
ANY = pl.BlockSpec(memory_space=pl.ANY)


def swap(block, axis, step):
    count = lax.axis_size(axis)
    return lax.ppermute(block, axis, [(i, i ^ step) for i in range(count)])


def exchanged(block, axis):
    return [block] + [swap(block, axis, step) for step in range(1, lax.axis_size(axis))]


def halo(volume, own, due=()):
    count = lax.axis_size("slab")
    other = swap(volume, "slab", 1)
    passed = edge(other, [own, *due])
    pairs = [(i, i + 2) for i in range(0, count - 2, 2)] + [(i, i - 2) for i in range(3, count, 2)]
    return other, lax.ppermute(passed, "slab", pairs)


def chips_apart(blocks):
    return [swap(block, "slab", 2 + 2 * number) for number, block in enumerate(blocks)]


def every_chip(block):
    blocks = [block]
    for step in range(1, lax.axis_size("slab") // 2):
        low = step & -step
        blocks.append(swap(blocks[step ^ low], "slab", 2 * low))
    return blocks


def call(body, out_shape, cost, *operands, in_specs, scratch_shapes=(), passed=(), after=()):
    flops, moved = cost
    single = not isinstance(out_shape, list)
    outs = [out_shape] if single else out_shape
    first, second = len(operands), len(operands) + len(passed) + len(after)
    third = second + len(outs)

    def inner(*refs):
        body(*refs[:first], *refs[second:third], *refs[third + len(passed) :])

    given = pl.pallas_call(
        inner,
        out_shape=[*outs, *(struct(array.shape, array.dtype) for array in passed)],
        cost_estimate=pl.CostEstimate(flops=flops, bytes_accessed=moved, transcendentals=0),
        compiler_params=pltpu.CompilerParams(vmem_limit_bytes=LIMIT),
        in_specs=[*in_specs] + [ANY] * (len(passed) + len(after)),
        out_specs=[VMEM] * len(outs) + [ANY] * len(passed),
        scratch_shapes=list(scratch_shapes),
        input_output_aliases={first + i: len(outs) + i for i in range(len(passed))},
    )(*operands, *passed, *after)
    if passed:
        return [*given[: len(outs)], list(given[len(outs) :])]
    return given[0] if single else list(given)


def struct(shape, dtype):
    return jax.ShapeDtypeStruct(tuple(shape), dtype)


def here(axis):
    return lax.axis_index(axis).astype(jnp.int32)


def core():
    return lax.rem(here("slab"), 2)


def far_owners(side):
    me = here("slab")
    return [me ^ (2 * step) ^ side for step in range(lax.axis_size("slab") // 2)]


TOKEN = struct((8, 128), jnp.float32)


def stage_body(count, *refs):
    sources, targets, sems = refs[:count], refs[count : 2 * count], refs[2 * count]
    copies = [pltpu.make_async_copy(sources[i], targets[i], sems.at[i]) for i in range(count)]
    for copy in copies:
        copy.start()
    for copy in copies:
        copy.wait()


def stage(*arrays):
    count = len(arrays)
    return call(
        functools.partial(stage_body, count),
        [struct(array.shape, array.dtype) for array in arrays],
        (0, sum(4 * array.size for array in arrays)),
        *arrays,
        in_specs=[pl.BlockSpec(memory_space=pltpu.HBM)] * count,
        scratch_shapes=[pltpu.SemaphoreType.DMA((count,))],
    )


def inside(shape, axis, b, e):
    spot = lax.broadcasted_iota(jnp.int32, shape, axis)
    column = spot % WIDTH + e
    moved = spot + WIDTH * b
    return (column >= 0) & (column < WIDTH) & (moved >= 0) & (moved < shape[axis])


def shifted(values, axis, b, e):
    if b == 0 and e == 0:
        return values
    size = values.shape[axis]
    turned = pltpu.roll(values, (-(WIDTH * b + e)) % size, axis)
    return jnp.where(inside(values.shape, axis, b, e), turned, 0.0)


def fold_shifts(products):
    rows = products.shape[0] // len(SHIFTS)
    total = None
    for number, (b, e) in enumerate(SHIFTS):
        term = shifted(products[number * rows : (number + 1) * rows, :], 1, b, e)
        total = term if total is None else total + term
    return total


def dot(left, right):
    return jnp.dot(left, right, preferred_element_type=jnp.float32)


def edge_body(other_ref, out_ref):
    out_ref[0] = other_ref[(1 - core()) * (other_ref.shape[0] - 1)]


def edge(other, after):
    shape = (1, *other.shape[1:])
    return call(edge_body, struct(shape, other.dtype), (0, other.size), other, in_specs=[VMEM], after=after)


def halves(rows):
    return 2 if rows % 32 == 0 and lax.axis_size("filt") % 2 == 0 else 1


def assemble_body(count, split, *refs):
    parts, whole_ref, shares = refs[:count], refs[count], refs[count + 1 :]
    size = parts[0].shape[1]
    me, chip = here("filt"), here("slab") // 2
    for step in range(count):
        place = pl.ds(pl.multiple_of((me ^ step) * size, size), size)
        whole_ref[:, place, :] = parts[step][...]
    rows = shares[0].shape[2]
    for step, share_ref in enumerate(shares):
        for side in range(2):
            begin = (((chip ^ step) * 2 + side) * split + lax.rem(me, split)) * rows
            share_ref[side] = whole_ref[:, pl.ds(pl.multiple_of(begin, rows), rows), :]


def assemble(parts, after=()):
    planes, size, plane = parts[0].shape
    count, slabs = len(parts), lax.axis_size("slab")
    channels = size * count
    split = halves(channels // slabs)
    kind = parts[0].dtype
    outs = [struct((planes, channels, plane), kind)]
    outs += [struct((2, planes, channels // slabs // split, plane), kind)] * (slabs // 2)
    whole, *shares = call(
        functools.partial(assemble_body, count, split),
        outs,
        (0, 4 * planes * channels * plane),
        *parts,
        in_specs=[VMEM] * count,
        after=after,
    )
    return whole, shares


def crossing_body(count, *refs):
    planes = refs[0].shape[1]
    for step in range(count):
        for j in range(planes):
            refs[count][step * planes + j] = refs[step][1 - core(), j]


def collect_body(count, crossed_ref, *refs):
    owners, side = far_owners(0), core()
    planes = refs[0].shape[1]
    for step in range(count):
        for j in range(planes):
            refs[count][owners[step] * planes + j] = refs[step][side, j]
            refs[count][(owners[step] ^ 1) * planes + j] = crossed_ref[step * planes + j]


def collected(shares, after, later=()):
    count = len(shares)
    _, planes, rows, plane = shares[0].shape
    kind, size = shares[0].dtype, shares[0].size * count
    crossing = call(
        functools.partial(crossing_body, count),
        struct((count * planes, rows, plane), kind),
        (0, 2 * size),
        *shares,
        in_specs=[VMEM] * count,
        after=after,
    )
    return call(
        functools.partial(collect_body, count),
        struct((2 * count * planes, rows, plane), kind),
        (0, 4 * size),
        swap(crossing, "slab", 1), *shares,
        in_specs=[VMEM] * (1 + count),
        after=later,
    )


def both_halves(volume, split):
    return [volume] + ([swap(volume, "filt", 1)] if split == 2 else [])


def pack_body(count, *refs):
    out_ref = refs[count]
    row = 0
    for number in range(count):
        planes, plane, filters = refs[number].shape
        for j in range(planes):
            for begin in range(0, plane, filters):
                out_ref[row : row + filters, begin : begin + filters] = refs[number][j, begin : begin + filters, :]
            row += filters


def pack(blocks, after=()):
    plane = blocks[0].shape[1]
    total = sum(block.size for block in blocks)
    return call(
        functools.partial(pack_body, len(blocks)),
        struct((total // plane, plane), blocks[0].dtype),
        (0, 4 * total),
        *blocks,
        in_specs=[VMEM] * len(blocks),
        after=after,
    )


def taps(weight_ref, number):
    block = weight_ref[pl.ds(9 * number, 9)]
    return block.reshape(block.shape[0] * block.shape[1], block.shape[2])


def forward_own_body(planes, volume_ref, weight_ref, out_ref, acc_ref):
    for a in (0, 1, -1):
        weight = taps(weight_ref, a + 1)
        for j in range(planes):
            if 0 <= j + a < planes:
                product = dot(weight, volume_ref[j + a])
                acc_ref[j] = product if a == 0 else acc_ref[j] + product
    for j in range(planes):
        out_ref[j] = fold_shifts(acc_ref.at[j])


def forward_own(volume, weight):
    planes, channels, plane = volume.shape
    filters = weight.shape[1]
    return call(
        functools.partial(forward_own_body, planes),
        struct((planes, filters, plane), jnp.float32),
        (2 * 9 * filters * channels * plane * (3 * planes - 2), weight.size * 2),
        volume, weight,
        in_specs=[VMEM] * 2,
        scratch_shapes=[pltpu.VMEM((planes, 9 * filters, plane), jnp.float32)],
    )


def forward_other_body(planes, other_ref, weight_ref, own_ref, out_ref, acc_ref):
    up, last = core(), planes - 1
    place = (1 - up) * last
    acc_ref[...] = dot(taps(weight_ref, 2 * (1 - up)), other_ref[up * last])
    out_ref[...] = own_ref[...]
    out_ref[place] = out_ref[place] + fold_shifts(acc_ref)


def forward_other(other, weight, own):
    planes, filters, plane = own.shape
    return call(
        functools.partial(forward_other_body, planes),
        struct(own.shape, jnp.float32),
        (2 * weight.size // 3 * plane, weight.size * 2 // 3),
        other, weight, own,
        in_specs=[VMEM] * 3,
        scratch_shapes=[pltpu.VMEM((9 * filters, plane), jnp.float32)],
    )


def silu_and_slope(values):
    sig = 1.0 / (1.0 + jnp.exp(-values))
    return values * sig, sig * (1.0 + values * (1.0 - sig))


def forward_rest_body(planes, beyond_ref, weight_ref, own_ref, *refs):
    head_ref = refs[0] if len(refs) == 5 else None
    slope_ref, made_ref, acc_ref, total_ref = refs[-4:]
    up = core()
    place = up * (planes - 1)
    total_ref[...] = own_ref[...]
    acc_ref[...] = dot(taps(weight_ref, 2 * up), beyond_ref[0])
    total_ref[place] = total_ref[place] + fold_shifts(acc_ref)
    for j in range(planes):
        value, slope = silu_and_slope(total_ref[j])
        value = value.astype(jnp.bfloat16)
        slope_ref[j] = slope.T if head_ref is None else slope
        made_ref[j] = value if head_ref is None else dot(head_ref[...], value)


def forward_rest(beyond, weight, own, after, head=None):
    planes, filters, plane = own.shape
    channels = weight.shape[2]
    ins = [beyond, weight, own]
    slope = own.shape
    if head is None:
        slope = (planes, plane, filters)
        made = struct(own.shape, jnp.bfloat16)
    else:
        ins.append(head)
        made = struct((planes, head.shape[0], plane), jnp.float32)
    return call(
        functools.partial(forward_rest_body, planes),
        [struct(slope, jnp.float32), made],
        (2 * 9 * filters * channels * plane, weight.size * 2 // 3),
        *ins,
        in_specs=[VMEM] * len(ins),
        scratch_shapes=[
            pltpu.VMEM((9 * filters, plane), jnp.float32),
            pltpu.VMEM(own.shape, jnp.float32),
        ],
        after=after,
    )


def loss_body(count, labels_ref, head_ref, slope_ref, *refs):
    parts, grad_ref = refs[:count], refs[count]
    for j in range(grad_ref.shape[0]):
        logits = parts[0][j]
        for part in parts[1:]:
            logits = logits + part[j]
        powers = jnp.exp(logits)
        likely = powers / jnp.sum(powers, axis=0, keepdims=True)
        classes = lax.broadcasted_iota(jnp.int32, logits.shape, 0)
        onehot = (labels_ref[j : j + 1, :] == classes).astype(jnp.float32)
        logit_grad = (likely - onehot).astype(jnp.bfloat16).astype(jnp.float32)
        back = lax.dot_general(
            head_ref[...].astype(jnp.float32),
            logit_grad,
            (((0,), (0,)), ((), ())),
            preferred_element_type=jnp.float32,
        )
        grad_ref[j] = (back * slope_ref[j]).T.astype(jnp.bfloat16)


def loss_grad(parts, labels, head, slope, after):
    planes, plane = labels.shape
    return call(
        functools.partial(loss_body, len(parts)),
        struct((planes, plane, slope.shape[1]), jnp.bfloat16),
        (2 * slope.size * head.shape[0], slope.size * 6),
        labels, head, slope, *parts,
        in_specs=[VMEM] * (3 + len(parts)),
        after=after,
    )


def spread_back(grad, spread_ref):
    filters = grad.shape[1]
    turned = grad.astype(jnp.float32)
    for number, (b, e) in enumerate(SHIFTS):
        moved = shifted(turned, 0, -b, -e).astype(jnp.bfloat16)
        spread_ref[:, number * filters : (number + 1) * filters] = moved


def backward_own_body(planes, grad_ref, weight_ref, out_ref, spread_ref):
    for j in range(planes):
        spread_back(grad_ref[j], spread_ref.at[j])
    for a in (0, 1, -1):
        weight = taps(weight_ref, a + 1)
        for j in range(planes):
            if 0 <= j - a < planes:
                product = dot(spread_ref[j - a], weight)
                out_ref[j] = product if a == 0 else out_ref[j] + product


def backward_own(grad, weight):
    planes, plane, filters = grad.shape
    channels = weight.shape[2]
    return call(
        functools.partial(backward_own_body, planes),
        struct((planes, plane, channels), jnp.float32),
        (2 * 9 * filters * channels * plane * (3 * planes - 2), weight.size * 2),
        grad, weight,
        in_specs=[VMEM] * 2,
        scratch_shapes=[pltpu.VMEM((planes, plane, 9 * filters), jnp.bfloat16)],
    )


def backward_other_body(planes, other_ref, weight_ref, own_ref, out_ref, spread_ref):
    up, last = core(), planes - 1
    place = (1 - up) * last
    spread_back(other_ref[up * last], spread_ref)
    out_ref[...] = own_ref[...]
    out_ref[place] = out_ref[place] + dot(spread_ref[...], taps(weight_ref, 2 * up))


def backward_other(other, weight, own):
    planes, plane, _ = own.shape
    filters = weight.shape[1]
    return call(
        functools.partial(backward_other_body, planes),
        struct(own.shape, jnp.float32),
        (2 * weight.size // 3 * plane, weight.size * 2 // 3),
        other, weight, own,
        in_specs=[VMEM] * 3,
        scratch_shapes=[pltpu.VMEM((plane, 9 * filters), jnp.bfloat16)],
    )


def backward_rest_body(planes, count, beyond_ref, weight_ref, own_ref, *refs):
    kept_ref, sent, (spread_ref, total_ref) = refs[0], refs[1:count], refs[count:]
    size = kept_ref.shape[2]
    up, me = core(), here("filt")
    place = up * (planes - 1)
    spread_back(beyond_ref[0], spread_ref)
    product = dot(spread_ref[...], taps(weight_ref, 2 * (1 - up)))
    for block in range(count):
        columns = slice(block * size, (block + 1) * size)
        for j in range(planes):
            total_ref[block, j] = own_ref[j, :, columns]
        total_ref[block, place] = total_ref[block, place] + product[:, columns]
    kept_ref[...] = total_ref[me]
    for number in range(1, count):
        sent[number - 1][...] = total_ref[me ^ number].astype(jnp.bfloat16)


def backward_rest(beyond, weight, own, count, after):
    planes, plane, channels = own.shape
    filters = weight.shape[1]
    size = channels // count
    outs = [struct((planes, plane, size), jnp.float32)]
    outs += [struct((planes, plane, size), jnp.bfloat16)] * (count - 1)
    return call(
        functools.partial(backward_rest_body, planes, count),
        outs,
        (2 * 9 * filters * channels * plane, weight.size * 2 // 3),
        beyond, weight, own,
        in_specs=[VMEM] * 3,
        scratch_shapes=[
            pltpu.VMEM((plane, 9 * filters), jnp.bfloat16),
            pltpu.VMEM((count, planes, plane, size), jnp.float32),
        ],
        after=after,
    )


def first_grad_body(count, slope_ref, *refs):
    parts, out_ref = refs[:count], refs[count]
    for j in range(out_ref.shape[0]):
        total = parts[0][j]
        for part in parts[1:]:
            total = total + part[j].astype(jnp.float32)
        out_ref[j] = (total * slope_ref[j]).astype(jnp.bfloat16)


def first_out(parts, slope, after):
    return call(
        functools.partial(first_grad_body, len(parts)),
        struct(slope.shape, jnp.bfloat16),
        (slope.size * 4, slope.size * 14),
        slope, *parts,
        in_specs=[VMEM] * (1 + len(parts)),
        after=after,
    )


def spread_body(split, *refs):
    spread_ref, token_ref = refs[split:]
    token_ref[...] = jnp.zeros_like(token_ref)
    depth, rows, plane = refs[0].shape
    me = lax.rem(here("filt"), split)
    for d in range(depth):
        for half in range(split):
            values = refs[half][d].astype(jnp.float32)
            for number, (b, e) in enumerate(SHIFTS):
                begin = (number * split + (me ^ half)) * rows
                moved = shifted(values, 1, b, e).astype(jnp.bfloat16)
                spread_ref[pl.ds(pl.multiple_of(begin, rows), rows), d * plane : (d + 1) * plane] = moved


def spread(halved):
    split = len(halved)
    depth, rows, plane = halved[0].shape
    channels = split * rows
    return call(
        functools.partial(spread_body, split),
        [struct((9 * channels, depth * plane), jnp.bfloat16), TOKEN],
        (9 * channels * depth * plane, 10 * channels * depth * plane),
        *halved,
        in_specs=[VMEM] * split,
    )


def weight_grad_body(count, second, spread_ref, crossed_ref, *refs):
    parts, (out_ref, token_ref, grad_ref) = refs[:count], refs[count:]
    token_ref[...] = jnp.zeros_like(token_ref)
    planes, plane, filters = parts[0].shape
    channels = spread_ref.shape[0] // 9
    depth = spread_ref.shape[1] // plane
    zero = jnp.zeros((plane, filters), jnp.bfloat16)
    grad_ref[depth * plane : (depth + 1) * plane, : filters] = zero
    grad_ref[plane : 2 * plane, 2 * filters :] = zero

    def one(block, d, begin):
        rows = block.shape[0]
        for a in (-1, 0, 1):
            place = pl.ds(pl.multiple_of((d + a + 1) * plane + begin, rows), rows)
            grad_ref[place, (a + 1) * filters : (a + 2) * filters] = block

    near, far = far_owners(0), far_owners(1)
    owners = [near[0], far[0], *near[1:], *far[1:]] if second else near + far
    row = 0
    for number in range(count):
        for j in range(planes):
            one(parts[number][j], owners[number] * planes + j, 0)
    for number in range(count, len(owners)):
        for j in range(planes):
            for begin in range(0, plane, filters):
                block = crossed_ref[row : row + filters, begin : begin + filters]
                one(block, owners[number] * planes + j, begin)
            row += filters

    product = dot(spread_ref[...], grad_ref[plane : (depth + 1) * plane, :])
    for r in range(3):
        for number in range(9):
            out_ref[r * 9 + number] = product[
                number * channels : (number + 1) * channels, r * filters : (r + 1) * filters
            ]


def weight_grad(spreads, blocks, crossed, second):
    channels, columns = spreads.shape[0] // 9, spreads.shape[1]
    _, plane, filters = blocks[0].shape
    return call(
        functools.partial(weight_grad_body, len(blocks), second),
        [struct((27, channels, filters), jnp.float32), TOKEN],
        (2 * 27 * filters * channels * columns, 27 * channels * filters * 4 + spreads.size * 2),
        spreads, crossed, *blocks,
        in_specs=[VMEM] * (2 + len(blocks)),
        scratch_shapes=[pltpu.VMEM((columns + 2 * plane, 3 * filters), jnp.bfloat16)],
    )


def shards(features, first_weight, second_weight, head_weight, labels):
    count = lax.axis_size("filt")
    chips = lax.axis_size("slab") // 2
    split = halves(features.shape[1] * count // lax.axis_size("slab"))
    near, first_weight, head_weight = stage(features, first_weight, head_weight)
    all_in, share_in = assemble([near] + exchanged(features, "filt")[1:])
    own = forward_own(all_in, first_weight)
    share_in = [share_in[0]] + chips_apart(share_in[1:])
    other, beyond = halo(all_in, own, share_in[1:])
    own = forward_other(other, first_weight, own)
    slope_first, hidden = forward_rest(beyond, first_weight, own, [])

    halved_in = collected(share_in, [hidden])
    all_hidden, share_hidden = assemble(exchanged(hidden, "filt"), [halved_in])
    own = forward_own(all_hidden, second_weight)
    share_hidden = [share_hidden[0]] + chips_apart(share_hidden[1:])
    other, beyond = halo(all_hidden, own, share_hidden[1:])
    own = forward_other(other, second_weight, own)
    halved_in = both_halves(halved_in, split)
    slope_second, logits = forward_rest(beyond, second_weight, own, halved_in, head_weight)

    logits_parts = exchanged(logits, "filt")
    second_out = loss_grad(logits_parts, labels, head_weight, slope_second, [])
    halved_hidden = both_halves(collected(share_hidden, [logits], [second_out]), split)
    own = backward_own(second_out, second_weight)
    second_other, beyond = halo(second_out, own)
    second_far = every_chip(second_out)[1:]
    own = backward_other(second_other, second_weight, own)
    due = halved_hidden + second_far[chips // 2 - 1 : chips // 2]
    kept, *sent = backward_rest(beyond, second_weight, own, count, due)
    parts = [kept] + [swap(part, "filt", 1 + number) for number, part in enumerate(sent)]
    spread_in, token_in = spread(halved_in)
    spread_hidden, token_hidden = spread(halved_hidden)
    first_out_grad = first_out(parts, slope_first, [token_in, token_hidden, *second_far])

    first_blocks = [first_out_grad] + chips_apart([first_out_grad] * (chips - 1))
    crossed = swap(pack(second_far, [first_out_grad]), "slab", 1)
    second_blocks = [second_out, second_other] + second_far
    second_grad, token = weight_grad(spread_hidden, second_blocks, crossed, True)
    crossed = swap(pack(first_blocks, [token]), "slab", 1)
    first_grad, _ = weight_grad(spread_in, first_blocks, crossed, False)
    return jnp.transpose(first_grad, (0, 2, 1)), jnp.transpose(second_grad, (0, 2, 1))


def solution(mesh):
    placed = (
        P("slab", "filt", None),
        P(None, "filt", None),
        P(None, "filt", None),
        P(None, "filt"),
        P("slab", None),
    )
    return jax.shard_map(
        shards,
        mesh=mesh,
        in_specs=placed,
        out_specs=(P(None, "filt", "slab"), P(None, "filt", "slab")),
        check_vma=False,
    )
```

```python
import functools

import jax
import jax.numpy as jnp
from jax import lax
from jax.experimental import pallas as pl
from jax.experimental.pallas import tpu as pltpu
from jax.sharding import PartitionSpec as P

WIDTH = 8
SHIFTS = [(b, e) for b in (-1, 0, 1) for e in (-1, 0, 1)]
LIMIT = 20 * 1024 * 1024
VMEM = pl.BlockSpec(memory_space=pltpu.VMEM)
ANY = pl.BlockSpec(memory_space=pl.ANY)


def swap(block, axis, step):
    count = lax.axis_size(axis)
    return lax.ppermute(block, axis, [(i, i ^ step) for i in range(count)])


def exchanged(block, axis):
    return swapped([block] * lax.axis_size(axis), axis, 1)


def swapped(blocks, axis, unit):
    return [blocks[0]] + [swap(blocks[step], axis, unit * step) for step in range(1, len(blocks))]


def halo(volume, own):
    count = lax.axis_size("slab")
    other = swap(volume, "slab", 1)
    passed = edge(other, [own])
    pairs = [(i, i + 2) for i in range(0, count - 2, 2)] + [(i, i - 2) for i in range(3, count, 2)]
    return other, lax.ppermute(passed, "slab", pairs)


def chips_apart(blocks):
    return swapped([None, *blocks], "slab", 2)[1:]


def every_chip(block):
    blocks = [block]
    for step in range(1, lax.axis_size("slab") // 2):
        low = step & -step
        blocks.append(swap(blocks[step ^ low], "slab", 2 * low))
    return blocks


def call(body, out_shape, cost, *operands, in_specs, scratch_shapes=(), passed=(), after=()):
    flops, moved = cost
    single = not isinstance(out_shape, list)
    outs = [out_shape] if single else out_shape
    first, second = len(operands), len(operands) + len(passed) + len(after)
    third = second + len(outs)

    def inner(*refs):
        body(*refs[:first], *refs[second:third], *refs[third + len(passed) :])

    given = pl.pallas_call(
        inner,
        out_shape=[*outs, *(struct(array.shape, array.dtype) for array in passed)],
        cost_estimate=pl.CostEstimate(flops=flops, bytes_accessed=moved, transcendentals=0),
        compiler_params=pltpu.CompilerParams(vmem_limit_bytes=LIMIT),
        in_specs=[*in_specs] + [ANY] * (len(passed) + len(after)),
        out_specs=[VMEM] * len(outs) + [ANY] * len(passed),
        scratch_shapes=list(scratch_shapes),
        input_output_aliases={first + i: len(outs) + i for i in range(len(passed))},
    )(*operands, *passed, *after)
    if passed:
        return [*given[: len(outs)], list(given[len(outs) :])]
    return given[0] if single else list(given)


def struct(shape, dtype):
    return jax.ShapeDtypeStruct(tuple(shape), dtype)


def here(axis):
    return lax.axis_index(axis).astype(jnp.int32)


def core():
    return lax.rem(here("slab"), 2)


def far_owners(side):
    me = here("slab")
    return [me ^ (2 * step) ^ side for step in range(lax.axis_size("slab") // 2)]


TOKEN = struct((8, 128), jnp.float32)


def stage_body(count, *refs):
    sources, targets, sems = refs[:count], refs[count : 2 * count], refs[2 * count]
    copies = [pltpu.make_async_copy(sources[i], targets[i], sems.at[i]) for i in range(count)]
    for copy in copies:
        copy.start()
    for copy in copies:
        copy.wait()


def stage(*arrays):
    count = len(arrays)
    return call(
        functools.partial(stage_body, count),
        [struct(array.shape, array.dtype) for array in arrays],
        (0, sum(4 * array.size for array in arrays)),
        *arrays,
        in_specs=[pl.BlockSpec(memory_space=pltpu.HBM)] * count,
        scratch_shapes=[pltpu.SemaphoreType.DMA((count,))],
    )


def inside(shape, axis, b, e):
    spot = lax.broadcasted_iota(jnp.int32, shape, axis)
    column = spot % WIDTH + e
    moved = spot + WIDTH * b
    return (column >= 0) & (column < WIDTH) & (moved >= 0) & (moved < shape[axis])


def shifted(values, axis, b, e):
    if b == 0 and e == 0:
        return values
    size = values.shape[axis]
    turned = pltpu.roll(values, (-(WIDTH * b + e)) % size, axis)
    return jnp.where(inside(values.shape, axis, b, e), turned, 0.0)


def fold_shifts(products):
    rows = products.shape[0] // len(SHIFTS)
    total = None
    for number, (b, e) in enumerate(SHIFTS):
        term = shifted(products[number * rows : (number + 1) * rows, :], 1, b, e)
        total = term if total is None else total + term
    return total


def dot(left, right):
    return jnp.dot(left, right, preferred_element_type=jnp.float32)


def edge_body(other_ref, out_ref):
    out_ref[0] = other_ref[(1 - core()) * (other_ref.shape[0] - 1)]


def edge(other, after):
    shape = (1, *other.shape[1:])
    return call(edge_body, struct(shape, other.dtype), (0, other.size), other, in_specs=[VMEM], after=after)


def halves(rows):
    return 2 if rows % 32 == 0 and lax.axis_size("filt") % 2 == 0 else 1


def assemble_body(count, split, *refs):
    parts, whole_ref, shares = refs[:count][::-1], refs[count], refs[count + 1 :]
    size = parts[0].shape[1]
    me, chip = here("filt"), here("slab") // 2
    for step in range(count):
        place = pl.ds(pl.multiple_of((me ^ step) * size, size), size)
        whole_ref[:, place, :] = parts[step][...]
    rows = shares[0].shape[2]
    for step, share_ref in enumerate(shares):
        for side in range(2):
            begin = (((chip ^ step) * 2 + side) * split + lax.rem(me, split)) * rows
            share_ref[side] = whole_ref[:, pl.ds(pl.multiple_of(begin, rows), rows), :]


def assemble(parts, after=()):
    planes, size, plane = parts[0].shape
    count, slabs = len(parts), lax.axis_size("slab")
    channels = size * count
    split = halves(channels // slabs)
    kind = parts[0].dtype
    outs = [struct((planes, channels, plane), kind)]
    outs += [struct((2, planes, channels // slabs // split, plane), kind)] * (slabs // 2)
    whole, *shares = call(
        functools.partial(assemble_body, count, split),
        outs,
        (0, 4 * planes * channels * plane),
        *parts[::-1],
        in_specs=[VMEM] * count,
        after=after,
    )
    return whole, shares


def crossing_body(count, *refs):
    planes = refs[0].shape[1]
    for step in range(count):
        for j in range(planes):
            refs[count][step * planes + j] = refs[step][1 - core(), j]


def collect_body(count, crossed_ref, *refs):
    owners, side = far_owners(0), core()
    planes = refs[0].shape[1]
    for step in range(count):
        for j in range(planes):
            refs[count][owners[step] * planes + j] = refs[step][side, j]
            refs[count][(owners[step] ^ 1) * planes + j] = crossed_ref[step * planes + j]


def collected(shares, after, later=()):
    count = len(shares)
    _, planes, rows, plane = shares[0].shape
    kind, size = shares[0].dtype, shares[0].size * count
    crossing = call(
        functools.partial(crossing_body, count),
        struct((count * planes, rows, plane), kind),
        (0, 2 * size),
        *shares,
        in_specs=[VMEM] * count,
        after=after,
    )
    return call(
        functools.partial(collect_body, count),
        struct((2 * count * planes, rows, plane), kind),
        (0, 4 * size),
        swap(crossing, "slab", 1), *shares,
        in_specs=[VMEM] * (1 + count),
        after=later,
    )


def both_halves(volume, split):
    return [volume] + ([swap(volume, "filt", 1)] if split == 2 else [])


def pack_body(count, *refs):
    out_ref = refs[count]
    blocks = refs[:count][::-1]
    row = 0
    for number in range(count):
        planes, plane, filters = blocks[number].shape
        for j in range(planes):
            for begin in range(0, plane, filters):
                out_ref[row : row + filters, begin : begin + filters] = blocks[number][j, begin : begin + filters, :]
            row += filters


def pack(blocks, after=()):
    plane = blocks[0].shape[1]
    total = sum(block.size for block in blocks)
    return call(
        functools.partial(pack_body, len(blocks)),
        struct((total // plane, plane), blocks[0].dtype),
        (0, 4 * total),
        *blocks[::-1],
        in_specs=[VMEM] * len(blocks),
        after=after,
    )


def taps(weight_ref, number):
    block = weight_ref[pl.ds(9 * number, 9)]
    return block.reshape(block.shape[0] * block.shape[1], block.shape[2])


def forward_own_body(planes, volume_ref, weight_ref, out_ref, acc_ref):
    for a in (0, 1, -1):
        weight = taps(weight_ref, a + 1)
        for j in range(planes):
            if 0 <= j + a < planes:
                product = dot(weight, volume_ref[j + a])
                acc_ref[j] = product if a == 0 else acc_ref[j] + product
    for j in range(planes):
        out_ref[j] = fold_shifts(acc_ref.at[j])


def forward_own(volume, weight):
    planes, channels, plane = volume.shape
    filters = weight.shape[1]
    return call(
        functools.partial(forward_own_body, planes),
        struct((planes, filters, plane), jnp.float32),
        (2 * 9 * filters * channels * plane * (3 * planes - 2), weight.size * 2),
        volume, weight,
        in_specs=[VMEM] * 2,
        scratch_shapes=[pltpu.VMEM((planes, 9 * filters, plane), jnp.float32)],
    )


def forward_other_body(planes, other_ref, weight_ref, own_ref, out_ref, acc_ref):
    up, last = core(), planes - 1
    place = (1 - up) * last
    acc_ref[...] = dot(taps(weight_ref, 2 * (1 - up)), other_ref[up * last])
    out_ref[...] = own_ref[...]
    out_ref[place] = out_ref[place] + fold_shifts(acc_ref)


def forward_other(other, weight, own):
    planes, filters, plane = own.shape
    return call(
        functools.partial(forward_other_body, planes),
        struct(own.shape, jnp.float32),
        (2 * weight.size // 3 * plane, weight.size * 2 // 3),
        other, weight, own,
        in_specs=[VMEM] * 3,
        scratch_shapes=[pltpu.VMEM((9 * filters, plane), jnp.float32)],
    )


def silu_and_slope(values):
    sig = 1.0 / (1.0 + jnp.exp(-values))
    return values * sig, sig * (1.0 + values * (1.0 - sig))


def forward_rest_body(planes, beyond_ref, weight_ref, own_ref, *refs):
    head_ref = refs[0] if len(refs) == 5 else None
    slope_ref, made_ref, acc_ref, total_ref = refs[-4:]
    up = core()
    place = up * (planes - 1)
    total_ref[...] = own_ref[...]
    acc_ref[...] = dot(taps(weight_ref, 2 * up), beyond_ref[0])
    total_ref[place] = total_ref[place] + fold_shifts(acc_ref)
    for j in range(planes):
        value, slope = silu_and_slope(total_ref[j])
        value = value.astype(jnp.bfloat16)
        slope_ref[j] = slope.T if head_ref is None else slope
        made_ref[j] = value if head_ref is None else dot(head_ref[...], value)


def forward_rest(beyond, weight, own, after, head=None):
    planes, filters, plane = own.shape
    channels = weight.shape[2]
    ins = [beyond, weight, own]
    slope = own.shape
    if head is None:
        slope = (planes, plane, filters)
        made = struct(own.shape, jnp.bfloat16)
    else:
        ins.append(head)
        made = struct((planes, head.shape[0], plane), jnp.float32)
    return call(
        functools.partial(forward_rest_body, planes),
        [struct(slope, jnp.float32), made],
        (2 * 9 * filters * channels * plane, weight.size * 2 // 3),
        *ins,
        in_specs=[VMEM] * len(ins),
        scratch_shapes=[
            pltpu.VMEM((9 * filters, plane), jnp.float32),
            pltpu.VMEM(own.shape, jnp.float32),
        ],
        after=after,
    )


def loss_body(count, labels_ref, head_ref, slope_ref, *refs):
    parts, grad_ref = refs[:count][::-1], refs[count]
    for j in range(grad_ref.shape[0]):
        logits = parts[0][j]
        for part in parts[1:]:
            logits = logits + part[j]
        powers = jnp.exp(logits)
        likely = powers / jnp.sum(powers, axis=0, keepdims=True)
        classes = lax.broadcasted_iota(jnp.int32, logits.shape, 0)
        onehot = (labels_ref[j : j + 1, :] == classes).astype(jnp.float32)
        logit_grad = (likely - onehot).astype(jnp.bfloat16).astype(jnp.float32)
        back = lax.dot_general(
            head_ref[...].astype(jnp.float32),
            logit_grad,
            (((0,), (0,)), ((), ())),
            preferred_element_type=jnp.float32,
        )
        grad_ref[j] = (back * slope_ref[j]).T.astype(jnp.bfloat16)


def loss_grad(parts, labels, head, slope, after):
    planes, plane = labels.shape
    return call(
        functools.partial(loss_body, len(parts)),
        struct((planes, plane, slope.shape[1]), jnp.bfloat16),
        (2 * slope.size * head.shape[0], slope.size * 6),
        labels, head, slope, *parts[::-1],
        in_specs=[VMEM] * (3 + len(parts)),
        after=after,
    )


def spread_back(grad, spread_ref):
    filters = grad.shape[1]
    turned = grad.astype(jnp.float32)
    for number, (b, e) in enumerate(SHIFTS):
        moved = shifted(turned, 0, -b, -e).astype(jnp.bfloat16)
        spread_ref[:, number * filters : (number + 1) * filters] = moved


def backward_own_body(planes, grad_ref, weight_ref, out_ref, spread_ref):
    for j in range(planes):
        spread_back(grad_ref[j], spread_ref.at[j])
    for a in (0, 1, -1):
        weight = taps(weight_ref, a + 1)
        for j in range(planes):
            if 0 <= j - a < planes:
                product = dot(spread_ref[j - a], weight)
                out_ref[j] = product if a == 0 else out_ref[j] + product


def backward_own(grad, weight):
    planes, plane, filters = grad.shape
    channels = weight.shape[2]
    return call(
        functools.partial(backward_own_body, planes),
        struct((planes, plane, channels), jnp.float32),
        (2 * 9 * filters * channels * plane * (3 * planes - 2), weight.size * 2),
        grad, weight,
        in_specs=[VMEM] * 2,
        scratch_shapes=[pltpu.VMEM((planes, plane, 9 * filters), jnp.bfloat16)],
    )


def backward_other_body(planes, other_ref, weight_ref, own_ref, out_ref, spread_ref):
    up, last = core(), planes - 1
    place = (1 - up) * last
    spread_back(other_ref[up * last], spread_ref)
    out_ref[...] = own_ref[...]
    out_ref[place] = out_ref[place] + dot(spread_ref[...], taps(weight_ref, 2 * up))


def backward_other(other, weight, own):
    planes, plane, _ = own.shape
    filters = weight.shape[1]
    return call(
        functools.partial(backward_other_body, planes),
        struct(own.shape, jnp.float32),
        (2 * weight.size // 3 * plane, weight.size * 2 // 3),
        other, weight, own,
        in_specs=[VMEM] * 3,
        scratch_shapes=[pltpu.VMEM((plane, 9 * filters), jnp.bfloat16)],
    )


def backward_rest_body(planes, count, beyond_ref, weight_ref, own_ref, *refs):
    kept_ref, sent, (spread_ref, total_ref) = refs[0], refs[1:count], refs[count:]
    size = kept_ref.shape[2]
    up, me = core(), here("filt")
    place = up * (planes - 1)
    spread_back(beyond_ref[0], spread_ref)
    product = dot(spread_ref[...], taps(weight_ref, 2 * (1 - up)))
    for block in range(count):
        columns = slice(block * size, (block + 1) * size)
        for j in range(planes):
            total_ref[block, j] = own_ref[j, :, columns]
        total_ref[block, place] = total_ref[block, place] + product[:, columns]
    kept_ref[...] = total_ref[me]
    for number in range(1, count):
        sent[number - 1][...] = total_ref[me ^ number].astype(jnp.bfloat16)


def backward_rest(beyond, weight, own, count, after):
    planes, plane, channels = own.shape
    filters = weight.shape[1]
    size = channels // count
    outs = [struct((planes, plane, size), jnp.float32)]
    outs += [struct((planes, plane, size), jnp.bfloat16)] * (count - 1)
    return call(
        functools.partial(backward_rest_body, planes, count),
        outs,
        (2 * 9 * filters * channels * plane, weight.size * 2 // 3),
        beyond, weight, own,
        in_specs=[VMEM] * 3,
        scratch_shapes=[
            pltpu.VMEM((plane, 9 * filters), jnp.bfloat16),
            pltpu.VMEM((count, planes, plane, size), jnp.float32),
        ],
        after=after,
    )


def first_grad_body(count, slope_ref, *refs):
    parts, out_ref = refs[:count][::-1], refs[count]
    for j in range(out_ref.shape[0]):
        total = parts[0][j]
        for part in parts[1:]:
            total = total + part[j].astype(jnp.float32)
        out_ref[j] = (total * slope_ref[j]).astype(jnp.bfloat16)


def first_out(parts, slope, after):
    return call(
        functools.partial(first_grad_body, len(parts)),
        struct(slope.shape, jnp.bfloat16),
        (slope.size * 4, slope.size * 14),
        slope, *parts[::-1],
        in_specs=[VMEM] * (1 + len(parts)),
        after=after,
    )


def spread_body(split, *refs):
    spread_ref, token_ref = refs[split:]
    token_ref[...] = jnp.zeros_like(token_ref)
    depth, rows, plane = refs[0].shape
    me = lax.rem(here("filt"), split)
    for d in range(depth):
        for half in range(split):
            values = refs[half][d].astype(jnp.float32)
            for number, (b, e) in enumerate(SHIFTS):
                begin = (number * split + (me ^ half)) * rows
                moved = shifted(values, 1, b, e).astype(jnp.bfloat16)
                spread_ref[pl.ds(pl.multiple_of(begin, rows), rows), d * plane : (d + 1) * plane] = moved


def spread(halved):
    split = len(halved)
    depth, rows, plane = halved[0].shape
    channels = split * rows
    return call(
        functools.partial(spread_body, split),
        [struct((9 * channels, depth * plane), jnp.bfloat16), TOKEN],
        (9 * channels * depth * plane, 10 * channels * depth * plane),
        *halved,
        in_specs=[VMEM] * split,
    )


def weight_grad_body(count, second, spread_ref, crossed_ref, *refs):
    parts, (out_ref, token_ref, grad_ref) = refs[:count], refs[count:]
    token_ref[...] = jnp.zeros_like(token_ref)
    planes, plane, filters = parts[0].shape
    channels = spread_ref.shape[0] // 9
    depth = spread_ref.shape[1] // plane
    zero = jnp.zeros((plane, filters), jnp.bfloat16)
    grad_ref[depth * plane : (depth + 1) * plane, : filters] = zero
    grad_ref[plane : 2 * plane, 2 * filters :] = zero

    def one(block, d, begin):
        rows = block.shape[0]
        for a in (-1, 0, 1):
            place = pl.ds(pl.multiple_of((d + a + 1) * plane + begin, rows), rows)
            grad_ref[place, (a + 1) * filters : (a + 2) * filters] = block

    near, far = far_owners(0), far_owners(1)
    owners = [near[0], far[0], *near[1:], *far[1:]] if second else near + far
    row = 0
    for number in range(count):
        for j in range(planes):
            one(parts[number][j], owners[number] * planes + j, 0)
    for number in range(count, len(owners)):
        for j in range(planes):
            for begin in range(0, plane, filters):
                block = crossed_ref[row : row + filters, begin : begin + filters]
                one(block, owners[number] * planes + j, begin)
            row += filters

    product = dot(spread_ref[...], grad_ref[plane : (depth + 1) * plane, :])
    for r in range(3):
        for number in range(9):
            out_ref[r * 9 + number] = product[
                number * channels : (number + 1) * channels, r * filters : (r + 1) * filters
            ]


def weight_grad(spreads, blocks, crossed, second):
    channels, columns = spreads.shape[0] // 9, spreads.shape[1]
    _, plane, filters = blocks[0].shape
    return call(
        functools.partial(weight_grad_body, len(blocks), second),
        [struct((27, channels, filters), jnp.float32), TOKEN],
        (2 * 27 * filters * channels * columns, 27 * channels * filters * 4 + spreads.size * 2),
        spreads, crossed, *blocks,
        in_specs=[VMEM] * (2 + len(blocks)),
        scratch_shapes=[pltpu.VMEM((columns + 2 * plane, 3 * filters), jnp.bfloat16)],
    )


def shards(features, first_weight, second_weight, head_weight, labels):
    count = lax.axis_size("filt")
    chips = lax.axis_size("slab") // 2
    split = halves(features.shape[1] * count // lax.axis_size("slab"))
    near, first_weight, head_weight = stage(features, first_weight, head_weight)
    all_in, share_in = assemble([near] + exchanged(features, "filt")[1:])
    own = forward_own(all_in, first_weight)
    share_in = [share_in[0]] + chips_apart(share_in[1:])
    other, beyond = halo(all_in, own)
    own = forward_other(other, first_weight, own)
    slope_first, hidden = forward_rest(beyond, first_weight, own, share_in[:0:-1])

    halved_in = collected(share_in, [hidden])
    all_hidden, share_hidden = assemble(exchanged(hidden, "filt"), [halved_in])
    own = forward_own(all_hidden, second_weight)
    share_hidden = [share_hidden[0]] + chips_apart(share_hidden[1:])
    other, beyond = halo(all_hidden, own)
    own = forward_other(other, second_weight, own)
    halved_in = both_halves(halved_in, split)
    slope_second, logits = forward_rest(beyond, second_weight, own, share_hidden[:0:-1] + halved_in, head_weight)

    logits_parts = exchanged(logits, "filt")
    second_out = loss_grad(logits_parts, labels, head_weight, slope_second, [])
    halved_hidden = both_halves(collected(share_hidden, [logits], [second_out]), split)
    own = backward_own(second_out, second_weight)
    second_other, beyond = halo(second_out, own)
    second_far = every_chip(second_out)[1:]
    own = backward_other(second_other, second_weight, own)
    due = halved_hidden + second_far[chips // 2 - 1 : chips // 2]
    kept, *sent = backward_rest(beyond, second_weight, own, count, due)
    parts = swapped([kept, *sent], "filt", 1)
    spread_in, token_in = spread(halved_in)
    spread_hidden, token_hidden = spread(halved_hidden)
    first_out_grad = first_out(parts, slope_first, [token_in, token_hidden, *second_far])

    first_blocks = [first_out_grad] + chips_apart([first_out_grad] * (chips - 1))
    crossed = swap(pack(second_far, [first_out_grad]), "slab", 1)
    second_blocks = [second_out, second_other] + second_far
    second_grad, token = weight_grad(spread_hidden, second_blocks, crossed, True)
    crossed = swap(pack(first_blocks, [token]), "slab", 1)
    first_grad, _ = weight_grad(spread_in, first_blocks, crossed, False)
    return jnp.transpose(first_grad, (0, 2, 1)), jnp.transpose(second_grad, (0, 2, 1))


def solution(mesh):
    placed = (
        P("slab", "filt", None),
        P(None, "filt", None),
        P(None, "filt", None),
        P(None, "filt"),
        P("slab", None),
    )
    return jax.shard_map(
        shards,
        mesh=mesh,
        in_specs=placed,
        out_specs=(P(None, "filt", "slab"), P(None, "filt", "slab")),
        check_vma=False,
    )
```

```python
import functools

import jax
import jax.numpy as jnp
from jax import lax
from jax.experimental import pallas as pl
from jax.experimental.pallas import tpu as pltpu
from jax.sharding import PartitionSpec as P

WIDTH = 8
SHIFTS = [(b, e) for b in (-1, 0, 1) for e in (-1, 0, 1)]
LIMIT = 20 * 1024 * 1024
VMEM = pl.BlockSpec(memory_space=pltpu.VMEM)
ANY = pl.BlockSpec(memory_space=pl.ANY)


def swap(block, axis, step):
    count = lax.axis_size(axis)
    return lax.ppermute(block, axis, [(i, i ^ step) for i in range(count)])


def exchanged(block, axis):
    return swapped([block] * lax.axis_size(axis), axis, 1)


def swapped(blocks, axis, unit):
    return [blocks[0]] + [swap(blocks[step], axis, unit * step) for step in range(1, len(blocks))]


def halo(volume, own):
    count = lax.axis_size("slab")
    other = swap(volume, "slab", 1)
    passed = edge(other, [own])
    pairs = [(i, i + 2) for i in range(0, count - 2, 2)] + [(i, i - 2) for i in range(3, count, 2)]
    return other, lax.ppermute(passed, "slab", pairs)


def chips_apart(blocks):
    return swapped([None, *blocks], "slab", 2)[1:]


def every_chip(block):
    blocks = [block]
    for step in range(1, lax.axis_size("slab") // 2):
        low = step & -step
        blocks.append(swap(blocks[step ^ low], "slab", 2 * low))
    return blocks


def call(body, out_shape, cost, *operands, in_specs, scratch_shapes=(), passed=(), after=()):
    flops, moved = cost
    single = not isinstance(out_shape, list)
    outs = [out_shape] if single else out_shape
    first, second = len(operands), len(operands) + len(passed) + len(after)
    third = second + len(outs)

    def inner(*refs):
        body(*refs[:first], *refs[second:third], *refs[third + len(passed) :])

    given = pl.pallas_call(
        inner,
        out_shape=[*outs, *(struct(array.shape, array.dtype) for array in passed)],
        cost_estimate=pl.CostEstimate(flops=flops, bytes_accessed=moved, transcendentals=0),
        compiler_params=pltpu.CompilerParams(vmem_limit_bytes=LIMIT),
        in_specs=[*in_specs] + [ANY] * (len(passed) + len(after)),
        out_specs=[VMEM] * len(outs) + [ANY] * len(passed),
        scratch_shapes=list(scratch_shapes),
        input_output_aliases={first + i: len(outs) + i for i in range(len(passed))},
    )(*operands, *passed, *after)
    if passed:
        return [*given[: len(outs)], list(given[len(outs) :])]
    return given[0] if single else list(given)


def struct(shape, dtype):
    return jax.ShapeDtypeStruct(tuple(shape), dtype)


def here(axis):
    return lax.axis_index(axis).astype(jnp.int32)


def core():
    return lax.rem(here("slab"), 2)


def far_owners(side):
    me = here("slab")
    return [me ^ (2 * step) ^ side for step in range(lax.axis_size("slab") // 2)]


TOKEN = struct((8, 128), jnp.float32)


def stage_body(count, *refs):
    sources, targets, sems = refs[:count], refs[count : 2 * count], refs[2 * count]
    copies = [pltpu.make_async_copy(sources[i], targets[i], sems.at[i]) for i in range(count)]
    for copy in copies:
        copy.start()
    for copy in copies:
        copy.wait()


def stage(*arrays):
    count = len(arrays)
    return call(
        functools.partial(stage_body, count),
        [struct(array.shape, array.dtype) for array in arrays],
        (0, sum(4 * array.size for array in arrays)),
        *arrays,
        in_specs=[pl.BlockSpec(memory_space=pltpu.HBM)] * count,
        scratch_shapes=[pltpu.SemaphoreType.DMA((count,))],
    )


def inside(shape, axis, b, e):
    spot = lax.broadcasted_iota(jnp.int32, shape, axis)
    column = spot % WIDTH + e
    moved = spot + WIDTH * b
    return (column >= 0) & (column < WIDTH) & (moved >= 0) & (moved < shape[axis])


def shifted(values, axis, b, e):
    if b == 0 and e == 0:
        return values
    size = values.shape[axis]
    turned = pltpu.roll(values, (-(WIDTH * b + e)) % size, axis)
    return jnp.where(inside(values.shape, axis, b, e), turned, 0.0)


def fold_shifts(products):
    rows = products.shape[0] // len(SHIFTS)
    total = None
    for number, (b, e) in enumerate(SHIFTS):
        term = shifted(products[number * rows : (number + 1) * rows, :], 1, b, e)
        total = term if total is None else total + term
    return total


def dot(left, right):
    return jnp.dot(left, right, preferred_element_type=jnp.float32)


def edge_body(other_ref, out_ref):
    out_ref[0] = other_ref[(1 - core()) * (other_ref.shape[0] - 1)]


def edge(other, after):
    shape = (1, *other.shape[1:])
    return call(edge_body, struct(shape, other.dtype), (0, other.size), other, in_specs=[VMEM], after=after)


def halves(rows):
    return 2 if rows % 32 == 0 and lax.axis_size("filt") % 2 == 0 else 1


def assemble_body(count, split, *refs):
    parts, whole_ref, shares = refs[:count][::-1], refs[count], refs[count + 1 :]
    size = parts[0].shape[1]
    me, chip = here("filt"), here("slab") // 2
    for step in range(count):
        place = pl.ds(pl.multiple_of((me ^ step) * size, size), size)
        whole_ref[:, place, :] = parts[step][...]
    rows = shares[0].shape[2]
    for step, share_ref in enumerate(shares):
        for side in range(2):
            begin = (((chip ^ step) * 2 + side) * split + lax.rem(me, split)) * rows
            share_ref[side] = whole_ref[:, pl.ds(pl.multiple_of(begin, rows), rows), :]


def assemble(parts, after=()):
    planes, size, plane = parts[0].shape
    count, slabs = len(parts), lax.axis_size("slab")
    channels = size * count
    split = halves(channels // slabs)
    kind = parts[0].dtype
    outs = [struct((planes, channels, plane), kind)]
    outs += [struct((2, planes, channels // slabs // split, plane), kind)] * (slabs // 2)
    whole, *shares = call(
        functools.partial(assemble_body, count, split),
        outs,
        (0, 4 * planes * channels * plane),
        *parts[::-1],
        in_specs=[VMEM] * count,
        after=after,
    )
    return whole, shares


def crossing_body(count, *refs):
    planes = refs[0].shape[1]
    for step in range(count):
        for j in range(planes):
            refs[count][step * planes + j] = refs[step][1 - core(), j]


def collect_body(count, crossed_ref, *refs):
    owners, side = far_owners(0), core()
    planes = refs[0].shape[1]
    for step in range(count):
        for j in range(planes):
            refs[count][owners[step] * planes + j] = refs[step][side, j]
            refs[count][(owners[step] ^ 1) * planes + j] = crossed_ref[step * planes + j]


def collected(shares, after, later=()):
    count = len(shares)
    _, planes, rows, plane = shares[0].shape
    kind, size = shares[0].dtype, shares[0].size * count
    crossing = call(
        functools.partial(crossing_body, count),
        struct((count * planes, rows, plane), kind),
        (0, 2 * size),
        *shares,
        in_specs=[VMEM] * count,
        after=after,
    )
    return call(
        functools.partial(collect_body, count),
        struct((2 * count * planes, rows, plane), kind),
        (0, 4 * size),
        swap(crossing, "slab", 1), *shares,
        in_specs=[VMEM] * (1 + count),
        after=later,
    )


def both_halves(volume, split):
    return [volume] + ([swap(volume, "filt", 1)] if split == 2 else [])


def pack_body(count, *refs):
    out_ref = refs[count]
    blocks = refs[:count]
    row = 0
    for number in range(count):
        planes, plane, filters = blocks[number].shape
        for j in range(planes):
            for begin in range(0, plane, filters):
                out_ref[row : row + filters, begin : begin + filters] = blocks[number][j, begin : begin + filters, :]
            row += filters


def pack(blocks, after=()):
    plane = blocks[0].shape[1]
    total = sum(block.size for block in blocks)
    return call(
        functools.partial(pack_body, len(blocks)),
        struct((total // plane, plane), blocks[0].dtype),
        (0, 4 * total),
        *blocks,
        in_specs=[VMEM] * len(blocks),
        after=after,
    )


def taps(weight_ref, number):
    block = weight_ref[pl.ds(9 * number, 9)]
    return block.reshape(block.shape[0] * block.shape[1], block.shape[2])


def forward_own_body(planes, volume_ref, weight_ref, out_ref, acc_ref):
    for a in (0, 1, -1):
        weight = taps(weight_ref, a + 1)
        for j in range(planes):
            if 0 <= j + a < planes:
                product = dot(weight, volume_ref[j + a])
                acc_ref[j] = product if a == 0 else acc_ref[j] + product
    for j in range(planes):
        out_ref[j] = fold_shifts(acc_ref.at[j])


def forward_own(volume, weight):
    planes, channels, plane = volume.shape
    filters = weight.shape[1]
    return call(
        functools.partial(forward_own_body, planes),
        struct((planes, filters, plane), jnp.float32),
        (2 * 9 * filters * channels * plane * (3 * planes - 2), weight.size * 2),
        volume, weight,
        in_specs=[VMEM] * 2,
        scratch_shapes=[pltpu.VMEM((planes, 9 * filters, plane), jnp.float32)],
    )


def forward_other_body(planes, other_ref, weight_ref, own_ref, out_ref, acc_ref):
    up, last = core(), planes - 1
    place = (1 - up) * last
    acc_ref[...] = dot(taps(weight_ref, 2 * (1 - up)), other_ref[up * last])
    out_ref[...] = own_ref[...]
    out_ref[place] = out_ref[place] + fold_shifts(acc_ref)


def forward_other(other, weight, own):
    planes, filters, plane = own.shape
    return call(
        functools.partial(forward_other_body, planes),
        struct(own.shape, jnp.float32),
        (2 * weight.size // 3 * plane, weight.size * 2 // 3),
        other, weight, own,
        in_specs=[VMEM] * 3,
        scratch_shapes=[pltpu.VMEM((9 * filters, plane), jnp.float32)],
    )


def silu_and_slope(values):
    sig = 1.0 / (1.0 + jnp.exp(-values))
    return values * sig, sig * (1.0 + values * (1.0 - sig))


def forward_rest_body(planes, beyond_ref, weight_ref, own_ref, *refs):
    head_ref = refs[0] if len(refs) == 5 else None
    slope_ref, made_ref, acc_ref, total_ref = refs[-4:]
    up = core()
    place = up * (planes - 1)
    total_ref[...] = own_ref[...]
    acc_ref[...] = dot(taps(weight_ref, 2 * up), beyond_ref[0])
    total_ref[place] = total_ref[place] + fold_shifts(acc_ref)
    for j in range(planes):
        value, slope = silu_and_slope(total_ref[j])
        value = value.astype(jnp.bfloat16)
        slope_ref[j] = slope.T if head_ref is None else slope
        made_ref[j] = value if head_ref is None else dot(head_ref[...], value)


def forward_rest(beyond, weight, own, after, head=None):
    planes, filters, plane = own.shape
    channels = weight.shape[2]
    ins = [beyond, weight, own]
    slope = own.shape
    if head is None:
        slope = (planes, plane, filters)
        made = struct(own.shape, jnp.bfloat16)
    else:
        ins.append(head)
        made = struct((planes, head.shape[0], plane), jnp.float32)
    return call(
        functools.partial(forward_rest_body, planes),
        [struct(slope, jnp.float32), made],
        (2 * 9 * filters * channels * plane, weight.size * 2 // 3),
        *ins,
        in_specs=[VMEM] * len(ins),
        scratch_shapes=[
            pltpu.VMEM((9 * filters, plane), jnp.float32),
            pltpu.VMEM(own.shape, jnp.float32),
        ],
        after=after,
    )


def loss_body(count, labels_ref, head_ref, slope_ref, *refs):
    parts, grad_ref = refs[:count][::-1], refs[count]
    for j in range(grad_ref.shape[0]):
        logits = parts[0][j]
        for part in parts[1:]:
            logits = logits + part[j]
        powers = jnp.exp(logits)
        likely = powers / jnp.sum(powers, axis=0, keepdims=True)
        classes = lax.broadcasted_iota(jnp.int32, logits.shape, 0)
        onehot = (labels_ref[j : j + 1, :] == classes).astype(jnp.float32)
        logit_grad = (likely - onehot).astype(jnp.bfloat16).astype(jnp.float32)
        back = lax.dot_general(
            head_ref[...].astype(jnp.float32),
            logit_grad,
            (((0,), (0,)), ((), ())),
            preferred_element_type=jnp.float32,
        )
        grad_ref[j] = (back * slope_ref[j]).T.astype(jnp.bfloat16)


def loss_grad(parts, labels, head, slope, after):
    planes, plane = labels.shape
    return call(
        functools.partial(loss_body, len(parts)),
        struct((planes, plane, slope.shape[1]), jnp.bfloat16),
        (2 * slope.size * head.shape[0], slope.size * 6),
        labels, head, slope, *parts[::-1],
        in_specs=[VMEM] * (3 + len(parts)),
        after=after,
    )


def spread_back(grad, spread_ref):
    filters = grad.shape[1]
    turned = grad.astype(jnp.float32)
    for number, (b, e) in enumerate(SHIFTS):
        moved = shifted(turned, 0, -b, -e).astype(jnp.bfloat16)
        spread_ref[:, number * filters : (number + 1) * filters] = moved


def backward_own_body(planes, grad_ref, weight_ref, out_ref, spread_ref):
    for j in range(planes):
        spread_back(grad_ref[j], spread_ref.at[j])
    for a in (0, 1, -1):
        weight = taps(weight_ref, a + 1)
        for j in range(planes):
            if 0 <= j - a < planes:
                product = dot(spread_ref[j - a], weight)
                out_ref[j] = product if a == 0 else out_ref[j] + product


def backward_own(grad, weight):
    planes, plane, filters = grad.shape
    channels = weight.shape[2]
    return call(
        functools.partial(backward_own_body, planes),
        struct((planes, plane, channels), jnp.float32),
        (2 * 9 * filters * channels * plane * (3 * planes - 2), weight.size * 2),
        grad, weight,
        in_specs=[VMEM] * 2,
        scratch_shapes=[pltpu.VMEM((planes, plane, 9 * filters), jnp.bfloat16)],
    )


def backward_other_body(planes, other_ref, weight_ref, own_ref, out_ref, spread_ref):
    up, last = core(), planes - 1
    place = (1 - up) * last
    spread_back(other_ref[up * last], spread_ref)
    out_ref[...] = own_ref[...]
    out_ref[place] = out_ref[place] + dot(spread_ref[...], taps(weight_ref, 2 * up))


def backward_other(other, weight, own):
    planes, plane, _ = own.shape
    filters = weight.shape[1]
    return call(
        functools.partial(backward_other_body, planes),
        struct(own.shape, jnp.float32),
        (2 * weight.size // 3 * plane, weight.size * 2 // 3),
        other, weight, own,
        in_specs=[VMEM] * 3,
        scratch_shapes=[pltpu.VMEM((plane, 9 * filters), jnp.bfloat16)],
    )


def backward_rest_body(planes, count, beyond_ref, weight_ref, own_ref, *refs):
    kept_ref, sent, (spread_ref, total_ref) = refs[0], refs[1:count], refs[count:]
    size = kept_ref.shape[2]
    up, me = core(), here("filt")
    place = up * (planes - 1)
    spread_back(beyond_ref[0], spread_ref)
    product = dot(spread_ref[...], taps(weight_ref, 2 * (1 - up)))
    for block in range(count):
        columns = slice(block * size, (block + 1) * size)
        for j in range(planes):
            total_ref[block, j] = own_ref[j, :, columns]
        total_ref[block, place] = total_ref[block, place] + product[:, columns]
    kept_ref[...] = total_ref[me]
    for number in range(1, count):
        sent[number - 1][...] = total_ref[me ^ number].astype(jnp.bfloat16)


def backward_rest(beyond, weight, own, count, after):
    planes, plane, channels = own.shape
    filters = weight.shape[1]
    size = channels // count
    outs = [struct((planes, plane, size), jnp.float32)]
    outs += [struct((planes, plane, size), jnp.bfloat16)] * (count - 1)
    return call(
        functools.partial(backward_rest_body, planes, count),
        outs,
        (2 * 9 * filters * channels * plane, weight.size * 2 // 3),
        beyond, weight, own,
        in_specs=[VMEM] * 3,
        scratch_shapes=[
            pltpu.VMEM((plane, 9 * filters), jnp.bfloat16),
            pltpu.VMEM((count, planes, plane, size), jnp.float32),
        ],
        after=after,
    )


def first_grad_body(count, slope_ref, *refs):
    parts, out_ref = refs[:count], refs[count]
    for j in range(out_ref.shape[0]):
        total = parts[0][j]
        for part in parts[1:]:
            total = total + part[j].astype(jnp.float32)
        out_ref[j] = (total * slope_ref[j]).astype(jnp.bfloat16)


def first_out(parts, slope, after):
    return call(
        functools.partial(first_grad_body, len(parts)),
        struct(slope.shape, jnp.bfloat16),
        (slope.size * 4, slope.size * 14),
        slope, *parts,
        in_specs=[VMEM] * (1 + len(parts)),
        after=after,
    )


def spread_body(split, *refs):
    spread_ref, token_ref = refs[split:]
    token_ref[...] = jnp.zeros_like(token_ref)
    depth, rows, plane = refs[0].shape
    me = lax.rem(here("filt"), split)
    for d in range(depth):
        for half in range(split):
            values = refs[half][d].astype(jnp.float32)
            for number, (b, e) in enumerate(SHIFTS):
                begin = (number * split + (me ^ half)) * rows
                moved = shifted(values, 1, b, e).astype(jnp.bfloat16)
                spread_ref[pl.ds(pl.multiple_of(begin, rows), rows), d * plane : (d + 1) * plane] = moved


def spread(halved):
    split = len(halved)
    depth, rows, plane = halved[0].shape
    channels = split * rows
    return call(
        functools.partial(spread_body, split),
        [struct((9 * channels, depth * plane), jnp.bfloat16), TOKEN],
        (9 * channels * depth * plane, 10 * channels * depth * plane),
        *halved,
        in_specs=[VMEM] * split,
    )


def weight_grad_body(count, second, spread_ref, crossed_ref, *refs):
    parts, (out_ref, token_ref, grad_ref) = refs[:count], refs[count:]
    token_ref[...] = jnp.zeros_like(token_ref)
    planes, plane, filters = parts[0].shape
    channels = spread_ref.shape[0] // 9
    depth = spread_ref.shape[1] // plane
    zero = jnp.zeros((plane, filters), jnp.bfloat16)
    grad_ref[depth * plane : (depth + 1) * plane, : filters] = zero
    grad_ref[plane : 2 * plane, 2 * filters :] = zero

    def one(block, d, begin):
        rows = block.shape[0]
        for a in (-1, 0, 1):
            place = pl.ds(pl.multiple_of((d + a + 1) * plane + begin, rows), rows)
            grad_ref[place, (a + 1) * filters : (a + 2) * filters] = block

    near, far = far_owners(0), far_owners(1)
    owners = [near[0], far[0], *near[1:], *far[1:]] if second else near + far
    row = 0
    for number in range(count):
        for j in range(planes):
            one(parts[number][j], owners[number] * planes + j, 0)
    for number in range(count, len(owners)):
        for j in range(planes):
            for begin in range(0, plane, filters):
                block = crossed_ref[row : row + filters, begin : begin + filters]
                one(block, owners[number] * planes + j, begin)
            row += filters

    product = dot(spread_ref[...], grad_ref[plane : (depth + 1) * plane, :])
    for r in range(3):
        for number in range(9):
            out_ref[r * 9 + number] = product[
                number * channels : (number + 1) * channels, r * filters : (r + 1) * filters
            ]


def weight_grad(spreads, blocks, crossed, second):
    channels, columns = spreads.shape[0] // 9, spreads.shape[1]
    _, plane, filters = blocks[0].shape
    return call(
        functools.partial(weight_grad_body, len(blocks), second),
        [struct((27, channels, filters), jnp.float32), TOKEN],
        (2 * 27 * filters * channels * columns, 27 * channels * filters * 4 + spreads.size * 2),
        spreads, crossed, *blocks,
        in_specs=[VMEM] * (2 + len(blocks)),
        scratch_shapes=[pltpu.VMEM((columns + 2 * plane, 3 * filters), jnp.bfloat16)],
    )


def shards(features, first_weight, second_weight, head_weight, labels):
    count = lax.axis_size("filt")
    chips = lax.axis_size("slab") // 2
    split = halves(features.shape[1] * count // lax.axis_size("slab"))
    near, first_weight, head_weight = stage(features, first_weight, head_weight)
    all_in, share_in = assemble([near] + exchanged(features, "filt")[1:])
    own = forward_own(all_in, first_weight)
    share_in = [share_in[0]] + chips_apart(share_in[1:])
    other, beyond = halo(all_in, own)
    own = forward_other(other, first_weight, own)
    slope_first, hidden = forward_rest(beyond, first_weight, own, share_in[1:])

    halved_in = collected(share_in, [hidden])
    all_hidden, share_hidden = assemble(exchanged(hidden, "filt"), [halved_in])
    own = forward_own(all_hidden, second_weight)
    share_hidden = [share_hidden[0]] + chips_apart(share_hidden[1:])
    other, beyond = halo(all_hidden, own)
    own = forward_other(other, second_weight, own)
    halved_in = both_halves(halved_in, split)
    slope_second, logits = forward_rest(beyond, second_weight, own, share_hidden[1:] + halved_in, head_weight)

    logits_parts = exchanged(logits, "filt")
    second_out = loss_grad(logits_parts, labels, head_weight, slope_second, [])
    halved_hidden = both_halves(collected(share_hidden, [logits], [second_out]), split)
    own = backward_own(second_out, second_weight)
    second_other, beyond = halo(second_out, own)
    second_far = every_chip(second_out)[1:]
    own = backward_other(second_other, second_weight, own)
    due = halved_hidden + second_far[chips // 2 - 1 : chips // 2]
    kept, *sent = backward_rest(beyond, second_weight, own, count, due)
    parts = swapped([kept, *sent], "filt", 1)
    spread_in, token_in = spread(halved_in)
    spread_hidden, token_hidden = spread(halved_hidden)
    first_out_grad = first_out(parts, slope_first, [token_in, token_hidden, *second_far])

    first_blocks = [first_out_grad] + chips_apart([first_out_grad] * (chips - 1))
    crossed = swap(pack(second_far, [first_out_grad]), "slab", 1)
    second_blocks = [second_out, second_other] + second_far
    second_grad, token = weight_grad(spread_hidden, second_blocks, crossed, True)
    crossed = swap(pack(first_blocks, [token]), "slab", 1)
    first_grad, _ = weight_grad(spread_in, first_blocks, crossed, False)
    return jnp.transpose(first_grad, (0, 2, 1)), jnp.transpose(second_grad, (0, 2, 1))


def solution(mesh):
    placed = (
        P("slab", "filt", None),
        P(None, "filt", None),
        P(None, "filt", None),
        P(None, "filt"),
        P("slab", None),
    )
    return jax.shard_map(
        shards,
        mesh=mesh,
        in_specs=placed,
        out_specs=(P(None, "filt", "slab"), P(None, "filt", "slab")),
        check_vma=False,
    )
```

```python
import functools

import jax
import jax.numpy as jnp
from jax import lax
from jax.experimental import pallas as pl
from jax.experimental.pallas import tpu as pltpu
from jax.sharding import PartitionSpec as P

WIDTH = 8
SHIFTS = [(b, e) for b in (-1, 0, 1) for e in (-1, 0, 1)]
LIMIT = 20 * 1024 * 1024
VMEM = pl.BlockSpec(memory_space=pltpu.VMEM)
ANY = pl.BlockSpec(memory_space=pl.ANY)


def swap(block, axis, step):
    count = lax.axis_size(axis)
    return lax.ppermute(block, axis, [(i, i ^ step) for i in range(count)])


def exchanged(block, axis):
    return swapped([block] * lax.axis_size(axis), axis, 1)


def swapped(blocks, axis, unit):
    return [blocks[0]] + [swap(blocks[step], axis, unit * step) for step in range(1, len(blocks))]


def halo(volume, own):
    count = lax.axis_size("slab")
    other = swap(volume, "slab", 1)
    passed = edge(other, [own])
    pairs = [(i, i + 2) for i in range(0, count - 2, 2)] + [(i, i - 2) for i in range(3, count, 2)]
    return other, lax.ppermute(passed, "slab", pairs)


def chips_apart(blocks):
    return swapped([None, *blocks], "slab", 2)[1:]


def every_chip(block):
    blocks = [block]
    for step in range(1, lax.axis_size("slab") // 2):
        low = step & -step
        blocks.append(swap(blocks[step ^ low], "slab", 2 * low))
    return blocks


def call(body, out_shape, cost, *operands, in_specs, scratch_shapes=(), passed=(), after=()):
    flops, moved = cost
    single = not isinstance(out_shape, list)
    outs = [out_shape] if single else out_shape
    first, second = len(operands), len(operands) + len(passed) + len(after)
    third = second + len(outs)

    def inner(*refs):
        body(*refs[:first], *refs[second:third], *refs[third + len(passed) :])

    given = pl.pallas_call(
        inner,
        out_shape=[*outs, *(struct(array.shape, array.dtype) for array in passed)],
        cost_estimate=pl.CostEstimate(flops=flops, bytes_accessed=moved, transcendentals=0),
        compiler_params=pltpu.CompilerParams(vmem_limit_bytes=LIMIT),
        in_specs=[*in_specs] + [ANY] * (len(passed) + len(after)),
        out_specs=[VMEM] * len(outs) + [ANY] * len(passed),
        scratch_shapes=list(scratch_shapes),
        input_output_aliases={first + i: len(outs) + i for i in range(len(passed))},
    )(*operands, *passed, *after)
    if passed:
        return [*given[: len(outs)], list(given[len(outs) :])]
    return given[0] if single else list(given)


def struct(shape, dtype):
    return jax.ShapeDtypeStruct(tuple(shape), dtype)


def here(axis):
    return lax.axis_index(axis).astype(jnp.int32)


def core():
    return lax.rem(here("slab"), 2)


def far_owners(side):
    me = here("slab")
    return [me ^ (2 * step) ^ side for step in range(lax.axis_size("slab") // 2)]


TOKEN = struct((8, 128), jnp.float32)


def stage_body(count, *refs):
    sources, targets, sems = refs[:count], refs[count : 2 * count], refs[2 * count]
    copies = [pltpu.make_async_copy(sources[i], targets[i], sems.at[i]) for i in range(count)]
    for copy in copies:
        copy.start()
    for copy in copies:
        copy.wait()


def stage(*arrays):
    count = len(arrays)
    return call(
        functools.partial(stage_body, count),
        [struct(array.shape, array.dtype) for array in arrays],
        (0, sum(4 * array.size for array in arrays)),
        *arrays,
        in_specs=[pl.BlockSpec(memory_space=pltpu.HBM)] * count,
        scratch_shapes=[pltpu.SemaphoreType.DMA((count,))],
    )


def inside(shape, axis, b, e):
    spot = lax.broadcasted_iota(jnp.int32, shape, axis)
    column = spot % WIDTH + e
    moved = spot + WIDTH * b
    return (column >= 0) & (column < WIDTH) & (moved >= 0) & (moved < shape[axis])


def shifted(values, axis, b, e):
    if b == 0 and e == 0:
        return values
    size = values.shape[axis]
    turned = pltpu.roll(values, (-(WIDTH * b + e)) % size, axis)
    return jnp.where(inside(values.shape, axis, b, e), turned, 0.0)


def fold_shifts(products):
    rows = products.shape[0] // len(SHIFTS)
    total = None
    for number, (b, e) in enumerate(SHIFTS):
        term = shifted(products[number * rows : (number + 1) * rows, :], 1, b, e)
        total = term if total is None else total + term
    return total


def dot(left, right):
    return jnp.dot(left, right, preferred_element_type=jnp.float32)


def edge_body(other_ref, out_ref):
    out_ref[0] = other_ref[(1 - core()) * (other_ref.shape[0] - 1)]


def edge(other, after):
    shape = (1, *other.shape[1:])
    return call(edge_body, struct(shape, other.dtype), (0, other.size), other, in_specs=[VMEM], after=after)


def halves(rows):
    return 2 if rows % 32 == 0 and lax.axis_size("filt") % 2 == 0 else 1


def assemble_body(count, split, *refs):
    parts, whole_ref, shares = refs[:count][::-1], refs[count], refs[count + 1 :]
    size = parts[0].shape[1]
    me, chip = here("filt"), here("slab") // 2
    for step in range(count):
        place = pl.ds(pl.multiple_of((me ^ step) * size, size), size)
        whole_ref[:, place, :] = parts[step][...]
    rows = shares[0].shape[2]
    for step, share_ref in enumerate(shares):
        for side in range(2):
            begin = (((chip ^ step) * 2 + side) * split + lax.rem(me, split)) * rows
            share_ref[side] = whole_ref[:, pl.ds(pl.multiple_of(begin, rows), rows), :]


def assemble(parts, after=()):
    planes, size, plane = parts[0].shape
    count, slabs = len(parts), lax.axis_size("slab")
    channels = size * count
    split = halves(channels // slabs)
    kind = parts[0].dtype
    outs = [struct((planes, channels, plane), kind)]
    outs += [struct((2, planes, channels // slabs // split, plane), kind)] * (slabs // 2)
    whole, *shares = call(
        functools.partial(assemble_body, count, split),
        outs,
        (0, 4 * planes * channels * plane),
        *parts[::-1],
        in_specs=[VMEM] * count,
        after=after,
    )
    return whole, shares


def crossing_body(count, *refs):
    planes = refs[0].shape[1]
    for step in range(count):
        for j in range(planes):
            refs[count][step * planes + j] = refs[step][1 - core(), j]


def collect_body(count, crossed_ref, *refs):
    owners, side = far_owners(0), core()
    planes = refs[0].shape[1]
    out_ref = refs[-1]
    base = out_ref.shape[0] - 2 * count * planes
    if base > 0:
        out_ref[:base] = refs[count][...]
    for step in range(count):
        for j in range(planes):
            out_ref[base + owners[step] * planes + j] = refs[step][side, j]
            out_ref[base + (owners[step] ^ 1) * planes + j] = crossed_ref[step * planes + j]


def collected(shares, after, later=(), earlier=()):
    count = len(shares)
    _, planes, rows, plane = shares[0].shape
    kind, size = shares[0].dtype, shares[0].size * count
    crossing = call(
        functools.partial(crossing_body, count),
        struct((count * planes, rows, plane), kind),
        (0, 2 * size),
        *shares,
        in_specs=[VMEM] * count,
        after=after,
    )
    return call(
        functools.partial(collect_body, count),
        struct((2 * count * planes * (1 + len(earlier)), rows, plane), kind),
        (0, 4 * size),
        swap(crossing, "slab", 1), *shares, *earlier,
        in_specs=[VMEM] * (1 + count + len(earlier)),
        after=later,
    )


def both_halves(volume, split):
    return [volume] + ([swap(volume, "filt", 1)] if split == 2 else [])


def pack_body(count, *refs):
    out_ref = refs[count]
    blocks = refs[:count]
    row = 0
    for number in range(count):
        planes, plane, filters = blocks[number].shape
        for j in range(planes):
            for begin in range(0, plane, filters):
                out_ref[row : row + filters, begin : begin + filters] = blocks[number][j, begin : begin + filters, :]
            row += filters


def pack(blocks, after=()):
    plane = blocks[0].shape[1]
    total = sum(block.size for block in blocks)
    return call(
        functools.partial(pack_body, len(blocks)),
        struct((total // plane, plane), blocks[0].dtype),
        (0, 4 * total),
        *blocks,
        in_specs=[VMEM] * len(blocks),
        after=after,
    )


def taps(weight_ref, number):
    block = weight_ref[pl.ds(9 * number, 9)]
    return block.reshape(block.shape[0] * block.shape[1], block.shape[2])


def forward_own_body(planes, volume_ref, weight_ref, out_ref, acc_ref):
    for a in (0, 1, -1):
        weight = taps(weight_ref, a + 1)
        for j in range(planes):
            if 0 <= j + a < planes:
                product = dot(weight, volume_ref[j + a])
                acc_ref[j] = product if a == 0 else acc_ref[j] + product
    for j in range(planes):
        out_ref[j] = fold_shifts(acc_ref.at[j])


def forward_own(volume, weight):
    planes, channels, plane = volume.shape
    filters = weight.shape[1]
    return call(
        functools.partial(forward_own_body, planes),
        struct((planes, filters, plane), jnp.float32),
        (2 * 9 * filters * channels * plane * (3 * planes - 2), weight.size * 2),
        volume, weight,
        in_specs=[VMEM] * 2,
        scratch_shapes=[pltpu.VMEM((planes, 9 * filters, plane), jnp.float32)],
    )


def forward_other_body(planes, other_ref, weight_ref, own_ref, out_ref, acc_ref):
    up, last = core(), planes - 1
    place = (1 - up) * last
    acc_ref[...] = dot(taps(weight_ref, 2 * (1 - up)), other_ref[up * last])
    out_ref[...] = own_ref[...]
    out_ref[place] = out_ref[place] + fold_shifts(acc_ref)


def forward_other(other, weight, own):
    planes, filters, plane = own.shape
    return call(
        functools.partial(forward_other_body, planes),
        struct(own.shape, jnp.float32),
        (2 * weight.size // 3 * plane, weight.size * 2 // 3),
        other, weight, own,
        in_specs=[VMEM] * 3,
        scratch_shapes=[pltpu.VMEM((9 * filters, plane), jnp.float32)],
    )


def silu_and_slope(values):
    sig = 1.0 / (1.0 + jnp.exp(-values))
    return values * sig, sig * (1.0 + values * (1.0 - sig))


def forward_rest_body(planes, beyond_ref, weight_ref, own_ref, *refs):
    head_ref = refs[0] if len(refs) == 5 else None
    slope_ref, made_ref, acc_ref, total_ref = refs[-4:]
    up = core()
    place = up * (planes - 1)
    total_ref[...] = own_ref[...]
    acc_ref[...] = dot(taps(weight_ref, 2 * up), beyond_ref[0])
    total_ref[place] = total_ref[place] + fold_shifts(acc_ref)
    for j in range(planes):
        value, slope = silu_and_slope(total_ref[j])
        value = value.astype(jnp.bfloat16)
        slope_ref[j] = slope.T if head_ref is None else slope
        made_ref[j] = value if head_ref is None else dot(head_ref[...], value)


def forward_rest(beyond, weight, own, after, head=None):
    planes, filters, plane = own.shape
    channels = weight.shape[2]
    ins = [beyond, weight, own]
    slope = own.shape
    if head is None:
        slope = (planes, plane, filters)
        made = struct(own.shape, jnp.bfloat16)
    else:
        ins.append(head)
        made = struct((planes, head.shape[0], plane), jnp.float32)
    return call(
        functools.partial(forward_rest_body, planes),
        [struct(slope, jnp.float32), made],
        (2 * 9 * filters * channels * plane, weight.size * 2 // 3),
        *ins,
        in_specs=[VMEM] * len(ins),
        scratch_shapes=[
            pltpu.VMEM((9 * filters, plane), jnp.float32),
            pltpu.VMEM(own.shape, jnp.float32),
        ],
        after=after,
    )


def loss_body(count, labels_ref, head_ref, slope_ref, *refs):
    parts, grad_ref = refs[:count][::-1], refs[count]
    for j in range(grad_ref.shape[0]):
        logits = parts[0][j]
        for part in parts[1:]:
            logits = logits + part[j]
        powers = jnp.exp(logits)
        likely = powers / jnp.sum(powers, axis=0, keepdims=True)
        classes = lax.broadcasted_iota(jnp.int32, logits.shape, 0)
        onehot = (labels_ref[j : j + 1, :] == classes).astype(jnp.float32)
        logit_grad = (likely - onehot).astype(jnp.bfloat16).astype(jnp.float32)
        back = lax.dot_general(
            head_ref[...].astype(jnp.float32),
            logit_grad,
            (((0,), (0,)), ((), ())),
            preferred_element_type=jnp.float32,
        )
        grad_ref[j] = (back * slope_ref[j]).T.astype(jnp.bfloat16)


def loss_grad(parts, labels, head, slope, after):
    planes, plane = labels.shape
    return call(
        functools.partial(loss_body, len(parts)),
        struct((planes, plane, slope.shape[1]), jnp.bfloat16),
        (2 * slope.size * head.shape[0], slope.size * 6),
        labels, head, slope, *parts[::-1],
        in_specs=[VMEM] * (3 + len(parts)),
        after=after,
    )


def spread_back(grad, spread_ref):
    filters = grad.shape[1]
    turned = grad.astype(jnp.float32)
    for number, (b, e) in enumerate(SHIFTS):
        moved = shifted(turned, 0, -b, -e).astype(jnp.bfloat16)
        spread_ref[:, number * filters : (number + 1) * filters] = moved


def backward_own_body(planes, grad_ref, weight_ref, out_ref, spread_ref):
    for j in range(planes):
        spread_back(grad_ref[j], spread_ref.at[j])
    for a in (0, 1, -1):
        weight = taps(weight_ref, a + 1)
        for j in range(planes):
            if 0 <= j - a < planes:
                product = dot(spread_ref[j - a], weight)
                out_ref[j] = product if a == 0 else out_ref[j] + product


def backward_own(grad, weight):
    planes, plane, filters = grad.shape
    channels = weight.shape[2]
    return call(
        functools.partial(backward_own_body, planes),
        struct((planes, plane, channels), jnp.float32),
        (2 * 9 * filters * channels * plane * (3 * planes - 2), weight.size * 2),
        grad, weight,
        in_specs=[VMEM] * 2,
        scratch_shapes=[pltpu.VMEM((planes, plane, 9 * filters), jnp.bfloat16)],
    )


def backward_other_body(planes, other_ref, weight_ref, own_ref, out_ref, spread_ref):
    up, last = core(), planes - 1
    place = (1 - up) * last
    spread_back(other_ref[up * last], spread_ref)
    out_ref[...] = own_ref[...]
    out_ref[place] = out_ref[place] + dot(spread_ref[...], taps(weight_ref, 2 * up))


def backward_other(other, weight, own):
    planes, plane, _ = own.shape
    filters = weight.shape[1]
    return call(
        functools.partial(backward_other_body, planes),
        struct(own.shape, jnp.float32),
        (2 * weight.size // 3 * plane, weight.size * 2 // 3),
        other, weight, own,
        in_specs=[VMEM] * 3,
        scratch_shapes=[pltpu.VMEM((plane, 9 * filters), jnp.bfloat16)],
    )


def backward_rest_body(planes, count, beyond_ref, weight_ref, own_ref, *refs):
    kept_ref, sent, (spread_ref, total_ref) = refs[0], refs[1:count], refs[count:]
    size = kept_ref.shape[2]
    up, me = core(), here("filt")
    place = up * (planes - 1)
    spread_back(beyond_ref[0], spread_ref)
    product = dot(spread_ref[...], taps(weight_ref, 2 * (1 - up)))
    for block in range(count):
        columns = slice(block * size, (block + 1) * size)
        for j in range(planes):
            total_ref[block, j] = own_ref[j, :, columns]
        total_ref[block, place] = total_ref[block, place] + product[:, columns]
    kept_ref[...] = total_ref[me]
    for number in range(1, count):
        sent[number - 1][...] = total_ref[me ^ number].astype(jnp.bfloat16)


def backward_rest(beyond, weight, own, count, after):
    planes, plane, channels = own.shape
    filters = weight.shape[1]
    size = channels // count
    outs = [struct((planes, plane, size), jnp.float32)]
    outs += [struct((planes, plane, size), jnp.bfloat16)] * (count - 1)
    return call(
        functools.partial(backward_rest_body, planes, count),
        outs,
        (2 * 9 * filters * channels * plane, weight.size * 2 // 3),
        beyond, weight, own,
        in_specs=[VMEM] * 3,
        scratch_shapes=[
            pltpu.VMEM((plane, 9 * filters), jnp.bfloat16),
            pltpu.VMEM((count, planes, plane, size), jnp.float32),
        ],
        after=after,
    )


def first_grad_body(count, slope_ref, *refs):
    parts, out_ref = refs[:count], refs[count]
    for j in range(out_ref.shape[0]):
        total = parts[0][j]
        for part in parts[1:]:
            total = total + part[j].astype(jnp.float32)
        out_ref[j] = (total * slope_ref[j]).astype(jnp.bfloat16)


def first_out(parts, slope, after):
    return call(
        functools.partial(first_grad_body, len(parts)),
        struct(slope.shape, jnp.bfloat16),
        (slope.size * 4, slope.size * 14),
        slope, *parts,
        in_specs=[VMEM] * (1 + len(parts)),
        after=after,
    )


def spread_body(split, first, *refs):
    spread_ref, token_ref = refs[split:]
    token_ref[...] = jnp.zeros_like(token_ref)
    both, rows, plane = refs[0].shape
    depth = both // 2
    me = lax.rem(here("filt"), split)
    for d in range(depth):
        for half in range(split):
            values = refs[half][first * depth + d].astype(jnp.float32)
            for number, (b, e) in enumerate(SHIFTS):
                begin = (number * split + (me ^ half)) * rows
                moved = shifted(values, 1, b, e).astype(jnp.bfloat16)
                spread_ref[pl.ds(pl.multiple_of(begin, rows), rows), d * plane : (d + 1) * plane] = moved


def spread(halved, first):
    split = len(halved)
    both, rows, plane = halved[0].shape
    depth = both // 2
    channels = split * rows
    return call(
        functools.partial(spread_body, split, first),
        [struct((9 * channels, depth * plane), jnp.bfloat16), TOKEN],
        (9 * channels * depth * plane, 10 * channels * depth * plane),
        *halved,
        in_specs=[VMEM] * split,
    )


def weight_grad_body(count, second, spread_ref, crossed_ref, *refs):
    parts, (out_ref, token_ref, grad_ref) = refs[:count], refs[count:]
    token_ref[...] = jnp.zeros_like(token_ref)
    planes, plane, filters = parts[0].shape
    channels = spread_ref.shape[0] // 9
    depth = spread_ref.shape[1] // plane
    zero = jnp.zeros((plane, filters), jnp.bfloat16)
    grad_ref[depth * plane : (depth + 1) * plane, : filters] = zero
    grad_ref[plane : 2 * plane, 2 * filters :] = zero

    def one(block, d, begin):
        rows = block.shape[0]
        for a in (-1, 0, 1):
            place = pl.ds(pl.multiple_of((d + a + 1) * plane + begin, rows), rows)
            grad_ref[place, (a + 1) * filters : (a + 2) * filters] = block

    near, far = far_owners(0), far_owners(1)
    owners = [near[0], far[0], *near[1:], *far[1:]] if second else near + far
    row = 0
    for number in range(count):
        for j in range(planes):
            one(parts[number][j], owners[number] * planes + j, 0)
    for number in range(count, len(owners)):
        for j in range(planes):
            for begin in range(0, plane, filters):
                block = crossed_ref[row : row + filters, begin : begin + filters]
                one(block, owners[number] * planes + j, begin)
            row += filters

    product = dot(spread_ref[...], grad_ref[plane : (depth + 1) * plane, :])
    for r in range(3):
        for number in range(9):
            out_ref[r * 9 + number] = product[
                number * channels : (number + 1) * channels, r * filters : (r + 1) * filters
            ]


def weight_grad(spreads, blocks, crossed, second):
    channels, columns = spreads.shape[0] // 9, spreads.shape[1]
    _, plane, filters = blocks[0].shape
    return call(
        functools.partial(weight_grad_body, len(blocks), second),
        [struct((27, channels, filters), jnp.float32), TOKEN],
        (2 * 27 * filters * channels * columns, 27 * channels * filters * 4 + spreads.size * 2),
        spreads, crossed, *blocks,
        in_specs=[VMEM] * (2 + len(blocks)),
        scratch_shapes=[pltpu.VMEM((columns + 2 * plane, 3 * filters), jnp.bfloat16)],
    )


def shards(features, first_weight, second_weight, head_weight, labels):
    count = lax.axis_size("filt")
    chips = lax.axis_size("slab") // 2
    split = halves(features.shape[1] * count // lax.axis_size("slab"))
    near, first_weight, head_weight = stage(features, first_weight, head_weight)
    all_in, share_in = assemble([near] + exchanged(features, "filt")[1:])
    own = forward_own(all_in, first_weight)
    share_in = [share_in[0]] + chips_apart(share_in[1:])
    other, beyond = halo(all_in, own)
    own = forward_other(other, first_weight, own)
    slope_first, hidden = forward_rest(beyond, first_weight, own, share_in[1:])

    halved_in = collected(share_in, [hidden])
    all_hidden, share_hidden = assemble(exchanged(hidden, "filt"), [halved_in])
    own = forward_own(all_hidden, second_weight)
    share_hidden = [share_hidden[0]] + chips_apart(share_hidden[1:])
    other, beyond = halo(all_hidden, own)
    own = forward_other(other, second_weight, own)
    slope_second, logits = forward_rest(beyond, second_weight, own, share_hidden[1:], head_weight)

    logits_parts = exchanged(logits, "filt")
    second_out = loss_grad(logits_parts, labels, head_weight, slope_second, [])
    halved = both_halves(collected(share_hidden, [logits], [second_out], [halved_in]), split)
    own = backward_own(second_out, second_weight)
    second_other, beyond = halo(second_out, own)
    second_far = every_chip(second_out)[1:]
    own = backward_other(second_other, second_weight, own)
    due = halved[:1] + second_far[chips // 2 - 1 : chips // 2]
    kept, *sent = backward_rest(beyond, second_weight, own, count, due)
    parts = swapped([kept, *sent], "filt", 1)
    spread_in, token_in = spread(halved, 0)
    spread_hidden, token_hidden = spread(halved, 1)
    first_out_grad = first_out(parts, slope_first, [token_in, token_hidden, *second_far])

    first_blocks = [first_out_grad] + chips_apart([first_out_grad] * (chips - 1))
    crossed = swap(pack(second_far, [first_out_grad]), "slab", 1)
    second_blocks = [second_out, second_other] + second_far
    second_grad, token = weight_grad(spread_hidden, second_blocks, crossed, True)
    crossed = swap(pack(first_blocks, [token]), "slab", 1)
    first_grad, _ = weight_grad(spread_in, first_blocks, crossed, False)
    return jnp.transpose(first_grad, (0, 2, 1)), jnp.transpose(second_grad, (0, 2, 1))


def solution(mesh):
    placed = (
        P("slab", "filt", None),
        P(None, "filt", None),
        P(None, "filt", None),
        P(None, "filt"),
        P("slab", None),
    )
    return jax.shard_map(
        shards,
        mesh=mesh,
        in_specs=placed,
        out_specs=(P(None, "filt", "slab"), P(None, "filt", "slab")),
        check_vma=False,
    )
```

```python
import functools

import jax
import jax.numpy as jnp
from jax import lax
from jax.experimental import pallas as pl
from jax.experimental.pallas import tpu as pltpu
from jax.sharding import PartitionSpec as P

WIDTH = 8
SHIFTS = [(b, e) for b in (-1, 0, 1) for e in (-1, 0, 1)]
LIMIT = 20 * 1024 * 1024
VMEM = pl.BlockSpec(memory_space=pltpu.VMEM)
ANY = pl.BlockSpec(memory_space=pl.ANY)


def swap(block, axis, step):
    count = lax.axis_size(axis)
    return lax.ppermute(block, axis, [(i, i ^ step) for i in range(count)])


def exchanged(block, axis):
    return swapped([block] * lax.axis_size(axis), axis, 1)


def swapped(blocks, axis, unit):
    return [blocks[0]] + [swap(blocks[step], axis, unit * step) for step in range(1, len(blocks))]


def halo(volume, own):
    count = lax.axis_size("slab")
    other = swap(volume, "slab", 1)
    passed = edge(other, [own])
    pairs = [(i, i + 2) for i in range(0, count - 2, 2)] + [(i, i - 2) for i in range(3, count, 2)]
    return other, lax.ppermute(passed, "slab", pairs)


def chips_apart(blocks):
    return swapped([None, *blocks], "slab", 2)[1:]


def every_chip(block):
    blocks = [block]
    for step in range(1, lax.axis_size("slab") // 2):
        low = step & -step
        blocks.append(swap(blocks[step ^ low], "slab", 2 * low))
    return blocks


def call(body, out_shape, cost, *operands, in_specs, scratch_shapes=(), passed=(), after=()):
    flops, moved = cost
    single = not isinstance(out_shape, list)
    outs = [out_shape] if single else out_shape
    first, second = len(operands), len(operands) + len(passed) + len(after)
    third = second + len(outs)

    def inner(*refs):
        body(*refs[:first], *refs[second:third], *refs[third + len(passed) :])

    given = pl.pallas_call(
        inner,
        out_shape=[*outs, *(struct(array.shape, array.dtype) for array in passed)],
        cost_estimate=pl.CostEstimate(flops=flops, bytes_accessed=moved, transcendentals=0),
        compiler_params=pltpu.CompilerParams(vmem_limit_bytes=LIMIT),
        in_specs=[*in_specs] + [ANY] * (len(passed) + len(after)),
        out_specs=[VMEM] * len(outs) + [ANY] * len(passed),
        scratch_shapes=list(scratch_shapes),
        input_output_aliases={first + i: len(outs) + i for i in range(len(passed))},
    )(*operands, *passed, *after)
    if passed:
        return [*given[: len(outs)], list(given[len(outs) :])]
    return given[0] if single else list(given)


def struct(shape, dtype):
    return jax.ShapeDtypeStruct(tuple(shape), dtype)


def here(axis):
    return lax.axis_index(axis).astype(jnp.int32)


def core():
    return lax.rem(here("slab"), 2)


def far_owners(side):
    me = here("slab")
    return [me ^ (2 * step) ^ side for step in range(lax.axis_size("slab") // 2)]


TOKEN = struct((8, 128), jnp.float32)


def stage_body(count, *refs):
    sources, targets, sems = refs[:count], refs[count : 2 * count], refs[2 * count]
    copies = [pltpu.make_async_copy(sources[i], targets[i], sems.at[i]) for i in range(count)]
    for copy in copies:
        copy.start()
    for copy in copies:
        copy.wait()


def stage(*arrays):
    count = len(arrays)
    return call(
        functools.partial(stage_body, count),
        [struct(array.shape, array.dtype) for array in arrays],
        (0, sum(4 * array.size for array in arrays)),
        *arrays,
        in_specs=[pl.BlockSpec(memory_space=pltpu.HBM)] * count,
        scratch_shapes=[pltpu.SemaphoreType.DMA((count,))],
    )


def inside(shape, axis, b, e):
    spot = lax.broadcasted_iota(jnp.int32, shape, axis)
    column = spot % WIDTH + e
    moved = spot + WIDTH * b
    return (column >= 0) & (column < WIDTH) & (moved >= 0) & (moved < shape[axis])


def shifted(values, axis, b, e):
    if b == 0 and e == 0:
        return values
    size = values.shape[axis]
    turned = pltpu.roll(values, (-(WIDTH * b + e)) % size, axis)
    return jnp.where(inside(values.shape, axis, b, e), turned, 0.0)


def fold_shifts(products):
    rows = products.shape[0] // len(SHIFTS)
    total = None
    for number, (b, e) in enumerate(SHIFTS):
        term = shifted(products[number * rows : (number + 1) * rows, :], 1, b, e)
        total = term if total is None else total + term
    return total


def dot(left, right):
    return jnp.dot(left, right, preferred_element_type=jnp.float32)


def edge_body(other_ref, out_ref):
    out_ref[0] = other_ref[(1 - core()) * (other_ref.shape[0] - 1)]


def edge(other, after):
    shape = (1, *other.shape[1:])
    return call(edge_body, struct(shape, other.dtype), (0, other.size), other, in_specs=[VMEM], after=after)


def halves(rows):
    return 2 if rows % 32 == 0 and lax.axis_size("filt") % 2 == 0 else 1


def assemble_body(count, split, order, *refs):
    parts, whole_ref, shares = refs[:count][::order], refs[count], refs[count + 1 :]
    size = parts[0].shape[1]
    me, chip = here("filt"), here("slab") // 2
    for step in range(count):
        place = pl.ds(pl.multiple_of((me ^ step) * size, size), size)
        whole_ref[:, place, :] = parts[step][...]
    rows = shares[0].shape[2]
    for step, share_ref in enumerate(shares):
        for side in range(2):
            begin = (((chip ^ step) * 2 + side) * split + lax.rem(me, split)) * rows
            share_ref[side] = whole_ref[:, pl.ds(pl.multiple_of(begin, rows), rows), :]


def assemble(parts, order, after=()):
    planes, size, plane = parts[0].shape
    count, slabs = len(parts), lax.axis_size("slab")
    channels = size * count
    split = halves(channels // slabs)
    kind = parts[0].dtype
    outs = [struct((planes, channels, plane), kind)]
    outs += [struct((2, planes, channels // slabs // split, plane), kind)] * (slabs // 2)
    whole, *shares = call(
        functools.partial(assemble_body, count, split, order),
        outs,
        (0, 4 * planes * channels * plane),
        *parts[::order],
        in_specs=[VMEM] * count,
        after=after,
    )
    return whole, shares


def crossing_body(count, *refs):
    planes = refs[0].shape[1]
    for step in range(count):
        for j in range(planes):
            refs[count][step * planes + j] = refs[step][1 - core(), j]


def collect_body(count, crossed_ref, *refs):
    owners, side = far_owners(0), core()
    planes = refs[0].shape[1]
    out_ref = refs[-1]
    base = out_ref.shape[0] - 2 * count * planes
    if base > 0:
        out_ref[:base] = refs[count][...]
    for step in range(count):
        for j in range(planes):
            out_ref[base + owners[step] * planes + j] = refs[step][side, j]
            out_ref[base + (owners[step] ^ 1) * planes + j] = crossed_ref[step * planes + j]


def collected(shares, after, later=(), earlier=()):
    count = len(shares)
    _, planes, rows, plane = shares[0].shape
    kind, size = shares[0].dtype, shares[0].size * count
    crossing = call(
        functools.partial(crossing_body, count),
        struct((count * planes, rows, plane), kind),
        (0, 2 * size),
        *shares,
        in_specs=[VMEM] * count,
        after=after,
    )
    return call(
        functools.partial(collect_body, count),
        struct((2 * count * planes * (1 + len(earlier)), rows, plane), kind),
        (0, 4 * size),
        swap(crossing, "slab", 1), *shares, *earlier,
        in_specs=[VMEM] * (1 + count + len(earlier)),
        after=later,
    )


def both_halves(volume, split):
    return [volume] + ([swap(volume, "filt", 1)] if split == 2 else [])


def pack_body(count, *refs):
    out_ref = refs[count]
    blocks = refs[:count]
    row = 0
    for number in range(count):
        planes, plane, filters = blocks[number].shape
        for j in range(planes):
            for begin in range(0, plane, filters):
                out_ref[row : row + filters, begin : begin + filters] = blocks[number][j, begin : begin + filters, :]
            row += filters


def pack(blocks, after=()):
    plane = blocks[0].shape[1]
    total = sum(block.size for block in blocks)
    return call(
        functools.partial(pack_body, len(blocks)),
        struct((total // plane, plane), blocks[0].dtype),
        (0, 4 * total),
        *blocks,
        in_specs=[VMEM] * len(blocks),
        after=after,
    )


def taps(weight_ref, number):
    block = weight_ref[pl.ds(9 * number, 9)]
    return block.reshape(block.shape[0] * block.shape[1], block.shape[2])


def forward_own_body(planes, volume_ref, weight_ref, out_ref, acc_ref):
    for a in (0, 1, -1):
        weight = taps(weight_ref, a + 1)
        for j in range(planes):
            if 0 <= j + a < planes:
                product = dot(weight, volume_ref[j + a])
                acc_ref[j] = product if a == 0 else acc_ref[j] + product
    for j in range(planes):
        out_ref[j] = fold_shifts(acc_ref.at[j])


def forward_own(volume, weight):
    planes, channels, plane = volume.shape
    filters = weight.shape[1]
    return call(
        functools.partial(forward_own_body, planes),
        struct((planes, filters, plane), jnp.float32),
        (2 * 9 * filters * channels * plane * (3 * planes - 2), weight.size * 2),
        volume, weight,
        in_specs=[VMEM] * 2,
        scratch_shapes=[pltpu.VMEM((planes, 9 * filters, plane), jnp.float32)],
    )


def forward_other_body(planes, other_ref, weight_ref, own_ref, out_ref, acc_ref):
    up, last = core(), planes - 1
    place = (1 - up) * last
    acc_ref[...] = dot(taps(weight_ref, 2 * (1 - up)), other_ref[up * last])
    out_ref[...] = own_ref[...]
    out_ref[place] = out_ref[place] + fold_shifts(acc_ref)


def forward_other(other, weight, own):
    planes, filters, plane = own.shape
    return call(
        functools.partial(forward_other_body, planes),
        struct(own.shape, jnp.float32),
        (2 * weight.size // 3 * plane, weight.size * 2 // 3),
        other, weight, own,
        in_specs=[VMEM] * 3,
        scratch_shapes=[pltpu.VMEM((9 * filters, plane), jnp.float32)],
    )


def silu_and_slope(values):
    sig = 1.0 / (1.0 + jnp.exp(-values))
    return values * sig, sig * (1.0 + values * (1.0 - sig))


def forward_rest_body(planes, beyond_ref, weight_ref, own_ref, *refs):
    head_ref = refs[0] if len(refs) == 5 else None
    slope_ref, made_ref, acc_ref, total_ref = refs[-4:]
    up = core()
    place = up * (planes - 1)
    total_ref[...] = own_ref[...]
    acc_ref[...] = dot(taps(weight_ref, 2 * up), beyond_ref[0])
    total_ref[place] = total_ref[place] + fold_shifts(acc_ref)
    for j in range(planes):
        value, slope = silu_and_slope(total_ref[j])
        value = value.astype(jnp.bfloat16)
        slope_ref[j] = slope.T if head_ref is None else slope
        made_ref[j] = value if head_ref is None else dot(head_ref[...], value)


def forward_rest(beyond, weight, own, after, head=None):
    planes, filters, plane = own.shape
    channels = weight.shape[2]
    ins = [beyond, weight, own]
    slope = own.shape
    if head is None:
        slope = (planes, plane, filters)
        made = struct(own.shape, jnp.bfloat16)
    else:
        ins.append(head)
        made = struct((planes, head.shape[0], plane), jnp.float32)
    return call(
        functools.partial(forward_rest_body, planes),
        [struct(slope, jnp.float32), made],
        (2 * 9 * filters * channels * plane, weight.size * 2 // 3),
        *ins,
        in_specs=[VMEM] * len(ins),
        scratch_shapes=[
            pltpu.VMEM((9 * filters, plane), jnp.float32),
            pltpu.VMEM(own.shape, jnp.float32),
        ],
        after=after,
    )


def loss_body(count, labels_ref, head_ref, slope_ref, *refs):
    parts, grad_ref = refs[:count][::-1], refs[count]
    for j in range(grad_ref.shape[0]):
        logits = parts[0][j]
        for part in parts[1:]:
            logits = logits + part[j]
        powers = jnp.exp(logits)
        likely = powers / jnp.sum(powers, axis=0, keepdims=True)
        classes = lax.broadcasted_iota(jnp.int32, logits.shape, 0)
        onehot = (labels_ref[j : j + 1, :] == classes).astype(jnp.float32)
        logit_grad = (likely - onehot).astype(jnp.bfloat16).astype(jnp.float32)
        back = lax.dot_general(
            head_ref[...].astype(jnp.float32),
            logit_grad,
            (((0,), (0,)), ((), ())),
            preferred_element_type=jnp.float32,
        )
        grad_ref[j] = (back * slope_ref[j]).T.astype(jnp.bfloat16)


def loss_grad(parts, labels, head, slope, after):
    planes, plane = labels.shape
    return call(
        functools.partial(loss_body, len(parts)),
        struct((planes, plane, slope.shape[1]), jnp.bfloat16),
        (2 * slope.size * head.shape[0], slope.size * 6),
        labels, head, slope, *parts[::-1],
        in_specs=[VMEM] * (3 + len(parts)),
        after=after,
    )


def spread_back(grad, spread_ref):
    filters = grad.shape[1]
    turned = grad.astype(jnp.float32)
    for number, (b, e) in enumerate(SHIFTS):
        moved = shifted(turned, 0, -b, -e).astype(jnp.bfloat16)
        spread_ref[:, number * filters : (number + 1) * filters] = moved


def backward_own_body(planes, grad_ref, weight_ref, out_ref, spread_ref):
    for j in range(planes):
        spread_back(grad_ref[j], spread_ref.at[j])
    for a in (0, 1, -1):
        weight = taps(weight_ref, a + 1)
        for j in range(planes):
            if 0 <= j - a < planes:
                product = dot(spread_ref[j - a], weight)
                out_ref[j] = product if a == 0 else out_ref[j] + product


def backward_own(grad, weight):
    planes, plane, filters = grad.shape
    channels = weight.shape[2]
    return call(
        functools.partial(backward_own_body, planes),
        struct((planes, plane, channels), jnp.float32),
        (2 * 9 * filters * channels * plane * (3 * planes - 2), weight.size * 2),
        grad, weight,
        in_specs=[VMEM] * 2,
        scratch_shapes=[pltpu.VMEM((planes, plane, 9 * filters), jnp.bfloat16)],
    )


def backward_other_body(planes, other_ref, weight_ref, own_ref, out_ref, spread_ref):
    up, last = core(), planes - 1
    place = (1 - up) * last
    spread_back(other_ref[up * last], spread_ref)
    out_ref[...] = own_ref[...]
    out_ref[place] = out_ref[place] + dot(spread_ref[...], taps(weight_ref, 2 * up))


def backward_other(other, weight, own):
    planes, plane, _ = own.shape
    filters = weight.shape[1]
    return call(
        functools.partial(backward_other_body, planes),
        struct(own.shape, jnp.float32),
        (2 * weight.size // 3 * plane, weight.size * 2 // 3),
        other, weight, own,
        in_specs=[VMEM] * 3,
        scratch_shapes=[pltpu.VMEM((plane, 9 * filters), jnp.bfloat16)],
    )


def backward_rest_body(planes, count, beyond_ref, weight_ref, own_ref, *refs):
    kept_ref, sent, (spread_ref, total_ref) = refs[0], refs[1:count], refs[count:]
    size = kept_ref.shape[2]
    up, me = core(), here("filt")
    place = up * (planes - 1)
    spread_back(beyond_ref[0], spread_ref)
    product = dot(spread_ref[...], taps(weight_ref, 2 * (1 - up)))
    for block in range(count):
        columns = slice(block * size, (block + 1) * size)
        for j in range(planes):
            total_ref[block, j] = own_ref[j, :, columns]
        total_ref[block, place] = total_ref[block, place] + product[:, columns]
    kept_ref[...] = total_ref[me]
    for number in range(1, count):
        sent[number - 1][...] = total_ref[me ^ number].astype(jnp.bfloat16)


def backward_rest(beyond, weight, own, count, after):
    planes, plane, channels = own.shape
    filters = weight.shape[1]
    size = channels // count
    outs = [struct((planes, plane, size), jnp.float32)]
    outs += [struct((planes, plane, size), jnp.bfloat16)] * (count - 1)
    return call(
        functools.partial(backward_rest_body, planes, count),
        outs,
        (2 * 9 * filters * channels * plane, weight.size * 2 // 3),
        beyond, weight, own,
        in_specs=[VMEM] * 3,
        scratch_shapes=[
            pltpu.VMEM((plane, 9 * filters), jnp.bfloat16),
            pltpu.VMEM((count, planes, plane, size), jnp.float32),
        ],
        after=after,
    )


def first_grad_body(count, slope_ref, *refs):
    parts, out_ref = refs[:count], refs[count]
    for j in range(out_ref.shape[0]):
        total = parts[0][j]
        for part in parts[1:]:
            total = total + part[j].astype(jnp.float32)
        out_ref[j] = (total * slope_ref[j]).astype(jnp.bfloat16)


def first_out(parts, slope, after):
    return call(
        functools.partial(first_grad_body, len(parts)),
        struct(slope.shape, jnp.bfloat16),
        (slope.size * 4, slope.size * 14),
        slope, *parts,
        in_specs=[VMEM] * (1 + len(parts)),
        after=after,
    )


def spread_body(split, first, *refs):
    spread_ref, token_ref = refs[split:]
    token_ref[...] = jnp.zeros_like(token_ref)
    both, rows, plane = refs[0].shape
    depth = both // 2
    me = lax.rem(here("filt"), split)
    for d in range(depth):
        for half in range(split):
            values = refs[half][first * depth + d].astype(jnp.float32)
            for number, (b, e) in enumerate(SHIFTS):
                begin = (number * split + (me ^ half)) * rows
                moved = shifted(values, 1, b, e).astype(jnp.bfloat16)
                spread_ref[pl.ds(pl.multiple_of(begin, rows), rows), d * plane : (d + 1) * plane] = moved


def spread(halved, first):
    split = len(halved)
    both, rows, plane = halved[0].shape
    depth = both // 2
    channels = split * rows
    return call(
        functools.partial(spread_body, split, first),
        [struct((9 * channels, depth * plane), jnp.bfloat16), TOKEN],
        (9 * channels * depth * plane, 10 * channels * depth * plane),
        *halved,
        in_specs=[VMEM] * split,
    )


def weight_grad_body(count, second, spread_ref, crossed_ref, *refs):
    parts, (out_ref, token_ref, grad_ref) = refs[:count], refs[count:]
    token_ref[...] = jnp.zeros_like(token_ref)
    planes, plane, filters = parts[0].shape
    channels = spread_ref.shape[0] // 9
    depth = spread_ref.shape[1] // plane
    zero = jnp.zeros((plane, filters), jnp.bfloat16)
    grad_ref[depth * plane : (depth + 1) * plane, : filters] = zero
    grad_ref[plane : 2 * plane, 2 * filters :] = zero

    def one(block, d, begin):
        rows = block.shape[0]
        for a in (-1, 0, 1):
            place = pl.ds(pl.multiple_of((d + a + 1) * plane + begin, rows), rows)
            grad_ref[place, (a + 1) * filters : (a + 2) * filters] = block

    near, far = far_owners(0), far_owners(1)
    owners = [near[0], far[0], *near[1:], *far[1:]] if second else near + far
    row = 0
    for number in range(count):
        for j in range(planes):
            one(parts[number][j], owners[number] * planes + j, 0)
    for number in range(count, len(owners)):
        for j in range(planes):
            for begin in range(0, plane, filters):
                block = crossed_ref[row : row + filters, begin : begin + filters]
                one(block, owners[number] * planes + j, begin)
            row += filters

    product = dot(spread_ref[...], grad_ref[plane : (depth + 1) * plane, :])
    for r in range(3):
        for number in range(9):
            out_ref[r * 9 + number] = product[
                number * channels : (number + 1) * channels, r * filters : (r + 1) * filters
            ]


def weight_grad(spreads, blocks, crossed, second):
    channels, columns = spreads.shape[0] // 9, spreads.shape[1]
    _, plane, filters = blocks[0].shape
    return call(
        functools.partial(weight_grad_body, len(blocks), second),
        [struct((27, channels, filters), jnp.float32), TOKEN],
        (2 * 27 * filters * channels * columns, 27 * channels * filters * 4 + spreads.size * 2),
        spreads, crossed, *blocks,
        in_specs=[VMEM] * (2 + len(blocks)),
        scratch_shapes=[pltpu.VMEM((columns + 2 * plane, 3 * filters), jnp.bfloat16)],
    )


def shards(features, first_weight, second_weight, head_weight, labels):
    count = lax.axis_size("filt")
    chips = lax.axis_size("slab") // 2
    split = halves(features.shape[1] * count // lax.axis_size("slab"))
    near, first_weight, head_weight = stage(features, first_weight, head_weight)
    all_in, share_in = assemble([near] + exchanged(features, "filt")[1:], -1)
    own = forward_own(all_in, first_weight)
    share_in = [share_in[0]] + chips_apart(share_in[1:])
    other, beyond = halo(all_in, own)
    own = forward_other(other, first_weight, own)
    slope_first, hidden = forward_rest(beyond, first_weight, own, share_in[1:])

    halved_in = collected(share_in, [hidden])
    all_hidden, share_hidden = assemble(exchanged(hidden, "filt"), 1, [halved_in])
    own = forward_own(all_hidden, second_weight)
    share_hidden = [share_hidden[0]] + chips_apart(share_hidden[1:])
    other, beyond = halo(all_hidden, own)
    own = forward_other(other, second_weight, own)
    slope_second, logits = forward_rest(beyond, second_weight, own, share_hidden[1:], head_weight)

    logits_parts = exchanged(logits, "filt")
    second_out = loss_grad(logits_parts, labels, head_weight, slope_second, [])
    halved = both_halves(collected(share_hidden, [logits], [second_out], [halved_in]), split)
    own = backward_own(second_out, second_weight)
    second_other, beyond = halo(second_out, own)
    second_far = every_chip(second_out)[1:]
    own = backward_other(second_other, second_weight, own)
    due = halved[:1] + second_far[chips // 2 - 1 : chips // 2]
    kept, *sent = backward_rest(beyond, second_weight, own, count, due)
    parts = swapped([kept, *sent], "filt", 1)
    spread_in, token_in = spread(halved, 0)
    spread_hidden, token_hidden = spread(halved, 1)
    first_out_grad = first_out(parts, slope_first, [token_in, token_hidden, *second_far])

    first_blocks = [first_out_grad] + chips_apart([first_out_grad] * (chips - 1))
    crossed = swap(pack(second_far, [first_out_grad]), "slab", 1)
    second_blocks = [second_out, second_other] + second_far
    second_grad, token = weight_grad(spread_hidden, second_blocks, crossed, True)
    crossed = swap(pack(first_blocks, [token]), "slab", 1)
    first_grad, _ = weight_grad(spread_in, first_blocks, crossed, False)
    return jnp.transpose(first_grad, (0, 2, 1)), jnp.transpose(second_grad, (0, 2, 1))


def solution(mesh):
    placed = (
        P("slab", "filt", None),
        P(None, "filt", None),
        P(None, "filt", None),
        P(None, "filt"),
        P("slab", None),
    )
    return jax.shard_map(
        shards,
        mesh=mesh,
        in_specs=placed,
        out_specs=(P(None, "filt", "slab"), P(None, "filt", "slab")),
        check_vma=False,
    )
```

```python
import functools

import jax
import jax.numpy as jnp
from jax import lax
from jax.experimental import pallas as pl
from jax.experimental.pallas import tpu as pltpu
from jax.sharding import PartitionSpec as P

WIDTH = 8
SHIFTS = [(b, e) for b in (-1, 0, 1) for e in (-1, 0, 1)]
LIMIT = 20 * 1024 * 1024
VMEM = pl.BlockSpec(memory_space=pltpu.VMEM)
ANY = pl.BlockSpec(memory_space=pl.ANY)


def swap(block, axis, step):
    count = lax.axis_size(axis)
    return lax.ppermute(block, axis, [(i, i ^ step) for i in range(count)])


def exchanged(block, axis):
    return swapped([block] * lax.axis_size(axis), axis, 1)


def swapped(blocks, axis, unit):
    return [blocks[0]] + [swap(blocks[step], axis, unit * step) for step in range(1, len(blocks))]


def halo(volume, own):
    count = lax.axis_size("slab")
    other = swap(volume, "slab", 1)
    passed = edge(other, [own])
    pairs = [(i, i + 2) for i in range(0, count - 2, 2)] + [(i, i - 2) for i in range(3, count, 2)]
    return other, lax.ppermute(passed, "slab", pairs)


def chips_apart(blocks):
    return swapped([None, *blocks], "slab", 2)[1:]


def every_chip(block):
    blocks = [block]
    for step in range(1, lax.axis_size("slab") // 2):
        low = step & -step
        blocks.append(swap(blocks[step ^ low], "slab", 2 * low))
    return blocks


def call(body, out_shape, cost, *operands, in_specs, scratch_shapes=(), passed=(), after=()):
    flops, moved = cost
    single = not isinstance(out_shape, list)
    outs = [out_shape] if single else out_shape
    first, second = len(operands), len(operands) + len(passed) + len(after)
    third = second + len(outs)

    def inner(*refs):
        body(*refs[:first], *refs[second:third], *refs[third + len(passed) :])

    given = pl.pallas_call(
        inner,
        out_shape=[*outs, *(struct(array.shape, array.dtype) for array in passed)],
        cost_estimate=pl.CostEstimate(flops=flops, bytes_accessed=moved, transcendentals=0),
        compiler_params=pltpu.CompilerParams(vmem_limit_bytes=LIMIT),
        in_specs=[*in_specs] + [ANY] * (len(passed) + len(after)),
        out_specs=[VMEM] * len(outs) + [ANY] * len(passed),
        scratch_shapes=list(scratch_shapes),
        input_output_aliases={first + i: len(outs) + i for i in range(len(passed))},
    )(*operands, *passed, *after)
    if passed:
        return [*given[: len(outs)], list(given[len(outs) :])]
    return given[0] if single else list(given)


def struct(shape, dtype):
    return jax.ShapeDtypeStruct(tuple(shape), dtype)


def here(axis):
    return lax.axis_index(axis).astype(jnp.int32)


def core():
    return lax.rem(here("slab"), 2)


def far_owners(side):
    me = here("slab")
    return [me ^ (2 * step) ^ side for step in range(lax.axis_size("slab") // 2)]


TOKEN = struct((8, 128), jnp.float32)


def stage_body(count, *refs):
    sources, targets, sems = refs[:count], refs[count : 2 * count], refs[2 * count]
    copies = [pltpu.make_async_copy(sources[i], targets[i], sems.at[i]) for i in range(count)]
    for copy in copies:
        copy.start()
    for copy in copies:
        copy.wait()


def stage(*arrays):
    count = len(arrays)
    return call(
        functools.partial(stage_body, count),
        [struct(array.shape, array.dtype) for array in arrays],
        (0, sum(4 * array.size for array in arrays)),
        *arrays,
        in_specs=[pl.BlockSpec(memory_space=pltpu.HBM)] * count,
        scratch_shapes=[pltpu.SemaphoreType.DMA((count,))],
    )


def inside(shape, axis, b, e):
    spot = lax.broadcasted_iota(jnp.int32, shape, axis)
    column = spot % WIDTH + e
    moved = spot + WIDTH * b
    return (column >= 0) & (column < WIDTH) & (moved >= 0) & (moved < shape[axis])


def shifted(values, axis, b, e):
    if b == 0 and e == 0:
        return values
    size = values.shape[axis]
    turned = pltpu.roll(values, (-(WIDTH * b + e)) % size, axis)
    return jnp.where(inside(values.shape, axis, b, e), turned, 0.0)


def fold_shifts(products):
    rows = products.shape[0] // len(SHIFTS)
    total = None
    for number, (b, e) in enumerate(SHIFTS):
        term = shifted(products[number * rows : (number + 1) * rows, :], 1, b, e)
        total = term if total is None else total + term
    return total


def dot(left, right):
    return jnp.dot(left, right, preferred_element_type=jnp.float32)


def edge_body(other_ref, out_ref):
    out_ref[0] = other_ref[(1 - core()) * (other_ref.shape[0] - 1)]


def edge(other, after):
    shape = (1, *other.shape[1:])
    return call(edge_body, struct(shape, other.dtype), (0, other.size), other, in_specs=[VMEM], after=after)


def halves(rows):
    return 2 if rows % 32 == 0 and lax.axis_size("filt") % 2 == 0 else 1


def assemble_body(count, split, order, *refs):
    parts, whole_ref, shares = refs[:count][::order], refs[count], refs[count + 1 :]
    size = parts[0].shape[1]
    me, chip = here("filt"), here("slab") // 2
    for step in range(count):
        place = pl.ds(pl.multiple_of((me ^ step) * size, size), size)
        whole_ref[:, place, :] = parts[step][...]
    rows = shares[0].shape[2]
    for step, share_ref in enumerate(shares):
        for side in range(2):
            begin = (((chip ^ step) * 2 + side) * split + lax.rem(me, split)) * rows
            share_ref[side] = whole_ref[:, pl.ds(pl.multiple_of(begin, rows), rows), :]


def assemble(parts, order, after=()):
    planes, size, plane = parts[0].shape
    count, slabs = len(parts), lax.axis_size("slab")
    channels = size * count
    split = halves(channels // slabs)
    kind = parts[0].dtype
    outs = [struct((planes, channels, plane), kind)]
    outs += [struct((2, planes, channels // slabs // split, plane), kind)] * (slabs // 2)
    whole, *shares = call(
        functools.partial(assemble_body, count, split, order),
        outs,
        (0, 4 * planes * channels * plane),
        *parts[::order],
        in_specs=[VMEM] * count,
        after=after,
    )
    return whole, shares


def crossing_body(count, *refs):
    planes = refs[0].shape[1]
    for step in range(count):
        for j in range(planes):
            refs[count][step * planes + j] = refs[step][1 - core(), j]


def collect_body(count, crossed_ref, *refs):
    owners, side = far_owners(0), core()
    planes = refs[0].shape[1]
    out_ref = refs[-1]
    base = out_ref.shape[0] - 2 * count * planes
    if base > 0:
        out_ref[:base] = refs[count][...]
    for step in range(count):
        for j in range(planes):
            out_ref[base + owners[step] * planes + j] = refs[step][side, j]
            out_ref[base + (owners[step] ^ 1) * planes + j] = crossed_ref[step * planes + j]


def collected(shares, after, later=(), earlier=()):
    count = len(shares)
    _, planes, rows, plane = shares[0].shape
    kind, size = shares[0].dtype, shares[0].size * count
    crossing = call(
        functools.partial(crossing_body, count),
        struct((count * planes, rows, plane), kind),
        (0, 2 * size),
        *shares,
        in_specs=[VMEM] * count,
        after=after,
    )
    return call(
        functools.partial(collect_body, count),
        struct((2 * count * planes * (1 + len(earlier)), rows, plane), kind),
        (0, 4 * size),
        swap(crossing, "slab", 1), *shares, *earlier,
        in_specs=[VMEM] * (1 + count + len(earlier)),
        after=later,
    )


def both_halves(volume, split):
    return [volume] + ([swap(volume, "filt", 1)] if split == 2 else [])


def pack_body(count, *refs):
    out_ref = refs[count]
    blocks = refs[:count]
    row = 0
    for number in range(count):
        planes, plane, filters = blocks[number].shape
        for j in range(planes):
            for begin in range(0, plane, filters):
                out_ref[row : row + filters, begin : begin + filters] = blocks[number][j, begin : begin + filters, :]
            row += filters


def pack(blocks, after=()):
    plane = blocks[0].shape[1]
    total = sum(block.size for block in blocks)
    return call(
        functools.partial(pack_body, len(blocks)),
        struct((total // plane, plane), blocks[0].dtype),
        (0, 4 * total),
        *blocks,
        in_specs=[VMEM] * len(blocks),
        after=after,
    )


def taps(weight_ref, number):
    block = weight_ref[pl.ds(9 * number, 9)]
    return block.reshape(block.shape[0] * block.shape[1], block.shape[2])


def forward_own_body(planes, volume_ref, weight_ref, out_ref, acc_ref):
    for a in (0, 1, -1):
        weight = taps(weight_ref, a + 1)
        for j in range(planes):
            if 0 <= j + a < planes:
                product = dot(weight, volume_ref[j + a])
                acc_ref[j] = product if a == 0 else acc_ref[j] + product
    for j in range(planes):
        out_ref[j] = fold_shifts(acc_ref.at[j])


def forward_own(volume, weight):
    planes, channels, plane = volume.shape
    filters = weight.shape[1]
    return call(
        functools.partial(forward_own_body, planes),
        struct((planes, filters, plane), jnp.float32),
        (2 * 9 * filters * channels * plane * (3 * planes - 2), weight.size * 2),
        volume, weight,
        in_specs=[VMEM] * 2,
        scratch_shapes=[pltpu.VMEM((planes, 9 * filters, plane), jnp.float32)],
    )


def forward_other_body(planes, other_ref, weight_ref, own_ref, out_ref, acc_ref):
    up, last = core(), planes - 1
    place = (1 - up) * last
    acc_ref[...] = dot(taps(weight_ref, 2 * (1 - up)), other_ref[up * last])
    out_ref[...] = own_ref[...]
    out_ref[place] = out_ref[place] + fold_shifts(acc_ref)


def forward_other(other, weight, own):
    planes, filters, plane = own.shape
    return call(
        functools.partial(forward_other_body, planes),
        struct(own.shape, jnp.float32),
        (2 * weight.size // 3 * plane, weight.size * 2 // 3),
        other, weight, own,
        in_specs=[VMEM] * 3,
        scratch_shapes=[pltpu.VMEM((9 * filters, plane), jnp.float32)],
    )


def silu_and_slope(values):
    sig = 1.0 / (1.0 + jnp.exp(-values))
    return values * sig, sig * (1.0 + values * (1.0 - sig))


def forward_rest_body(planes, beyond_ref, weight_ref, own_ref, *refs):
    head_ref = refs[0] if len(refs) == 5 else None
    slope_ref, made_ref, acc_ref, total_ref = refs[-4:]
    up = core()
    place = up * (planes - 1)
    total_ref[...] = own_ref[...]
    acc_ref[...] = dot(taps(weight_ref, 2 * up), beyond_ref[0])
    total_ref[place] = total_ref[place] + fold_shifts(acc_ref)
    for j in range(planes):
        value, slope = silu_and_slope(total_ref[j])
        value = value.astype(jnp.bfloat16)
        slope_ref[j] = slope.T if head_ref is None else slope
        made_ref[j] = value if head_ref is None else dot(head_ref[...], value)


def forward_rest(beyond, weight, own, after, head=None):
    planes, filters, plane = own.shape
    channels = weight.shape[2]
    ins = [beyond, weight, own]
    slope = own.shape
    if head is None:
        slope = (planes, plane, filters)
        made = struct(own.shape, jnp.bfloat16)
    else:
        ins.append(head)
        made = struct((planes, head.shape[0], plane), jnp.float32)
    return call(
        functools.partial(forward_rest_body, planes),
        [struct(slope, jnp.float32), made],
        (2 * 9 * filters * channels * plane, weight.size * 2 // 3),
        *ins,
        in_specs=[VMEM] * len(ins),
        scratch_shapes=[
            pltpu.VMEM((9 * filters, plane), jnp.float32),
            pltpu.VMEM(own.shape, jnp.float32),
        ],
        after=after,
    )


def loss_body(count, labels_ref, head_ref, slope_ref, *refs):
    parts, grad_ref = refs[:count][::-1], refs[count]
    for j in range(grad_ref.shape[0]):
        logits = parts[0][j]
        for part in parts[1:]:
            logits = logits + part[j]
        powers = jnp.exp(logits)
        likely = powers / jnp.sum(powers, axis=0, keepdims=True)
        classes = lax.broadcasted_iota(jnp.int32, logits.shape, 0)
        onehot = (labels_ref[j : j + 1, :] == classes).astype(jnp.float32)
        logit_grad = (likely - onehot).astype(jnp.bfloat16).astype(jnp.float32)
        back = lax.dot_general(
            head_ref[...].astype(jnp.float32),
            logit_grad,
            (((0,), (0,)), ((), ())),
            preferred_element_type=jnp.float32,
        )
        grad_ref[j] = (back * slope_ref[j]).T.astype(jnp.bfloat16)


def loss_grad(parts, labels, head, slope, after):
    planes, plane = labels.shape
    return call(
        functools.partial(loss_body, len(parts)),
        struct((planes, plane, slope.shape[1]), jnp.bfloat16),
        (2 * slope.size * head.shape[0], slope.size * 6),
        labels, head, slope, *parts[::-1],
        in_specs=[VMEM] * (3 + len(parts)),
        after=after,
    )


def spread_back(grad, spread_ref):
    filters = grad.shape[1]
    turned = grad.astype(jnp.float32)
    for number, (b, e) in enumerate(SHIFTS):
        moved = shifted(turned, 0, -b, -e).astype(jnp.bfloat16)
        spread_ref[:, number * filters : (number + 1) * filters] = moved


def backward_own_body(planes, grad_ref, weight_ref, out_ref, spread_ref):
    for j in range(planes):
        spread_back(grad_ref[j], spread_ref.at[j])
    for a in (0, 1, -1):
        weight = taps(weight_ref, a + 1)
        for j in range(planes):
            if 0 <= j - a < planes:
                product = dot(spread_ref[j - a], weight)
                out_ref[j] = product if a == 0 else out_ref[j] + product


def backward_own(grad, weight):
    planes, plane, filters = grad.shape
    channels = weight.shape[2]
    return call(
        functools.partial(backward_own_body, planes),
        struct((planes, plane, channels), jnp.float32),
        (2 * 9 * filters * channels * plane * (3 * planes - 2), weight.size * 2),
        grad, weight,
        in_specs=[VMEM] * 2,
        scratch_shapes=[pltpu.VMEM((planes, plane, 9 * filters), jnp.bfloat16)],
    )


def backward_other_body(planes, other_ref, weight_ref, own_ref, out_ref, spread_ref):
    up, last = core(), planes - 1
    place = (1 - up) * last
    spread_back(other_ref[up * last], spread_ref)
    out_ref[...] = own_ref[...]
    out_ref[place] = out_ref[place] + dot(spread_ref[...], taps(weight_ref, 2 * up))


def backward_other(other, weight, own):
    planes, plane, _ = own.shape
    filters = weight.shape[1]
    return call(
        functools.partial(backward_other_body, planes),
        struct(own.shape, jnp.float32),
        (2 * weight.size // 3 * plane, weight.size * 2 // 3),
        other, weight, own,
        in_specs=[VMEM] * 3,
        scratch_shapes=[pltpu.VMEM((plane, 9 * filters), jnp.bfloat16)],
    )


def backward_rest_body(planes, count, beyond_ref, weight_ref, own_ref, *refs):
    kept_ref, sent, (spread_ref, total_ref) = refs[0], refs[1:count], refs[count:]
    size = kept_ref.shape[2]
    up, me = core(), here("filt")
    place = up * (planes - 1)
    spread_back(beyond_ref[0], spread_ref)
    product = dot(spread_ref[...], taps(weight_ref, 2 * (1 - up)))
    for block in range(count):
        columns = slice(block * size, (block + 1) * size)
        for j in range(planes):
            total_ref[block, j] = own_ref[j, :, columns]
        total_ref[block, place] = total_ref[block, place] + product[:, columns]
    kept_ref[...] = total_ref[me]
    for number in range(1, count):
        sent[number - 1][...] = total_ref[me ^ number].astype(jnp.bfloat16)


def backward_rest(beyond, weight, own, count, after):
    planes, plane, channels = own.shape
    filters = weight.shape[1]
    size = channels // count
    outs = [struct((planes, plane, size), jnp.float32)]
    outs += [struct((planes, plane, size), jnp.bfloat16)] * (count - 1)
    return call(
        functools.partial(backward_rest_body, planes, count),
        outs,
        (2 * 9 * filters * channels * plane, weight.size * 2 // 3),
        beyond, weight, own,
        in_specs=[VMEM] * 3,
        scratch_shapes=[
            pltpu.VMEM((plane, 9 * filters), jnp.bfloat16),
            pltpu.VMEM((count, planes, plane, size), jnp.float32),
        ],
        after=after,
    )


def first_grad_body(count, slope_ref, *refs):
    parts, out_ref = refs[:count], refs[count]
    for j in range(out_ref.shape[0]):
        total = parts[0][j]
        for part in parts[1:]:
            total = total + part[j].astype(jnp.float32)
        out_ref[j] = (total * slope_ref[j]).astype(jnp.bfloat16)


def first_out(parts, slope, after):
    return call(
        functools.partial(first_grad_body, len(parts)),
        struct(slope.shape, jnp.bfloat16),
        (slope.size * 4, slope.size * 14),
        slope, *parts,
        in_specs=[VMEM] * (1 + len(parts)),
        after=after,
    )


def spread_body(split, first, *refs):
    spread_ref, token_ref = refs[split:]
    token_ref[...] = jnp.zeros_like(token_ref)
    both, rows, plane = refs[0].shape
    depth = both // 2
    me = lax.rem(here("filt"), split)
    for d in range(depth):
        for half in range(split):
            values = refs[half][first * depth + d].astype(jnp.float32)
            for number, (b, e) in enumerate(SHIFTS):
                begin = (number * split + (me ^ half)) * rows
                moved = shifted(values, 1, b, e).astype(jnp.bfloat16)
                spread_ref[pl.ds(pl.multiple_of(begin, rows), rows), d * plane : (d + 1) * plane] = moved


def spread(halved, first):
    split = len(halved)
    both, rows, plane = halved[0].shape
    depth = both // 2
    channels = split * rows
    return call(
        functools.partial(spread_body, split, first),
        [struct((9 * channels, depth * plane), jnp.bfloat16), TOKEN],
        (9 * channels * depth * plane, 10 * channels * depth * plane),
        *halved,
        in_specs=[VMEM] * split,
    )


def weight_grad_body(count, second, spread_ref, crossed_ref, *refs):
    parts, (out_ref, token_ref, grad_ref) = refs[:count], refs[count:]
    token_ref[...] = jnp.zeros_like(token_ref)
    planes, plane, filters = parts[0].shape
    channels = spread_ref.shape[0] // 9
    depth = spread_ref.shape[1] // plane
    zero = jnp.zeros((plane, filters), jnp.bfloat16)
    grad_ref[depth * plane : (depth + 1) * plane, : filters] = zero
    grad_ref[plane : 2 * plane, 2 * filters :] = zero

    def one(block, d, begin):
        rows = block.shape[0]
        for a in (-1, 0, 1):
            place = pl.ds(pl.multiple_of((d + a + 1) * plane + begin, rows), rows)
            grad_ref[place, (a + 1) * filters : (a + 2) * filters] = block

    near, far = far_owners(0), far_owners(1)
    owners = [near[0], far[0], *near[1:], *far[1:]] if second else near + far
    row = 0
    for number in range(count):
        for j in range(planes):
            one(parts[number][j], owners[number] * planes + j, 0)
    for number in range(count, len(owners)):
        for j in range(planes):
            for begin in range(0, plane, filters):
                block = crossed_ref[row : row + filters, begin : begin + filters]
                one(block, owners[number] * planes + j, begin)
            row += filters

    product = dot(spread_ref[...], grad_ref[plane : (depth + 1) * plane, :])
    for r in range(3):
        for number in range(9):
            out_ref[r * 9 + number] = product[
                number * channels : (number + 1) * channels, r * filters : (r + 1) * filters
            ]


def weight_grad(spreads, blocks, crossed, second):
    channels, columns = spreads.shape[0] // 9, spreads.shape[1]
    _, plane, filters = blocks[0].shape
    return call(
        functools.partial(weight_grad_body, len(blocks), second),
        [struct((27, channels, filters), jnp.float32), TOKEN],
        (2 * 27 * filters * channels * columns, 27 * channels * filters * 4 + spreads.size * 2),
        spreads, crossed, *blocks,
        in_specs=[VMEM] * (2 + len(blocks)),
        scratch_shapes=[pltpu.VMEM((columns + 2 * plane, 3 * filters), jnp.bfloat16)],
    )


def shards(features, first_weight, second_weight, head_weight, labels):
    count = lax.axis_size("filt")
    chips = lax.axis_size("slab") // 2
    split = halves(features.shape[1] * count // lax.axis_size("slab"))
    near, first_weight, head_weight = stage(features, first_weight, head_weight)
    all_in, share_in = assemble([near] + exchanged(features, "filt")[1:], -1)
    own = forward_own(all_in, first_weight)
    share_in = [share_in[0]] + chips_apart(share_in[1:])
    other, beyond = halo(all_in, own)
    own = forward_other(other, first_weight, own)
    slope_first, hidden = forward_rest(beyond, first_weight, own, share_in[1:-1])

    hidden_parts = exchanged(hidden, "filt")
    halved_in = collected(share_in, hidden_parts[1:])
    all_hidden, share_hidden = assemble(hidden_parts, 1, share_in[-1:])
    own = forward_own(all_hidden, second_weight)
    share_hidden = [share_hidden[0]] + chips_apart(share_hidden[1:])
    other, beyond = halo(all_hidden, own)
    own = forward_other(other, second_weight, own)
    slope_second, logits = forward_rest(beyond, second_weight, own, share_hidden[1:], head_weight)

    logits_parts = exchanged(logits, "filt")
    second_out = loss_grad(logits_parts, labels, head_weight, slope_second, [])
    halved = both_halves(collected(share_hidden, [logits], [second_out], [halved_in]), split)
    own = backward_own(second_out, second_weight)
    second_other, beyond = halo(second_out, own)
    second_far = every_chip(second_out)[1:]
    own = backward_other(second_other, second_weight, own)
    due = halved[:1] + second_far[chips // 2 - 1 : chips // 2]
    kept, *sent = backward_rest(beyond, second_weight, own, count, due)
    parts = swapped([kept, *sent], "filt", 1)
    spread_in, token_in = spread(halved, 0)
    spread_hidden, token_hidden = spread(halved, 1)
    first_out_grad = first_out(parts, slope_first, [token_in, token_hidden, *second_far])

    first_blocks = [first_out_grad] + chips_apart([first_out_grad] * (chips - 1))
    crossed = swap(pack(second_far, [first_out_grad]), "slab", 1)
    second_blocks = [second_out, second_other] + second_far
    second_grad, token = weight_grad(spread_hidden, second_blocks, crossed, True)
    crossed = swap(pack(first_blocks, [token]), "slab", 1)
    first_grad, _ = weight_grad(spread_in, first_blocks, crossed, False)
    return jnp.transpose(first_grad, (0, 2, 1)), jnp.transpose(second_grad, (0, 2, 1))


def solution(mesh):
    placed = (
        P("slab", "filt", None),
        P(None, "filt", None),
        P(None, "filt", None),
        P(None, "filt"),
        P("slab", None),
    )
    return jax.shard_map(
        shards,
        mesh=mesh,
        in_specs=placed,
        out_specs=(P(None, "filt", "slab"), P(None, "filt", "slab")),
        check_vma=False,
    )
```

```python
import functools

import jax
import jax.numpy as jnp
from jax import lax
from jax.experimental import pallas as pl
from jax.experimental.pallas import tpu as pltpu
from jax.sharding import PartitionSpec as P

WIDTH = 8
SHIFTS = [(b, e) for b in (-1, 0, 1) for e in (-1, 0, 1)]
LIMIT = 20 * 1024 * 1024
VMEM = pl.BlockSpec(memory_space=pltpu.VMEM)
ANY = pl.BlockSpec(memory_space=pl.ANY)


def swap(block, axis, step):
    count = lax.axis_size(axis)
    return lax.ppermute(block, axis, [(i, i ^ step) for i in range(count)])


def exchanged(block, axis):
    return swapped([block] * lax.axis_size(axis), axis, 1)


def swapped(blocks, axis, unit):
    return [blocks[0]] + [swap(blocks[step], axis, unit * step) for step in range(1, len(blocks))]


def halo(volume, own):
    count = lax.axis_size("slab")
    other = swap(volume, "slab", 1)
    passed = edge(other, [own])
    pairs = [(i, i + 2) for i in range(0, count - 2, 2)] + [(i, i - 2) for i in range(3, count, 2)]
    return other, lax.ppermute(passed, "slab", pairs)


def chips_apart(blocks):
    return swapped([None, *blocks], "slab", 2)[1:]


def every_chip(block):
    blocks = [block]
    for step in range(1, lax.axis_size("slab") // 2):
        low = step & -step
        blocks.append(swap(blocks[step ^ low], "slab", 2 * low))
    return blocks


def call(body, out_shape, cost, *operands, in_specs, scratch_shapes=(), passed=(), after=()):
    flops, moved = cost
    single = not isinstance(out_shape, list)
    outs = [out_shape] if single else out_shape
    first, second = len(operands), len(operands) + len(passed) + len(after)
    third = second + len(outs)

    def inner(*refs):
        body(*refs[:first], *refs[second:third], *refs[third + len(passed) :])

    given = pl.pallas_call(
        inner,
        out_shape=[*outs, *(struct(array.shape, array.dtype) for array in passed)],
        cost_estimate=pl.CostEstimate(flops=flops, bytes_accessed=moved, transcendentals=0),
        compiler_params=pltpu.CompilerParams(vmem_limit_bytes=LIMIT),
        in_specs=[*in_specs] + [ANY] * (len(passed) + len(after)),
        out_specs=[VMEM] * len(outs) + [ANY] * len(passed),
        scratch_shapes=list(scratch_shapes),
        input_output_aliases={first + i: len(outs) + i for i in range(len(passed))},
    )(*operands, *passed, *after)
    if passed:
        return [*given[: len(outs)], list(given[len(outs) :])]
    return given[0] if single else list(given)


def struct(shape, dtype):
    return jax.ShapeDtypeStruct(tuple(shape), dtype)


def here(axis):
    return lax.axis_index(axis).astype(jnp.int32)


def core():
    return lax.rem(here("slab"), 2)


def far_owners(side):
    me = here("slab")
    return [me ^ (2 * step) ^ side for step in range(lax.axis_size("slab") // 2)]


TOKEN = struct((8, 128), jnp.float32)


def stage_body(count, *refs):
    sources, targets, sems = refs[:count], refs[count : 2 * count], refs[2 * count]
    copies = [pltpu.make_async_copy(sources[i], targets[i], sems.at[i]) for i in range(count)]
    for copy in copies:
        copy.start()
    for copy in copies:
        copy.wait()


def stage(*arrays):
    count = len(arrays)
    return call(
        functools.partial(stage_body, count),
        [struct(array.shape, array.dtype) for array in arrays],
        (0, sum(4 * array.size for array in arrays)),
        *arrays,
        in_specs=[pl.BlockSpec(memory_space=pltpu.HBM)] * count,
        scratch_shapes=[pltpu.SemaphoreType.DMA((count,))],
    )


def inside(shape, axis, b, e):
    spot = lax.broadcasted_iota(jnp.int32, shape, axis)
    column = spot % WIDTH + e
    moved = spot + WIDTH * b
    return (column >= 0) & (column < WIDTH) & (moved >= 0) & (moved < shape[axis])


def shifted(values, axis, b, e):
    if b == 0 and e == 0:
        return values
    size = values.shape[axis]
    turned = pltpu.roll(values, (-(WIDTH * b + e)) % size, axis)
    return jnp.where(inside(values.shape, axis, b, e), turned, 0.0)


def fold_shifts(products):
    rows = products.shape[0] // len(SHIFTS)
    total = None
    for number, (b, e) in enumerate(SHIFTS):
        term = shifted(products[number * rows : (number + 1) * rows, :], 1, b, e)
        total = term if total is None else total + term
    return total


def dot(left, right):
    return jnp.dot(left, right, preferred_element_type=jnp.float32)


def edge_body(other_ref, out_ref):
    out_ref[0] = other_ref[(1 - core()) * (other_ref.shape[0] - 1)]


def edge(other, after):
    shape = (1, *other.shape[1:])
    return call(edge_body, struct(shape, other.dtype), (0, other.size), other, in_specs=[VMEM], after=after)


def halves(rows):
    return 2 if rows % 32 == 0 and lax.axis_size("filt") % 2 == 0 else 1


def assemble_body(count, split, order, *refs):
    parts, whole_ref, shares = refs[:count][::order], refs[count], refs[count + 1 :]
    size = parts[0].shape[1]
    me, chip = here("filt"), here("slab") // 2
    for step in range(count):
        place = pl.ds(pl.multiple_of((me ^ step) * size, size), size)
        whole_ref[:, place, :] = parts[step][...]
    rows = shares[0].shape[2]
    for step, share_ref in enumerate(shares):
        for side in range(2):
            begin = (((chip ^ step) * 2 + side) * split + lax.rem(me, split)) * rows
            share_ref[side] = whole_ref[:, pl.ds(pl.multiple_of(begin, rows), rows), :]


def assemble(parts, order, after=()):
    planes, size, plane = parts[0].shape
    count, slabs = len(parts), lax.axis_size("slab")
    channels = size * count
    split = halves(channels // slabs)
    kind = parts[0].dtype
    outs = [struct((planes, channels, plane), kind)]
    outs += [struct((2, planes, channels // slabs // split, plane), kind)] * (slabs // 2)
    whole, *shares = call(
        functools.partial(assemble_body, count, split, order),
        outs,
        (0, 4 * planes * channels * plane),
        *parts[::order],
        in_specs=[VMEM] * count,
        after=after,
    )
    return whole, shares


def crossing_body(count, *refs):
    planes = refs[0].shape[1]
    for step in range(count):
        for j in range(planes):
            refs[count][step * planes + j] = refs[step][1 - core(), j]


def collect_body(count, crossed_ref, *refs):
    owners, side = far_owners(0), core()
    planes = refs[0].shape[1]
    out_ref = refs[-1]
    base = out_ref.shape[0] - 2 * count * planes
    if base > 0:
        out_ref[:base] = refs[count][...]
    for step in range(count):
        for j in range(planes):
            out_ref[base + owners[step] * planes + j] = refs[step][side, j]
            out_ref[base + (owners[step] ^ 1) * planes + j] = crossed_ref[step * planes + j]


def collected(shares, after, later=(), earlier=()):
    count = len(shares)
    _, planes, rows, plane = shares[0].shape
    kind, size = shares[0].dtype, shares[0].size * count
    crossing = call(
        functools.partial(crossing_body, count),
        struct((count * planes, rows, plane), kind),
        (0, 2 * size),
        *shares,
        in_specs=[VMEM] * count,
        after=after,
    )
    return call(
        functools.partial(collect_body, count),
        struct((2 * count * planes * (1 + len(earlier)), rows, plane), kind),
        (0, 4 * size),
        swap(crossing, "slab", 1), *shares, *earlier,
        in_specs=[VMEM] * (1 + count + len(earlier)),
        after=later,
    )


def both_halves(volume, split):
    return [volume] + ([swap(volume, "filt", 1)] if split == 2 else [])


def pack_body(count, *refs):
    out_ref = refs[count]
    blocks = refs[:count]
    row = 0
    for number in range(count):
        planes, plane, filters = blocks[number].shape
        for j in range(planes):
            for begin in range(0, plane, filters):
                out_ref[row : row + filters, begin : begin + filters] = blocks[number][j, begin : begin + filters, :]
            row += filters


def pack(blocks, after=()):
    plane = blocks[0].shape[1]
    total = sum(block.size for block in blocks)
    return call(
        functools.partial(pack_body, len(blocks)),
        struct((total // plane, plane), blocks[0].dtype),
        (0, 4 * total),
        *blocks,
        in_specs=[VMEM] * len(blocks),
        after=after,
    )


def taps(weight_ref, number):
    block = weight_ref[pl.ds(9 * number, 9)]
    return block.reshape(block.shape[0] * block.shape[1], block.shape[2])


def forward_own_body(planes, volume_ref, weight_ref, out_ref, acc_ref):
    for a in (0, 1, -1):
        weight = taps(weight_ref, a + 1)
        for j in range(planes):
            if 0 <= j + a < planes:
                product = dot(weight, volume_ref[j + a])
                acc_ref[j] = product if a == 0 else acc_ref[j] + product
    for j in range(planes):
        out_ref[j] = fold_shifts(acc_ref.at[j])


def forward_own(volume, weight):
    planes, channels, plane = volume.shape
    filters = weight.shape[1]
    return call(
        functools.partial(forward_own_body, planes),
        struct((planes, filters, plane), jnp.float32),
        (2 * 9 * filters * channels * plane * (3 * planes - 2), weight.size * 2),
        volume, weight,
        in_specs=[VMEM] * 2,
        scratch_shapes=[pltpu.VMEM((planes, 9 * filters, plane), jnp.float32)],
    )


def forward_other_body(planes, other_ref, weight_ref, own_ref, out_ref, acc_ref):
    up, last = core(), planes - 1
    place = (1 - up) * last
    acc_ref[...] = dot(taps(weight_ref, 2 * (1 - up)), other_ref[up * last])
    out_ref[...] = own_ref[...]
    out_ref[place] = out_ref[place] + fold_shifts(acc_ref)


def forward_other(other, weight, own):
    planes, filters, plane = own.shape
    return call(
        functools.partial(forward_other_body, planes),
        struct(own.shape, jnp.float32),
        (2 * weight.size // 3 * plane, weight.size * 2 // 3),
        other, weight, own,
        in_specs=[VMEM] * 3,
        scratch_shapes=[pltpu.VMEM((9 * filters, plane), jnp.float32)],
    )


def silu_and_slope(values):
    sig = 1.0 / (1.0 + jnp.exp(-values))
    return values * sig, sig * (1.0 + values * (1.0 - sig))


def forward_rest_body(planes, beyond_ref, weight_ref, own_ref, *refs):
    head_ref = refs[0] if len(refs) == 5 else None
    slope_ref, made_ref, acc_ref, total_ref = refs[-4:]
    up = core()
    place = up * (planes - 1)
    total_ref[...] = own_ref[...]
    acc_ref[...] = dot(taps(weight_ref, 2 * up), beyond_ref[0])
    total_ref[place] = total_ref[place] + fold_shifts(acc_ref)
    for j in range(planes):
        value, slope = silu_and_slope(total_ref[j])
        value = value.astype(jnp.bfloat16)
        slope_ref[j] = slope.T if head_ref is None else slope
        made_ref[j] = value if head_ref is None else dot(head_ref[...], value)


def forward_rest(beyond, weight, own, after, head=None):
    planes, filters, plane = own.shape
    channels = weight.shape[2]
    ins = [beyond, weight, own]
    slope = own.shape
    if head is None:
        slope = (planes, plane, filters)
        made = struct(own.shape, jnp.bfloat16)
    else:
        ins.append(head)
        made = struct((planes, head.shape[0], plane), jnp.float32)
    return call(
        functools.partial(forward_rest_body, planes),
        [struct(slope, jnp.float32), made],
        (2 * 9 * filters * channels * plane, weight.size * 2 // 3),
        *ins,
        in_specs=[VMEM] * len(ins),
        scratch_shapes=[
            pltpu.VMEM((9 * filters, plane), jnp.float32),
            pltpu.VMEM(own.shape, jnp.float32),
        ],
        after=after,
    )


def loss_body(count, labels_ref, head_ref, slope_ref, *refs):
    parts, grad_ref = refs[:count][::-1], refs[count]
    for j in range(grad_ref.shape[0]):
        logits = parts[0][j]
        for part in parts[1:]:
            logits = logits + part[j]
        powers = jnp.exp(logits)
        likely = powers / jnp.sum(powers, axis=0, keepdims=True)
        classes = lax.broadcasted_iota(jnp.int32, logits.shape, 0)
        onehot = (labels_ref[j : j + 1, :] == classes).astype(jnp.float32)
        logit_grad = (likely - onehot).astype(jnp.bfloat16).astype(jnp.float32)
        back = lax.dot_general(
            head_ref[...].astype(jnp.float32),
            logit_grad,
            (((0,), (0,)), ((), ())),
            preferred_element_type=jnp.float32,
        )
        grad_ref[j] = (back * slope_ref[j]).T.astype(jnp.bfloat16)


def loss_grad(parts, labels, head, slope, after):
    planes, plane = labels.shape
    return call(
        functools.partial(loss_body, len(parts)),
        struct((planes, plane, slope.shape[1]), jnp.bfloat16),
        (2 * slope.size * head.shape[0], slope.size * 6),
        labels, head, slope, *parts[::-1],
        in_specs=[VMEM] * (3 + len(parts)),
        after=after,
    )


def spread_back(grad, spread_ref):
    filters = grad.shape[1]
    turned = grad.astype(jnp.float32)
    for number, (b, e) in enumerate(SHIFTS):
        moved = shifted(turned, 0, -b, -e).astype(jnp.bfloat16)
        spread_ref[:, number * filters : (number + 1) * filters] = moved


def backward_own_body(planes, grad_ref, weight_ref, out_ref, spread_ref):
    for j in range(planes):
        spread_back(grad_ref[j], spread_ref.at[j])
    for a in (0, 1, -1):
        weight = taps(weight_ref, a + 1)
        for j in range(planes):
            if 0 <= j - a < planes:
                product = dot(spread_ref[j - a], weight)
                out_ref[j] = product if a == 0 else out_ref[j] + product


def backward_own(grad, weight):
    planes, plane, filters = grad.shape
    channels = weight.shape[2]
    return call(
        functools.partial(backward_own_body, planes),
        struct((planes, plane, channels), jnp.float32),
        (2 * 9 * filters * channels * plane * (3 * planes - 2), weight.size * 2),
        grad, weight,
        in_specs=[VMEM] * 2,
        scratch_shapes=[pltpu.VMEM((planes, plane, 9 * filters), jnp.bfloat16)],
    )


def backward_other_body(planes, other_ref, weight_ref, own_ref, out_ref, spread_ref):
    up, last = core(), planes - 1
    place = (1 - up) * last
    spread_back(other_ref[up * last], spread_ref)
    out_ref[...] = own_ref[...]
    out_ref[place] = out_ref[place] + dot(spread_ref[...], taps(weight_ref, 2 * up))


def backward_other(other, weight, own):
    planes, plane, _ = own.shape
    filters = weight.shape[1]
    return call(
        functools.partial(backward_other_body, planes),
        struct(own.shape, jnp.float32),
        (2 * weight.size // 3 * plane, weight.size * 2 // 3),
        other, weight, own,
        in_specs=[VMEM] * 3,
        scratch_shapes=[pltpu.VMEM((plane, 9 * filters), jnp.bfloat16)],
    )


def backward_rest_body(planes, count, beyond_ref, weight_ref, own_ref, *refs):
    kept_ref, sent, (spread_ref, total_ref) = refs[0], refs[1:count], refs[count:]
    size = kept_ref.shape[2]
    up, me = core(), here("filt")
    place = up * (planes - 1)
    spread_back(beyond_ref[0], spread_ref)
    product = dot(spread_ref[...], taps(weight_ref, 2 * (1 - up)))
    for block in range(count):
        columns = slice(block * size, (block + 1) * size)
        for j in range(planes):
            total_ref[block, j] = own_ref[j, :, columns]
        total_ref[block, place] = total_ref[block, place] + product[:, columns]
    kept_ref[...] = total_ref[me]
    for number in range(1, count):
        sent[number - 1][...] = total_ref[me ^ number].astype(jnp.bfloat16)


def backward_rest(beyond, weight, own, count, after):
    planes, plane, channels = own.shape
    filters = weight.shape[1]
    size = channels // count
    outs = [struct((planes, plane, size), jnp.float32)]
    outs += [struct((planes, plane, size), jnp.bfloat16)] * (count - 1)
    return call(
        functools.partial(backward_rest_body, planes, count),
        outs,
        (2 * 9 * filters * channels * plane, weight.size * 2 // 3),
        beyond, weight, own,
        in_specs=[VMEM] * 3,
        scratch_shapes=[
            pltpu.VMEM((plane, 9 * filters), jnp.bfloat16),
            pltpu.VMEM((count, planes, plane, size), jnp.float32),
        ],
        after=after,
    )


def first_grad_body(count, slope_ref, *refs):
    parts, out_ref = refs[:count], refs[count]
    for j in range(out_ref.shape[0]):
        total = parts[0][j]
        for part in parts[1:]:
            total = total + part[j].astype(jnp.float32)
        out_ref[j] = (total * slope_ref[j]).astype(jnp.bfloat16)


def first_out(parts, slope, after):
    return call(
        functools.partial(first_grad_body, len(parts)),
        struct(slope.shape, jnp.bfloat16),
        (slope.size * 4, slope.size * 14),
        slope, *parts,
        in_specs=[VMEM] * (1 + len(parts)),
        after=after,
    )


def spread_body(split, first, *refs):
    spread_ref, token_ref = refs[split:]
    token_ref[...] = jnp.zeros_like(token_ref)
    both, rows, plane = refs[0].shape
    depth = both // 2
    me = lax.rem(here("filt"), split)
    for d in range(depth):
        for half in range(split):
            values = refs[half][first * depth + d].astype(jnp.float32)
            for number, (b, e) in enumerate(SHIFTS):
                begin = (number * split + (me ^ half)) * rows
                moved = shifted(values, 1, b, e).astype(jnp.bfloat16)
                spread_ref[pl.ds(pl.multiple_of(begin, rows), rows), d * plane : (d + 1) * plane] = moved


def spread(halved, first):
    split = len(halved)
    both, rows, plane = halved[0].shape
    depth = both // 2
    channels = split * rows
    return call(
        functools.partial(spread_body, split, first),
        [struct((9 * channels, depth * plane), jnp.bfloat16), TOKEN],
        (9 * channels * depth * plane, 10 * channels * depth * plane),
        *halved,
        in_specs=[VMEM] * split,
    )


def weight_grad_body(count, second, spread_ref, crossed_ref, *refs):
    parts, (out_ref, token_ref, grad_ref) = refs[:count], refs[count:]
    token_ref[...] = jnp.zeros_like(token_ref)
    planes, plane, filters = parts[0].shape
    channels = spread_ref.shape[0] // 9
    depth = spread_ref.shape[1] // plane
    zero = jnp.zeros((plane, filters), jnp.bfloat16)
    grad_ref[depth * plane : (depth + 1) * plane, : filters] = zero
    grad_ref[plane : 2 * plane, 2 * filters :] = zero

    def one(block, d, begin):
        rows = block.shape[0]
        for a in (-1, 0, 1):
            place = pl.ds(pl.multiple_of((d + a + 1) * plane + begin, rows), rows)
            grad_ref[place, (a + 1) * filters : (a + 2) * filters] = block

    near, far = far_owners(0), far_owners(1)
    owners = [near[0], far[0], *near[1:], *far[1:]] if second else near + far
    row = 0
    for number in range(count):
        for j in range(planes):
            one(parts[number][j], owners[number] * planes + j, 0)
    for number in range(count, len(owners)):
        for j in range(planes):
            for begin in range(0, plane, filters):
                block = crossed_ref[row : row + filters, begin : begin + filters]
                one(block, owners[number] * planes + j, begin)
            row += filters

    product = dot(spread_ref[...], grad_ref[plane : (depth + 1) * plane, :])
    for r in range(3):
        for number in range(9):
            out_ref[r * 9 + number] = product[
                number * channels : (number + 1) * channels, r * filters : (r + 1) * filters
            ]


def weight_grad(spreads, blocks, crossed, second):
    channels, columns = spreads.shape[0] // 9, spreads.shape[1]
    _, plane, filters = blocks[0].shape
    return call(
        functools.partial(weight_grad_body, len(blocks), second),
        [struct((27, channels, filters), jnp.float32), TOKEN],
        (2 * 27 * filters * channels * columns, 27 * channels * filters * 4 + spreads.size * 2),
        spreads, crossed, *blocks,
        in_specs=[VMEM] * (2 + len(blocks)),
        scratch_shapes=[pltpu.VMEM((columns + 2 * plane, 3 * filters), jnp.bfloat16)],
    )


def shards(features, first_weight, second_weight, head_weight, labels):
    count = lax.axis_size("filt")
    chips = lax.axis_size("slab") // 2
    split = halves(features.shape[1] * count // lax.axis_size("slab"))
    near, first_weight, head_weight = stage(features, first_weight, head_weight)
    all_in, share_in = assemble([near] + exchanged(features, "filt")[1:], -1)
    own = forward_own(all_in, first_weight)
    share_in = [share_in[0]] + chips_apart(share_in[1:])
    other, beyond = halo(all_in, own)
    own = forward_other(other, first_weight, own)
    slope_first, hidden = forward_rest(beyond, first_weight, own, share_in[1:-1])

    hidden_parts = exchanged(hidden, "filt")
    halved_in = collected(share_in, hidden_parts[1:])
    all_hidden, share_hidden = assemble(hidden_parts, 1, share_in[-1:])
    own = forward_own(all_hidden, second_weight)
    share_hidden = [share_hidden[0]] + chips_apart(share_hidden[1:])
    other, beyond = halo(all_hidden, own)
    own = forward_other(other, second_weight, own)
    slope_second, logits = forward_rest(beyond, second_weight, own, share_hidden[1:-1], head_weight)

    logits_parts = exchanged(logits, "filt")
    second_out = loss_grad(logits_parts, labels, head_weight, slope_second, share_hidden[-1:])
    halved = both_halves(collected(share_hidden, logits_parts[1:], [second_out], [halved_in]), split)
    own = backward_own(second_out, second_weight)
    second_other, beyond = halo(second_out, own)
    second_far = every_chip(second_out)[1:]
    own = backward_other(second_other, second_weight, own)
    due = halved[:1] + second_far[chips // 2 - 1 : chips // 2]
    kept, *sent = backward_rest(beyond, second_weight, own, count, due)
    parts = swapped([kept, *sent], "filt", 1)
    spread_in, token_in = spread(halved, 0)
    spread_hidden, token_hidden = spread(halved, 1)
    first_out_grad = first_out(parts, slope_first, [token_in, token_hidden, *second_far])

    first_blocks = [first_out_grad] + chips_apart([first_out_grad] * (chips - 1))
    crossed = swap(pack(second_far, [first_out_grad]), "slab", 1)
    second_blocks = [second_out, second_other] + second_far
    second_grad, token = weight_grad(spread_hidden, second_blocks, crossed, True)
    crossed = swap(pack(first_blocks, [token]), "slab", 1)
    first_grad, _ = weight_grad(spread_in, first_blocks, crossed, False)
    return jnp.transpose(first_grad, (0, 2, 1)), jnp.transpose(second_grad, (0, 2, 1))


def solution(mesh):
    placed = (
        P("slab", "filt", None),
        P(None, "filt", None),
        P(None, "filt", None),
        P(None, "filt"),
        P("slab", None),
    )
    return jax.shard_map(
        shards,
        mesh=mesh,
        in_specs=placed,
        out_specs=(P(None, "filt", "slab"), P(None, "filt", "slab")),
        check_vma=False,
    )
```
